32 devices in a mesh: inner: 4 (over y, x), outer: 2 (over core), head: 4 (over z).
Axes of the slice: x: 2, y: 2, z: 4, core: 2. Of those that a mesh axis runs over, the one named last changes fastest.
Arguments:
- queries: bfloat16 [1024, 24, 128], P(('outer', 'inner'), 'head'), may hold values from -6 to 6
- key_rows: bfloat16 [1024, 4, 128], P(('outer', 'inner'), 'head'), may hold values from -6 to 6
- value_rows: bfloat16 [1024, 4, 128], P(('outer', 'inner'), 'head'), may hold values from -6 to 6
- attn_out: bfloat16 [1024, 24, 128], P(('outer', 'inner'), 'head'), may hold values from -3 to 3
- grad_out: bfloat16 [1024, 24, 128], P(('outer', 'inner'), 'head'), may hold values from -96 to 96
- log_norms: float32 [24, 1024], P('head', ('outer', 'inner'))
- pair_order: int32 [4], replicated, may hold values from 0 to 3, each once
Outputs:
- grad_queries: bfloat16 [1024, 24, 128], P(('outer', 'inner'), 'head')
- grad_keys: bfloat16 [1024, 4, 128], P(('outer', 'inner'), 'head')
- grad_values: bfloat16 [1024, 4, 128], P(('outer', 'inner'), 'head')
The draws below stay inside these ranges and needn't reach their ends.
Inputs may be any that keep to these rules, and one draw needn't show every extreme that they name: Index i of inner holds, in every segment, span pair_order[i] in its first 64 rows and span 8 - 1 - pair_order[i] in its last 64 rows.
All inputs are finite; a program needn't handle non-finite values.
Results may differ from the reference program's by a relative error of at most 0.0053.
Values may be sent and summed in bfloat16 or wider, within the bound.
No kernel may reach another device: no remote copies, remote signals or barrier semaphores. Data moves between devices by JAX's collectives and lax.ppermute only.
A program may use at most 64 MiB of HBM per device.

```python
import math
import jax
import jax.numpy as jnp
from jax import lax

SPAN = 64
HEAD_DIM = 128
KV_HEADS = 4
GROUP = 6
Q_HEADS = 24
SEG = 512
SEQ = 1024
N_INNER = 4
N_OUTER = 2


def draw_log_norms(key, part):
    key = jax.random.fold_in(key, 11)
    base_level = jnp.log(jnp.float32(SEG))
    offset = 1.25 + 0.4 * jax.random.truncated_normal(key, -3.0, 3.0, (Q_HEADS, SEQ), jnp.float32)
    return (base_level + offset).astype(jnp.float32)


def levels(key, shape, cuts, least, high):
    def one(axis_at, shards_of):
        steps = jax.random.uniform(jax.random.fold_in(jax.random.fold_in(key, 6), axis_at), (shards_of,), jnp.float32, least / len(cuts), high / len(cuts))
        return jnp.repeat(jnp.exp(steps), shape[axis_at] // shards_of).reshape((-1,) + (1,) * (len(shape) - axis_at - 1))

    factor_of = one(*cuts[0])
    for cut in cuts[1:]:
        factor_of = factor_of * one(*cut)
    return factor_of


def scatter_about(rng, dims, scale, reach, cuts=(), kind=jnp.bfloat16):
    values = jax.random.normal(rng, dims, jnp.float32) * scale
    if len(cuts) > 0:
        values = levels(rng, dims, cuts, -0.22, 0.18) * values
    return jnp.clip(values, min=-reach, max=reach).astype(kind)


def setup_inputs(seed: int = 0) -> dict:
    seeds = jax.random.split(jax.random.key(seed), 8)
    return {
        "queries": scatter_about(seeds[0], (SEQ, Q_HEADS, HEAD_DIM), 1.0, 6.0, ((0, 8), (1, 4))),
        "key_rows": scatter_about(seeds[1], (SEQ, KV_HEADS, HEAD_DIM), 1.0, 6.0, ((0, 8), (1, 4))),
        "value_rows": scatter_about(seeds[2], (SEQ, KV_HEADS, HEAD_DIM), 1.0, 6.0, ((0, 8), (1, 4))),
        "attn_out": scatter_about(seeds[3], (SEQ, Q_HEADS, HEAD_DIM), 0.5, 3.0, ((0, 8), (1, 4))),
        "grad_out": scatter_about(seeds[4], (SEQ, Q_HEADS, HEAD_DIM), 16.0, 96.0, ((0, 8), (1, 4))),
        "log_norms": draw_log_norms(jax.random.fold_in(seeds[7], 71), 0),
        "pair_order": jax.random.permutation(seeds[6], N_INNER).astype(jnp.int32),
    }


def segment_positions(pair_order, within, span_rows):
    slot_index = within // (2 * span_rows)
    local_rows = within % (2 * span_rows)
    rank_value = jnp.take(pair_order, slot_index)
    span_count = 2 * pair_order.shape[0]
    first_half = rank_value * span_rows + local_rows
    second_half = (span_count - 1 - rank_value) * span_rows + local_rows - span_rows
    return jnp.where(local_rows < span_rows, first_half, second_half).astype(jnp.int32)

def block_grads(queries_five, grad_five, norms_four, dots_four, key_blocks, value_blocks, visible, inv_root):
    queries_wide = queries_five.astype(jnp.float32)
    grad_wide = grad_five.astype(jnp.float32)
    scores = jnp.einsum('arhgd,bkhd->ahgrbk', queries_wide, key_blocks.astype(jnp.float32)) * inv_root
    attn_weights = jnp.where(visible[:, None, None], jnp.exp(scores - norms_four[..., None, None]), 0.0)
    weights_half = attn_weights.astype(jnp.bfloat16)
    grad_weights = jnp.einsum('arhgd,bkhd->ahgrbk', grad_wide, value_blocks.astype(jnp.float32))
    grad_scores = (attn_weights * (grad_weights - dots_four[..., None, None])).astype(jnp.bfloat16)
    score_wide = grad_scores.astype(jnp.float32)
    value_grad = jnp.einsum('ahgrbk,arhgd->bkhd', weights_half.astype(jnp.float32), grad_wide)
    key_grad = jnp.einsum('ahgrbk,arhgd->bkhd', score_wide, queries_wide) * inv_root
    query_grad = jnp.einsum('ahgrbk,bkhd->arhgd', score_wide, key_blocks.astype(jnp.float32)) * inv_root
    return (query_grad, key_grad, value_grad)

def reference(queries, key_rows, value_rows, attn_out, grad_out, log_norms, pair_order):
    inv_root = 1.0 / math.sqrt(HEAD_DIM)
    row_dot = lax.optimization_barrier(jnp.sum(grad_out.astype(jnp.float32) * attn_out.astype(jnp.float32), axis=-1))
    within = jnp.arange(SEG, dtype=jnp.int32)
    positions = segment_positions(pair_order, within, SPAN)
    causal = positions[None, :] <= positions[:, None]
    query_heads = jnp.moveaxis(queries.reshape(SEQ, KV_HEADS, GROUP, HEAD_DIM), 1, 0)
    grad_heads = jnp.moveaxis(grad_out.reshape(SEQ, KV_HEADS, GROUP, HEAD_DIM), 1, 0)
    key_heads = jnp.moveaxis(key_rows, 1, 0)
    value_heads = jnp.moveaxis(value_rows, 1, 0)
    norm_heads = log_norms.reshape(KV_HEADS, GROUP, SEQ)
    dot_heads = row_dot.T.reshape(KV_HEADS, GROUP, SEQ)

    def one_head(operands):
        head_queries, head_grads, head_keys, head_values, head_norms, head_dots = operands
        query_parts = []
        key_parts = [jnp.zeros((SEG, HEAD_DIM), jnp.float32) for segment in range(N_OUTER)]
        value_parts = [jnp.zeros((SEG, HEAD_DIM), jnp.float32) for segment in range(N_OUTER)]
        for segment in range(N_OUTER):
            start_row = segment * SEG
            stop_row = start_row + SEG
            own_keys = head_keys[start_row:stop_row]
            own_values = head_values[start_row:stop_row]
            if segment > 0:
                prev_keys = head_keys[start_row - SEG:start_row]
                prev_values = head_values[start_row - SEG:start_row]
            else:
                prev_keys = jnp.zeros_like(own_keys)
                prev_values = jnp.zeros_like(own_values)
            key_blocks = jnp.stack([prev_keys, own_keys])[:, :, None, :]
            value_blocks = jnp.stack([prev_values, own_values])[:, :, None, :]
            visible = jnp.stack([jnp.full((SEG, SEG), segment > 0), causal], axis=1)[None]
            query_grad, key_grad, value_grad = block_grads(head_queries[start_row:stop_row][None, :, None], head_grads[start_row:stop_row][None, :, None], head_norms[:, start_row:stop_row][None, None], head_dots[:, start_row:stop_row][None, None], key_blocks, value_blocks, visible, inv_root)
            query_parts.append(query_grad[0, :, 0])
            key_parts[segment] = key_parts[segment] + key_grad[1, :, 0]
            value_parts[segment] = value_parts[segment] + value_grad[1, :, 0]
            if segment > 0:
                key_parts[segment - 1] = key_parts[segment - 1] + key_grad[0, :, 0]
                value_parts[segment - 1] = value_parts[segment - 1] + value_grad[0, :, 0]
        return (jnp.concatenate(query_parts), jnp.concatenate(key_parts), jnp.concatenate(value_parts))
    query_grad, key_grad, value_grad = lax.map(one_head, (query_heads, grad_heads, key_heads, value_heads, norm_heads, dot_heads))
    grad_queries = jnp.moveaxis(query_grad, 0, 1).reshape(SEQ, Q_HEADS, HEAD_DIM).astype(jnp.bfloat16)
    grad_keys = jnp.moveaxis(key_grad, 0, 1).astype(jnp.bfloat16)
    grad_values = jnp.moveaxis(value_grad, 0, 1).astype(jnp.bfloat16)
    return (grad_queries, grad_keys, grad_values)
```

```python
import functools
import math

import jax
import jax.numpy as jnp
from jax import lax
from jax.experimental import pallas as pl
from jax.experimental.pallas import tpu as pltpu
from jax.sharding import PartitionSpec as P

LOG2E = math.log2(math.e)
STAT_ROWS = 16
SPLIT = 3


def contract(lhs, rhs, lhs_dim, rhs_dim):
    return lax.dot_general(
        lhs, rhs, (((lhs_dim,), (rhs_dim,)), ((), ())), preferred_element_type=jnp.float32
    )


def span_positions(rank_value, rows, span_rows, span_count):
    return jnp.where(
        rows < span_rows,
        rank_value * span_rows + rows,
        (span_count - 2 - rank_value) * span_rows + rows,
    )


def packet_rows(sizes):
    group_size, row_count, _ = sizes
    return 2 * group_size * row_count + SPLIT * STAT_ROWS


def pack_kernel(
    sizes, inner_count, query_hbm, grad_hbm, out_hbm, norm_hbm, key_hbm, value_hbm,
    packet_ref, pairs_ref, out_ref, norm_ref, stat_ref, sems,
):
    group_size, row_count, head_size = sizes
    half = group_size * row_count
    copies = [
        pltpu.make_async_copy(source, target, sems.at[at])
        for at, (source, target) in enumerate(
            [
                (key_hbm, pairs_ref.at[0, 0]),
                (value_hbm, pairs_ref.at[0, 1]),
                (norm_hbm, norm_ref),
                (grad_hbm, packet_ref.at[pl.ds(half, half)]),
                (out_hbm, out_ref),
                (query_hbm, packet_ref.at[pl.ds(0, half)]),
            ]
        )
    ]
    for copy in copies:
        copy.start()
    copies[0].wait()
    copies[1].wait()
    for peer in range(1, inner_count):
        pairs_ref[peer] = pairs_ref[0]
    stat_ref[...] = jnp.zeros_like(stat_ref)
    copies[2].wait()
    stat_ref[:group_size] = norm_ref[...]
    copies[3].wait()
    copies[4].wait()
    for head in range(group_size):
        rows = slice(head * row_count, (head + 1) * row_count)
        grads = packet_ref[half + head * row_count : half + (head + 1) * row_count, :]
        product = grads.astype(jnp.float32) * out_ref[rows, :].astype(jnp.float32)
        stat_ref[8 + head : 9 + head, :] = jnp.sum(product.T, axis=0, keepdims=True)
    rest = jnp.clip(stat_ref[...], -3.38e38, 3.38e38)
    for term in range(SPLIT):
        piece = rest.astype(jnp.bfloat16)
        start = 2 * half + term * STAT_ROWS
        packet_ref[start : start + STAT_ROWS, :] = piece
        rest = rest - piece.astype(jnp.float32)
    copies[5].wait()


def packet_stats(packet_ref, sizes):
    group_size, row_count, _ = sizes
    start = 2 * group_size * row_count
    pieces = [
        packet_ref[start + term * STAT_ROWS : start + (term + 1) * STAT_ROWS, :].astype(jnp.float32)
        for term in range(SPLIT)
    ]
    stats = pieces[0] + (pieces[1] + pieces[2])
    return stats[:8] * LOG2E, stats[8:]


def block_terms(keys, values, visible, packet_ref, sizes):
    group_size, row_count, head_size = sizes
    half = group_size * row_count
    scale = LOG2E / math.sqrt(head_size)
    per_step = 2 if group_size % 2 == 0 else 1
    all_norms, all_dots = packet_stats(packet_ref, sizes)
    key_total = jnp.zeros((keys.shape[0], head_size), jnp.float32)
    value_total = jnp.zeros((keys.shape[0], head_size), jnp.float32)
    query_terms = []
    for first in range(0, group_size, per_step):
        start, stop = first * row_count, (first + per_step) * row_count
        queries = packet_ref[start:stop, :]
        grads = packet_ref[half + start : half + stop, :]
        scores = contract(keys, queries, 1, 1)
        grad_weights = contract(values, grads, 1, 1)
        weights_parts = []
        score_parts = []
        for at in range(per_step):
            head = first + at
            lanes = slice(at * row_count, (at + 1) * row_count)
            weights = jnp.exp2(scores[:, lanes] * scale - all_norms[head : head + 1, :])
            if visible is not None:
                weights = jnp.where(visible, weights, 0.0)
            weights_parts.append(weights.astype(jnp.bfloat16))
            score_parts.append(
                (weights * (grad_weights[:, lanes] - all_dots[head : head + 1, :])).astype(jnp.bfloat16)
            )
        weights_half = jnp.concatenate(weights_parts, axis=1)
        grad_scores = jnp.concatenate(score_parts, axis=1)
        value_total += contract(weights_half, grads, 1, 0)
        key_total += contract(grad_scores, queries, 1, 0)
        query_terms.append(contract(keys, grad_scores, 0, 0))
    return key_total, value_total, query_terms


def store_queries(result_ref, query_terms, sizes):
    group_size, row_count, head_size = sizes
    inv_root = 1.0 / math.sqrt(head_size)
    whole = jnp.concatenate(query_terms, axis=1)
    for head in range(group_size):
        rows = slice(head * row_count, (head + 1) * row_count)
        result_ref[rows, :] = (whole[:, rows] * inv_root).T.astype(result_ref.dtype)


def main_kernel(
    sizes, inner_count, outer_count, pair_ref, packet_ref, next_ref, gathered_ref,
    query_ref, next_query_ref, sums_ref, total_ref,
):
    group_size, row_count, head_size = sizes
    span_rows = row_count // 2
    inv_root = 1.0 / math.sqrt(head_size)
    my_index = lax.axis_index("inner")
    has_next = lax.axis_index("outer") < outer_count - 1

    key_rows = lax.broadcasted_iota(jnp.int32, (row_count, row_count), 0)
    my_rows = lax.broadcasted_iota(jnp.int32, (row_count, row_count), 1)
    my_positions = span_positions(pair_ref[my_index], my_rows, span_rows, 2 * inner_count)
    visible = jnp.concatenate(
        [
            span_positions(pair_ref[peer], key_rows, span_rows, 2 * inner_count) <= my_positions
            for peer in range(inner_count)
        ],
        axis=0,
    )
    keys = jnp.concatenate([gathered_ref[peer, 0] for peer in range(inner_count)], axis=0)
    values = jnp.concatenate([gathered_ref[peer, 1] for peer in range(inner_count)], axis=0)
    key_terms, value_terms, query_terms = block_terms(keys, values, visible, packet_ref, sizes)
    store_queries(query_ref, query_terms, sizes)
    total_ref[0] = key_terms
    total_ref[1] = value_terms

    @pl.when(has_next)
    def _():
        key_terms, value_terms, query_terms = block_terms(keys, values, None, next_ref, sizes)
        store_queries(next_query_ref, query_terms, sizes)
        total_ref[0] += key_terms
        total_ref[1] += value_terms

    for peer in range(inner_count):
        rows = slice(peer * row_count, (peer + 1) * row_count)
        sums_ref[peer, 0] = (total_ref[0, rows, :] * inv_root).astype(jnp.bfloat16)
        sums_ref[peer, 1] = total_ref[1, rows, :].astype(jnp.bfloat16)


def final_kernel(
    inner_count, query_ref, back_ref, sums_ref, query_hbm, key_hbm, value_hbm,
    query_out, key_out, value_out, sems,
):
    key_out[...] = sum(sums_ref[peer, 0].astype(jnp.float32) for peer in range(inner_count)).astype(jnp.bfloat16)
    value_out[...] = sum(sums_ref[peer, 1].astype(jnp.float32) for peer in range(inner_count)).astype(jnp.bfloat16)
    key_copy = pltpu.make_async_copy(key_out, key_hbm, sems.at[0])
    key_copy.start()
    value_copy = pltpu.make_async_copy(value_out, value_hbm, sems.at[1])
    value_copy.start()
    query_out[...] = (query_ref[...] + back_ref[...].astype(jnp.float32)).astype(jnp.bfloat16)
    query_copy = pltpu.make_async_copy(query_out, query_hbm, sems.at[2])
    query_copy.start()
    key_copy.wait()
    value_copy.wait()
    query_copy.wait()


def on_device(queries, key_rows, value_rows, attn_out, grad_out, log_norms, pair_order):
    row_count, group_size, head_size = queries.shape
    inner_count = lax.axis_size("inner")
    outer_count = lax.axis_size("outer")
    sizes = (group_size, row_count, head_size)
    half = group_size * row_count

    def flat(array):
        return jnp.swapaxes(array, 0, 1).reshape(-1, head_size)

    def to_segment(block, ahead):
        route = [(at, at + ahead) for at in range(outer_count) if 0 <= at + ahead < outer_count]
        return lax.ppermute(block, "outer", route)

    smem = pl.BlockSpec(memory_space=pltpu.SMEM)
    vmem = pl.BlockSpec(memory_space=pltpu.VMEM)
    anywhere = pl.BlockSpec(memory_space=pl.ANY)
    params = pltpu.CompilerParams(vmem_limit_bytes=32 * 2**20)
    block_flops = 10 * group_size * row_count * row_count * head_size

    packet, pairs = pl.pallas_call(
        functools.partial(pack_kernel, sizes, inner_count),
        out_shape=(
            jax.ShapeDtypeStruct((packet_rows(sizes), head_size), jnp.bfloat16),
            jax.ShapeDtypeStruct((inner_count, 2, row_count, head_size), jnp.bfloat16),
        ),
        in_specs=[anywhere] * 6,
        out_specs=(vmem, vmem),
        scratch_shapes=[
            pltpu.VMEM((half, head_size), jnp.bfloat16),
            pltpu.VMEM((group_size, row_count), jnp.float32),
            pltpu.VMEM((STAT_ROWS, row_count), jnp.float32),
            pltpu.SemaphoreType.DMA((6,)),
        ],
        cost_estimate=pl.CostEstimate(flops=half * head_size, bytes_accessed=2**20, transcendentals=0),
        compiler_params=params,
    )(flat(queries), flat(grad_out), flat(attn_out), log_norms, flat(key_rows), flat(value_rows))

    next_packet = to_segment(packet, -1)
    gathered = lax.all_to_all(pairs, "inner", 0, 0)

    query_own, query_next, sums = pl.pallas_call(
        functools.partial(main_kernel, sizes, inner_count, outer_count),
        out_shape=(
            jax.ShapeDtypeStruct((half, head_size), jnp.float32),
            jax.ShapeDtypeStruct((half, head_size), jnp.bfloat16),
            jax.ShapeDtypeStruct((inner_count, 2, row_count, head_size), jnp.bfloat16),
        ),
        in_specs=[smem] + [vmem] * 3,
        out_specs=(vmem,) * 3,
        scratch_shapes=[pltpu.VMEM((2, inner_count * row_count, head_size), jnp.float32)],
        cost_estimate=pl.CostEstimate(
            flops=2 * inner_count * block_flops,
            bytes_accessed=2**21,
            transcendentals=2 * inner_count * group_size * row_count**2,
        ),
        compiler_params=params,
    )(pair_order, packet, next_packet, gathered)

    query_back = to_segment(query_next, 1)
    returned = lax.all_to_all(sums, "inner", 0, 0)

    query_out, key_out, value_out = pl.pallas_call(
        functools.partial(final_kernel, inner_count),
        out_shape=(
            jax.ShapeDtypeStruct((half, head_size), jnp.bfloat16),
            jax.ShapeDtypeStruct((row_count, head_size), jnp.bfloat16),
            jax.ShapeDtypeStruct((row_count, head_size), jnp.bfloat16),
        ),
        in_specs=[vmem] * 3,
        out_specs=(anywhere,) * 3,
        scratch_shapes=[
            pltpu.VMEM((half, head_size), jnp.bfloat16),
            pltpu.VMEM((row_count, head_size), jnp.bfloat16),
            pltpu.VMEM((row_count, head_size), jnp.bfloat16),
            pltpu.SemaphoreType.DMA((3,)),
        ],
        compiler_params=params,
    )(query_own, query_back, returned)
    grad_queries = jnp.swapaxes(query_out.reshape(group_size, row_count, head_size), 0, 1)
    return (grad_queries, key_out[:, None, :], value_out[:, None, :])


def solution(mesh):
    in_specs = (
        P(("outer", "inner"), "head", None),
        P(("outer", "inner"), "head", None),
        P(("outer", "inner"), "head", None),
        P(("outer", "inner"), "head", None),
        P(("outer", "inner"), "head", None),
        P("head", ("outer", "inner")),
        P(),
    )
    out_specs = (
        P(("outer", "inner"), "head", None),
        P(("outer", "inner"), "head", None),
        P(("outer", "inner"), "head", None),
    )
    return jax.shard_map(
        on_device, mesh=mesh, in_specs=in_specs, out_specs=out_specs, check_vma=False
    )
```

```python
import functools
import math

import jax
import jax.numpy as jnp
from jax import lax
from jax.experimental import pallas as pl
from jax.experimental.pallas import tpu as pltpu
from jax.sharding import PartitionSpec as P

LOG2E = math.log2(math.e)
STAT_ROWS = 16
SPLIT = 3


def contract(lhs, rhs, lhs_dim, rhs_dim):
    return lax.dot_general(
        lhs, rhs, (((lhs_dim,), (rhs_dim,)), ((), ())), preferred_element_type=jnp.float32
    )


def packet_rows(sizes):
    group_size, row_count, _ = sizes
    return 2 * group_size * row_count + SPLIT * STAT_ROWS


def slot_offset(slot, outer_index, bits):
    offset = 0
    for step in range(bits):
        if (slot >> step) & 1:
            offset = offset | lax.shift_left(jnp.int32(1), lax.rem(outer_index + step, bits))
    return offset


def pair_kernel(key_hbm, value_hbm, pair_ref, sems):
    copies = [
        pltpu.make_async_copy(key_hbm, pair_ref.at[0, 0], sems.at[0]),
        pltpu.make_async_copy(value_hbm, pair_ref.at[0, 1], sems.at[1]),
    ]
    for copy in copies:
        copy.start()
    for copy in copies:
        copy.wait()


def pack_kernel(
    sizes, inner_count, bits, query_hbm, grad_hbm, out_hbm, norm_hbm, order_hbm,
    packet_ref, rank_ref, out_ref, norm_ref, stat_ref, order_ref, sems,
):
    group_size, row_count, _ = sizes
    half = group_size * row_count
    copies = [
        pltpu.make_async_copy(source, target, sems.at[at])
        for at, (source, target) in enumerate(
            [
                (grad_hbm, packet_ref.at[pl.ds(half, half)]),
                (out_hbm, out_ref),
                (norm_hbm, norm_ref),
                (order_hbm, order_ref),
                (query_hbm, packet_ref.at[pl.ds(0, half)]),
            ]
        )
    ]
    for copy in copies:
        copy.start()
    stat_ref[...] = jnp.zeros_like(stat_ref)
    for copy in copies[:3]:
        copy.wait()
    stat_ref[:group_size] = norm_ref[...]
    for head in range(group_size):
        rows = slice(head * row_count, (head + 1) * row_count)
        grads = packet_ref[half + head * row_count : half + (head + 1) * row_count, :]
        product = grads.astype(jnp.float32) * out_ref[rows, :].astype(jnp.float32)
        stat_ref[8 + head : 9 + head, :] = jnp.sum(product.T, axis=0, keepdims=True)
    rest = jnp.clip(stat_ref[...], -3.38e38, 3.38e38)
    for term in range(SPLIT):
        piece = rest.astype(jnp.bfloat16)
        start = 2 * half + term * STAT_ROWS
        packet_ref[start : start + STAT_ROWS, :] = piece
        rest = rest - piece.astype(jnp.float32)
    copies[3].wait()
    my_index = lax.axis_index("inner")
    outer_index = lax.axis_index("outer")
    for slot in range(inner_count):
        peer = my_index ^ slot_offset(slot, outer_index, bits)
        rank_ref[slot : slot + 1, :] = jnp.full((1, row_count), order_ref[peer], jnp.int32)
    copies[4].wait()


def packet_stats(packet_ref, sizes):
    group_size, row_count, _ = sizes
    start = 2 * group_size * row_count
    pieces = [
        packet_ref[start + term * STAT_ROWS : start + (term + 1) * STAT_ROWS, :].astype(jnp.float32)
        for term in range(SPLIT)
    ]
    stats = pieces[0] + (pieces[1] + pieces[2])
    return stats[:8] * LOG2E, stats[8:]


def block_terms(keys, values, visible, packet_ref, sizes):
    group_size, row_count, head_size = sizes
    half = group_size * row_count
    scale = LOG2E / math.sqrt(head_size)
    per_step = 2 if group_size % 2 == 0 else 1
    all_norms, all_dots = packet_stats(packet_ref, sizes)
    key_total = jnp.zeros((keys.shape[0], head_size), jnp.float32)
    value_total = jnp.zeros((keys.shape[0], head_size), jnp.float32)
    query_terms = []
    for first in range(0, group_size, per_step):
        start, stop = first * row_count, (first + per_step) * row_count
        queries = packet_ref[start:stop, :]
        grads = packet_ref[half + start : half + stop, :]
        scores = contract(keys, queries, 1, 1)
        grad_weights = contract(values, grads, 1, 1)
        weights_parts = []
        score_parts = []
        for at in range(per_step):
            head = first + at
            lanes = slice(at * row_count, (at + 1) * row_count)
            weights = jnp.exp2(scores[:, lanes] * scale - all_norms[head : head + 1, :])
            if visible is not None:
                weights = jnp.where(visible, weights, 0.0)
            weights_parts.append(weights.astype(jnp.bfloat16))
            score_parts.append(
                (weights * (grad_weights[:, lanes] - all_dots[head : head + 1, :])).astype(jnp.bfloat16)
            )
        weights_half = jnp.concatenate(weights_parts, axis=1)
        grad_scores = jnp.concatenate(score_parts, axis=1)
        value_total += contract(weights_half, grads, 1, 0)
        key_total += contract(grad_scores, queries, 1, 0)
        query_terms.append(contract(keys, grad_scores, 0, 0))
    return key_total, value_total, jnp.concatenate(query_terms, axis=1)


def visible_rows(rank_ref, slots, inner_count, row_count):
    span_rows = row_count // 2
    key_rows = lax.broadcasted_iota(jnp.int32, (row_count, row_count), 0)
    my_rows = lax.broadcasted_iota(jnp.int32, (row_count, row_count), 1)

    def positions(rank, rows):
        return jnp.where(
            rows < span_rows,
            rank * span_rows + rows,
            (2 * inner_count - 2 - rank) * span_rows + rows,
        )

    mine = positions(rank_ref[0:1, :], my_rows)
    return jnp.concatenate(
        [positions(rank_ref[slot : slot + 1, :], key_rows) <= mine for slot in slots], axis=0
    )


def stacked(blocks_ref, which):
    return jnp.concatenate([blocks_ref[at, which] for at in range(blocks_ref.shape[0])], axis=0)


def near_kernel(sizes, inner_count, packet_ref, rank_ref, blocks_ref, query_ref, total_ref):
    count = blocks_ref.shape[0]
    visible = visible_rows(rank_ref, range(count), inner_count, sizes[1])
    key_terms, value_terms, query_terms = block_terms(
        stacked(blocks_ref, 0), stacked(blocks_ref, 1), visible, packet_ref, sizes
    )
    query_ref[...] = query_terms
    total_ref[0] = key_terms
    total_ref[1] = value_terms


def near_next_kernel(
    sizes, outer_count, next_ref, blocks_ref, total_in, next_query_ref, total_ref
):
    has_next = lax.axis_index("outer") < outer_count - 1
    total_ref[...] = total_in[...]

    @pl.when(has_next)
    def _():
        key_terms, value_terms, query_terms = block_terms(
            stacked(blocks_ref, 0), stacked(blocks_ref, 1), None, next_ref, sizes
        )
        next_query_ref[...] = query_terms
        total_ref[0] += key_terms
        total_ref[1] += value_terms


def far_kernel(
    sizes, inner_count, outer_count, packet_ref, next_ref, rank_ref, blocks_ref, query_in,
    next_query_in, query_ref, next_query_ref, sums_ref, total_ref,
):
    _, row_count, head_size = sizes
    count = blocks_ref.shape[0]
    inv_root = 1.0 / math.sqrt(head_size)
    has_next = lax.axis_index("outer") < outer_count - 1
    keys, values = stacked(blocks_ref, 0), stacked(blocks_ref, 1)
    total_ref[...] = jnp.zeros_like(total_ref)

    @pl.when(has_next)
    def _():
        key_terms, value_terms, query_terms = block_terms(keys, values, None, next_ref, sizes)
        next_query_ref[...] = (next_query_in[...] + query_terms).astype(jnp.bfloat16)
        total_ref[0] = key_terms
        total_ref[1] = value_terms

    visible = visible_rows(rank_ref, range(count, 2 * count), inner_count, row_count)
    key_terms, value_terms, query_terms = block_terms(keys, values, visible, packet_ref, sizes)
    query_ref[...] = query_in[...] + query_terms
    key_terms = (key_terms + total_ref[0]) * inv_root
    value_terms += total_ref[1]
    for slot in range(count):
        rows = slice(slot * row_count, (slot + 1) * row_count)
        sums_ref[slot, 0] = key_terms[rows].astype(jnp.bfloat16)
        sums_ref[slot, 1] = value_terms[rows].astype(jnp.bfloat16)


def query_kernel(sizes, query_ref, back_ref, result_hbm, total_ref, result_ref, sem):
    group_size, row_count, head_size = sizes
    inv_root = 1.0 / math.sqrt(head_size)
    has_prev = lax.axis_index("outer") > 0
    total_ref[...] = query_ref[...]

    @pl.when(has_prev)
    def _():
        total_ref[...] += back_ref[...].astype(jnp.float32)

    for head in range(group_size):
        rows = slice(head * row_count, (head + 1) * row_count)
        result_ref[rows, :] = (total_ref[:, rows] * inv_root).T.astype(jnp.bfloat16)
    copy = pltpu.make_async_copy(result_ref, result_hbm, sem)
    copy.start()
    copy.wait()


def turn_kernel(sizes, slots, total_ref, *refs):
    _, row_count, head_size = sizes
    inv_root = 1.0 / math.sqrt(head_size)
    returned, send_ref = refs[:-1], refs[-1]
    for at, slot in enumerate(slots):
        rows = slice(slot * row_count, (slot + 1) * row_count)
        for which, factor in ((0, inv_root), (1, 1.0)):
            total = total_ref[which, rows, :] * factor
            for ref in returned:
                total += ref[slot, which].astype(jnp.float32)
            send_ref[at, which] = total.astype(jnp.bfloat16)


def sum_kernel(sizes, *refs):
    _, row_count, head_size = sizes
    inv_root = 1.0 / math.sqrt(head_size)
    total_ref, returned = refs[0], refs[1:-5]
    key_hbm, value_hbm, key_ref, value_ref, sems = refs[-5:]
    key_total = total_ref[0, :row_count, :] * inv_root
    value_total = total_ref[1, :row_count, :]
    for ref in returned:
        key_total += ref[0, 0].astype(jnp.float32)
        value_total += ref[0, 1].astype(jnp.float32)
    key_ref[...] = key_total.astype(jnp.bfloat16)
    value_ref[...] = value_total.astype(jnp.bfloat16)
    copies = [
        pltpu.make_async_copy(key_ref, key_hbm, sems.at[0]),
        pltpu.make_async_copy(value_ref, value_hbm, sems.at[1]),
    ]
    for copy in copies:
        copy.start()
    for copy in copies:
        copy.wait()


def on_device(queries, key_rows, value_rows, attn_out, grad_out, log_norms, pair_order):
    row_count, group_size, head_size = queries.shape
    inner_count = lax.axis_size("inner")
    outer_count = lax.axis_size("outer")
    bits = inner_count.bit_length() - 1
    assert inner_count == 1 << bits and bits > 0
    sizes = (group_size, row_count, head_size)
    half = group_size * row_count
    near = inner_count // 2

    def flat(array):
        return jnp.swapaxes(array, 0, 1).reshape(-1, head_size)

    def in_hbm(array):
        return pltpu.with_memory_space_constraint(array, pltpu.HBM)

    def to_segment(block, ahead):
        route = [(at, (at + ahead) % outer_count) for at in range(outer_count)]
        return lax.ppermute(block, "outer", route)

    def exchange(block, step):
        route = []
        for inner in range(inner_count):
            for outer in range(outer_count):
                peer = inner ^ (1 << ((step + outer) % bits))
                route.append((inner * outer_count + outer, peer * outer_count + outer))
        return lax.ppermute(block, ("inner", "outer"), route)

    vmem = pl.BlockSpec(memory_space=pltpu.VMEM)
    hbm = pl.BlockSpec(memory_space=pltpu.HBM)
    roomy = pltpu.CompilerParams(vmem_limit_bytes=32 * 2**20)

    def shape(dims, dtype):
        return jax.ShapeDtypeStruct(dims, dtype)

    def cost(blocks, data=2**20):
        each = group_size * row_count * row_count
        return pl.CostEstimate(
            flops=10 * blocks * each * head_size, bytes_accessed=data, transcendentals=blocks * each
        )

    pair = pl.pallas_call(
        pair_kernel,
        out_shape=shape((1, 2, row_count, head_size), jnp.bfloat16),
        in_specs=[hbm] * 2,
        out_specs=vmem,
        scratch_shapes=[pltpu.SemaphoreType.DMA((2,))],
        compiler_params=roomy,
    )(in_hbm(flat(key_rows)), in_hbm(flat(value_rows)))
    first = exchange(pair, 0)
    pack_inputs = (flat(queries), flat(grad_out), flat(attn_out), log_norms, pair_order)
    pair, pack_inputs = lax.optimization_barrier((pair, pack_inputs))

    packet, rank = pl.pallas_call(
        functools.partial(pack_kernel, sizes, inner_count, bits),
        out_shape=(
            shape((packet_rows(sizes), head_size), jnp.bfloat16),
            shape((max(8, inner_count), row_count), jnp.int32),
        ),
        in_specs=[hbm] * 5,
        out_specs=(vmem, vmem),
        scratch_shapes=[
            pltpu.VMEM((half, head_size), jnp.bfloat16),
            pltpu.VMEM((group_size, row_count), jnp.float32),
            pltpu.VMEM((STAT_ROWS, row_count), jnp.float32),
            pltpu.SMEM((inner_count,), jnp.int32),
            pltpu.SemaphoreType.DMA((5,)),
        ],
        cost_estimate=cost(1),
        compiler_params=roomy,
    )(*(in_hbm(array) for array in pack_inputs))
    first, packet = lax.optimization_barrier((first, packet))

    near_blocks = jnp.concatenate([pair, first], axis=0)
    next_packet = to_segment(packet, -1)
    for step in range(1, bits - 1):
        near_blocks = jnp.concatenate([near_blocks, exchange(near_blocks, step)], axis=0)
    far_blocks = exchange(near_blocks, bits - 1) if bits > 1 else first
    if bits == 1:
        near_blocks = pair

    query_near, near_total = pl.pallas_call(
        functools.partial(near_kernel, sizes, inner_count),
        out_shape=(
            shape((head_size, half), jnp.float32),
            shape((2, near * row_count, head_size), jnp.float32),
        ),
        in_specs=[vmem] * 3,
        out_specs=(vmem,) * 2,
        cost_estimate=cost(near),
        compiler_params=roomy,
    )(packet, rank, near_blocks)

    next_near, near_total = pl.pallas_call(
        functools.partial(near_next_kernel, sizes, outer_count),
        out_shape=(
            shape((head_size, half), jnp.float32),
            shape((2, near * row_count, head_size), jnp.float32),
        ),
        in_specs=[vmem] * 3,
        out_specs=(vmem,) * 2,
        cost_estimate=cost(near),
        compiler_params=roomy,
    )(next_packet, near_blocks, near_total)

    query_own, query_next, sums = pl.pallas_call(
        functools.partial(far_kernel, sizes, inner_count, outer_count),
        out_shape=(
            shape((head_size, half), jnp.float32),
            shape((head_size, half), jnp.bfloat16),
            shape((near, 2, row_count, head_size), jnp.bfloat16),
        ),
        in_specs=[vmem] * 6,
        out_specs=(vmem,) * 3,
        scratch_shapes=[pltpu.VMEM((2, near * row_count, head_size), jnp.float32)],
        cost_estimate=cost(2 * near),
        compiler_params=roomy,
    )(packet, next_packet, rank, far_blocks, query_near, next_near)

    returned = [exchange(sums, bits - 1)]
    query_back = to_segment(query_next, 1)

    query_out = pl.pallas_call(
        functools.partial(query_kernel, sizes),
        out_shape=shape((half, head_size), jnp.bfloat16),
        in_specs=[vmem] * 2,
        out_specs=hbm,
        scratch_shapes=[
            pltpu.VMEM((head_size, half), jnp.float32),
            pltpu.VMEM((half, head_size), jnp.bfloat16),
            pltpu.SemaphoreType.DMA,
        ],
        cost_estimate=cost(1),
        compiler_params=roomy,
    )(query_own, query_back)

    for step in range(bits - 2, -1, -1):
        slots = range(1 << step, 2 << step)
        send = pl.pallas_call(
            functools.partial(turn_kernel, sizes, slots),
            out_shape=shape((len(slots), 2, row_count, head_size), jnp.bfloat16),
            in_specs=[vmem] * (1 + len(returned)),
            out_specs=vmem,
            compiler_params=roomy,
        )(near_total, *returned)
        returned.append(exchange(send, step))

    near_total, query_out = lax.optimization_barrier((near_total, query_out))
    key_out, value_out = pl.pallas_call(
        functools.partial(sum_kernel, sizes),
        out_shape=(shape((row_count, head_size), jnp.bfloat16),) * 2,
        in_specs=[vmem] * (1 + len(returned)),
        out_specs=(hbm, hbm),
        scratch_shapes=[
            pltpu.VMEM((row_count, head_size), jnp.bfloat16),
            pltpu.VMEM((row_count, head_size), jnp.bfloat16),
            pltpu.SemaphoreType.DMA((2,)),
        ],
        compiler_params=roomy,
    )(near_total, *returned)
    grad_queries = jnp.swapaxes(query_out.reshape(group_size, row_count, head_size), 0, 1)
    return (grad_queries, key_out[:, None, :], value_out[:, None, :])


def solution(mesh):
    in_specs = (
        P(("outer", "inner"), "head", None),
        P(("outer", "inner"), "head", None),
        P(("outer", "inner"), "head", None),
        P(("outer", "inner"), "head", None),
        P(("outer", "inner"), "head", None),
        P("head", ("outer", "inner")),
        P(),
    )
    out_specs = (
        P(("outer", "inner"), "head", None),
        P(("outer", "inner"), "head", None),
        P(("outer", "inner"), "head", None),
    )
    return jax.shard_map(
        on_device, mesh=mesh, in_specs=in_specs, out_specs=out_specs, check_vma=False
    )
```

```python
import functools
import math

import jax
import jax.numpy as jnp
from jax import lax
from jax.experimental import pallas as pl
from jax.experimental.pallas import tpu as pltpu
from jax.sharding import PartitionSpec as P

LOG2E = math.log2(math.e)
STAT_ROWS = 16
SPLIT = 3


def contract(lhs, rhs, lhs_dim, rhs_dim):
    return lax.dot_general(
        lhs, rhs, (((lhs_dim,), (rhs_dim,)), ((), ())), preferred_element_type=jnp.float32
    )


def packet_rows(sizes):
    group_size, row_count, _ = sizes
    return 2 * group_size * row_count + SPLIT * STAT_ROWS


def load_kernel(
    sizes, inner_count, query_hbm, grad_hbm, out_hbm, norm_hbm, order_hbm, key_hbm, value_hbm,
    pair_ref, packet_ref, rank_ref, out_ref, norm_ref, stat_ref, order_ref, sems,
):
    group_size, row_count, _ = sizes
    half = group_size * row_count
    copies = [
        pltpu.make_async_copy(source, target, sems.at[at])
        for at, (source, target) in enumerate(
            [
                (order_hbm, order_ref),
                (norm_hbm, norm_ref),
                (grad_hbm, packet_ref.at[pl.ds(half, half)]),
                (out_hbm, out_ref),
                (key_hbm, pair_ref.at[0]),
                (value_hbm, pair_ref.at[1]),
                (query_hbm, packet_ref.at[pl.ds(0, half)]),
            ]
        )
    ]
    for copy in copies:
        copy.start()
    stat_ref[...] = jnp.zeros_like(stat_ref)
    copies[0].wait()
    my_index = lax.axis_index("inner")
    for step in range(inner_count):
        rank_ref[step : step + 1, :] = jnp.full((1, row_count), order_ref[my_index ^ step], jnp.int32)
    for copy in copies[1:4]:
        copy.wait()
    stat_ref[:group_size] = norm_ref[...]
    for head in range(group_size):
        rows = slice(head * row_count, (head + 1) * row_count)
        grads = packet_ref[half + head * row_count : half + (head + 1) * row_count, :]
        product = grads.astype(jnp.float32) * out_ref[rows, :].astype(jnp.float32)
        stat_ref[8 + head : 9 + head, :] = jnp.sum(product.T, axis=0, keepdims=True)
    rest = jnp.clip(stat_ref[...], -3.38e38, 3.38e38)
    for term in range(SPLIT):
        piece = rest.astype(jnp.bfloat16)
        start = 2 * half + term * STAT_ROWS
        packet_ref[start : start + STAT_ROWS, :] = piece
        rest = rest - piece.astype(jnp.float32)
    for copy in copies[4:]:
        copy.wait()


def packet_stats(packet_ref, sizes):
    group_size, row_count, _ = sizes
    start = 2 * group_size * row_count
    pieces = [
        packet_ref[start + term * STAT_ROWS : start + (term + 1) * STAT_ROWS, :].astype(jnp.float32)
        for term in range(SPLIT)
    ]
    stats = pieces[0] + (pieces[1] + pieces[2])
    return stats[:8] * LOG2E, stats[8:]


def block_terms(keys, values, visible, packet_ref, scores_ref, sizes):
    group_size, row_count, head_size = sizes
    half = group_size * row_count
    scale = LOG2E / math.sqrt(head_size)
    per_step = 2 if group_size % 2 == 0 else 1
    all_norms, all_dots = packet_stats(packet_ref, sizes)
    key_total = jnp.zeros((keys.shape[0], head_size), jnp.float32)
    value_total = jnp.zeros((keys.shape[0], head_size), jnp.float32)
    for first in range(0, group_size, per_step):
        start, stop = first * row_count, (first + per_step) * row_count
        queries = packet_ref[start:stop, :]
        grads = packet_ref[half + start : half + stop, :]
        scores = contract(keys, queries, 1, 1)
        grad_weights = contract(values, grads, 1, 1)
        weights_parts = []
        score_parts = []
        for at in range(per_step):
            head = first + at
            lanes = slice(at * row_count, (at + 1) * row_count)
            weights = jnp.exp2(scores[:, lanes] * scale - all_norms[head : head + 1, :])
            if visible is not None:
                weights = jnp.where(visible, weights, 0.0)
            weights_parts.append(weights.astype(jnp.bfloat16))
            score_parts.append(
                (weights * (grad_weights[:, lanes] - all_dots[head : head + 1, :])).astype(jnp.bfloat16)
            )
        weights_half = jnp.concatenate(weights_parts, axis=1)
        grad_scores = jnp.concatenate(score_parts, axis=1)
        scores_ref[:, start:stop] = grad_scores
        value_total += contract(weights_half, grads, 1, 0)
        key_total += contract(grad_scores, queries, 1, 0)
    return key_total, value_total


def visible_rows(rank_ref, steps, inner_count, row_count):
    span_rows = row_count // 2
    key_rows = lax.broadcasted_iota(jnp.int32, (row_count, row_count), 0)
    my_rows = lax.broadcasted_iota(jnp.int32, (row_count, row_count), 1)

    def positions(rank, rows):
        return jnp.where(
            rows < span_rows,
            rank * span_rows + rows,
            (2 * inner_count - 2 - rank) * span_rows + rows,
        )

    mine = positions(rank_ref[0:1, :], my_rows)
    return jnp.concatenate(
        [positions(rank_ref[step : step + 1, :], key_rows) <= mine for step in steps], axis=0
    )


def stacked(blocks, which):
    return jnp.concatenate([ref[which] for ref in blocks], axis=0)


def key_kernel(sizes, inner_count, outer_count, steps, packet_ref, next_ref, rank_ref, *refs):
    count = len(steps)
    _, row_count, _ = sizes
    blocks, (scores_ref, next_scores_ref, total_ref) = refs[:count], refs[count:]
    has_next = lax.axis_index("outer") < outer_count - 1
    keys, values = stacked(blocks, 0), stacked(blocks, 1)
    visible = visible_rows(rank_ref, steps, inner_count, row_count)
    key_terms, value_terms = block_terms(keys, values, visible, packet_ref, scores_ref, sizes)
    total_ref[0] = key_terms
    total_ref[1] = value_terms

    @pl.when(has_next)
    def _():
        key_terms, value_terms = block_terms(keys, values, None, next_ref, next_scores_ref, sizes)
        total_ref[0] += key_terms
        total_ref[1] += value_terms


def far_kernel(sizes, inner_count, outer_count, steps, packet_ref, next_ref, rank_ref, *refs):
    count = len(steps)
    _, row_count, head_size = sizes
    inv_root = 1.0 / math.sqrt(head_size)
    blocks, score_refs, sums, total_ref = refs[:count], refs[count : count + 2], refs[count + 2 : -1], refs[-1]
    key_kernel(
        sizes, inner_count, outer_count, steps, packet_ref, next_ref, rank_ref, *blocks, *score_refs, total_ref
    )
    for at, ref in enumerate(sums):
        rows = slice(at * row_count, (at + 1) * row_count)
        ref[0] = (total_ref[0, rows, :] * inv_root).astype(jnp.bfloat16)
        ref[1] = total_ref[1, rows, :].astype(jnp.bfloat16)


def query_terms(refs, lanes):
    scores = jnp.concatenate([refs[0][:, lanes], refs[1][:, lanes]], axis=0)
    return contract(stacked(refs[2:], 0), scores, 0, 0)


def back_kernel(sizes, outer_count, *refs):
    group_size, row_count, _ = sizes
    has_next = lax.axis_index("outer") < outer_count - 1

    @pl.when(has_next)
    def _():
        refs[-1][...] = query_terms(refs[:-1], slice(None)).astype(jnp.bfloat16)


def query_kernel(sizes, *refs):
    group_size, row_count, head_size = sizes
    inv_root = 1.0 / math.sqrt(head_size)
    back_ref, inputs = refs[0], refs[1:-4]
    result_hbm, total_ref, result_ref, sem = refs[-4:]
    has_prev = lax.axis_index("outer") > 0
    total_ref[...] = query_terms(inputs, slice(None))

    @pl.when(has_prev)
    def _():
        total_ref[...] += back_ref[...].astype(jnp.float32)

    for head in range(group_size):
        rows = slice(head * row_count, (head + 1) * row_count)
        result_ref[rows, :] = (total_ref[:, rows] * inv_root).T.astype(jnp.bfloat16)
    copy = pltpu.make_async_copy(result_ref, result_hbm, sem)
    copy.start()
    copy.wait()


def sum_kernel(sizes, *refs):
    _, _, head_size = sizes
    inv_root = 1.0 / math.sqrt(head_size)
    own_ref, returned = refs[0], refs[1:-5]
    key_hbm, value_hbm, key_ref, value_ref, sems = refs[-5:]
    key_total = own_ref[0] * inv_root
    value_total = own_ref[1]
    for ref in returned:
        key_total += ref[0].astype(jnp.float32)
        value_total += ref[1].astype(jnp.float32)
    key_ref[...] = key_total.astype(jnp.bfloat16)
    value_ref[...] = value_total.astype(jnp.bfloat16)
    copies = [
        pltpu.make_async_copy(key_ref, key_hbm, sems.at[0]),
        pltpu.make_async_copy(value_ref, value_hbm, sems.at[1]),
    ]
    for copy in copies:
        copy.start()
    for copy in copies:
        copy.wait()


def on_device(queries, key_rows, value_rows, attn_out, grad_out, log_norms, pair_order):
    row_count, group_size, head_size = queries.shape
    inner_count = lax.axis_size("inner")
    outer_count = lax.axis_size("outer")
    assert inner_count & (inner_count - 1) == 0 and inner_count > 1
    sizes = (group_size, row_count, head_size)
    half = group_size * row_count
    away = list(range(inner_count - 1, 0, -1))

    def flat(array):
        return jnp.swapaxes(array, 0, 1).reshape(-1, head_size)

    def in_hbm(array):
        return pltpu.with_memory_space_constraint(array, pltpu.HBM)

    def to_segment(block, ahead):
        route = [(at, (at + ahead) % outer_count) for at in range(outer_count)]
        return lax.ppermute(block, "outer", route)

    def exchange(block, step):
        return lax.ppermute(block, "inner", [(at, at ^ step) for at in range(inner_count)])

    vmem = pl.BlockSpec(memory_space=pltpu.VMEM)
    hbm = pl.BlockSpec(memory_space=pltpu.HBM)
    roomy = pltpu.CompilerParams(vmem_limit_bytes=32 * 2**20)

    def shape(dims, dtype):
        return jax.ShapeDtypeStruct(dims, dtype)

    def cost(blocks, data=2**20):
        each = group_size * row_count * row_count
        return pl.CostEstimate(
            flops=10 * blocks * each * head_size, bytes_accessed=data, transcendentals=blocks * each
        )

    block_shape = shape((2, row_count, head_size), jnp.bfloat16)

    pair, packet, rank = pl.pallas_call(
        functools.partial(load_kernel, sizes, inner_count),
        out_shape=(
            block_shape,
            shape((packet_rows(sizes), head_size), jnp.bfloat16),
            shape((max(8, inner_count), row_count), jnp.int32),
        ),
        in_specs=[hbm] * 7,
        out_specs=(vmem,) * 3,
        scratch_shapes=[
            pltpu.VMEM((half, head_size), jnp.bfloat16),
            pltpu.VMEM((group_size, row_count), jnp.float32),
            pltpu.VMEM((STAT_ROWS, row_count), jnp.float32),
            pltpu.SMEM((inner_count,), jnp.int32),
            pltpu.SemaphoreType.DMA((7,)),
        ],
        cost_estimate=cost(0),
        compiler_params=roomy,
    )(
        *(
            in_hbm(array)
            for array in (
                flat(queries), flat(grad_out), flat(attn_out), log_norms, pair_order,
                flat(key_rows), flat(value_rows),
            )
        )
    )
    next_packet = to_segment(packet, -1)
    blocks = {0: pair}
    for step in reversed(away):
        blocks[step] = exchange(pair, step)

    all_blocks = [blocks[step] for step in [0] + away]

    def scores_shape(count):
        return shape((count * row_count, half), jnp.bfloat16)

    near_scores, near_next_scores, own_total = pl.pallas_call(
        functools.partial(key_kernel, sizes, inner_count, outer_count, [0]),
        out_shape=(scores_shape(1), scores_shape(1), shape((2, row_count, head_size), jnp.float32)),
        in_specs=[vmem] * 4,
        out_specs=(vmem,) * 3,
        cost_estimate=cost(2),
        compiler_params=roomy,
    )(packet, next_packet, rank, pair)

    far_scores, far_next_scores, *sums = pl.pallas_call(
        functools.partial(far_kernel, sizes, inner_count, outer_count, away),
        out_shape=(scores_shape(len(away)),) * 2 + (block_shape,) * len(away),
        in_specs=[vmem] * (3 + len(away)),
        out_specs=(vmem,) * (2 + len(away)),
        scratch_shapes=[pltpu.VMEM((2, len(away) * row_count, head_size), jnp.float32)],
        cost_estimate=cost(2 * len(away)),
        compiler_params=roomy,
    )(packet, next_packet, rank, *all_blocks[1:])
    returned = [exchange(terms, step) for terms, step in zip(sums, away)]

    query_next = pl.pallas_call(
        functools.partial(back_kernel, sizes, outer_count),
        out_shape=shape((head_size, half), jnp.bfloat16),
        in_specs=[vmem] * (2 + inner_count),
        out_specs=vmem,
        cost_estimate=cost(inner_count),
        compiler_params=roomy,
    )(near_next_scores, far_next_scores, *all_blocks)
    query_back = to_segment(query_next, 1)

    query_out = pl.pallas_call(
        functools.partial(query_kernel, sizes),
        out_shape=shape((half, head_size), jnp.bfloat16),
        in_specs=[vmem] * (3 + inner_count),
        out_specs=hbm,
        scratch_shapes=[
            pltpu.VMEM((head_size, half), jnp.float32),
            pltpu.VMEM((half, head_size), jnp.bfloat16),
            pltpu.SemaphoreType.DMA,
        ],
        cost_estimate=cost(inner_count),
        compiler_params=roomy,
    )(query_back, near_scores, far_scores, *all_blocks)

    own_total, query_out = lax.optimization_barrier((own_total, query_out))
    key_out, value_out = pl.pallas_call(
        functools.partial(sum_kernel, sizes),
        out_shape=(shape((row_count, head_size), jnp.bfloat16),) * 2,
        in_specs=[vmem] * (1 + len(returned)),
        out_specs=(hbm, hbm),
        scratch_shapes=[
            pltpu.VMEM((row_count, head_size), jnp.bfloat16),
            pltpu.VMEM((row_count, head_size), jnp.bfloat16),
            pltpu.SemaphoreType.DMA((2,)),
        ],
        compiler_params=roomy,
    )(own_total, *returned)
    grad_queries = jnp.swapaxes(query_out.reshape(group_size, row_count, head_size), 0, 1)
    return (grad_queries, key_out[:, None, :], value_out[:, None, :])


def solution(mesh):
    in_specs = (
        P(("outer", "inner"), "head", None),
        P(("outer", "inner"), "head", None),
        P(("outer", "inner"), "head", None),
        P(("outer", "inner"), "head", None),
        P(("outer", "inner"), "head", None),
        P("head", ("outer", "inner")),
        P(),
    )
    out_specs = (
        P(("outer", "inner"), "head", None),
        P(("outer", "inner"), "head", None),
        P(("outer", "inner"), "head", None),
    )
    return jax.shard_map(
        on_device, mesh=mesh, in_specs=in_specs, out_specs=out_specs, check_vma=False
    )
```

```python
import functools
import math

import jax
import jax.numpy as jnp
from jax import lax
from jax.experimental import pallas as pl
from jax.experimental.pallas import tpu as pltpu
from jax.sharding import PartitionSpec as P

LOG2E = math.log2(math.e)
STAT_ROWS = 16
SPLIT = 3


def contract(lhs, rhs, lhs_dim, rhs_dim):
    return lax.dot_general(
        lhs, rhs, (((lhs_dim,), (rhs_dim,)), ((), ())), preferred_element_type=jnp.float32
    )


def packet_rows(sizes):
    group_size, row_count, _ = sizes
    return 2 * group_size * row_count + SPLIT * STAT_ROWS


def peer_offset(step, outer, inner_count):
    bits = inner_count.bit_length() - 1
    turn = outer % 2
    return ((step << turn) | (step >> (bits - turn))) & (inner_count - 1)


def load_kernel(
    sizes, inner_count, query_hbm, grad_hbm, out_hbm, norm_hbm, order_hbm, key_hbm, value_hbm,
    pair_ref, packet_ref, rank_ref, out_ref, norm_ref, stat_ref, order_ref, sems,
):
    group_size, row_count, _ = sizes
    half = group_size * row_count
    copies = [
        pltpu.make_async_copy(source, target, sems.at[at])
        for at, (source, target) in enumerate(
            [
                (order_hbm, order_ref),
                (norm_hbm, norm_ref),
                (grad_hbm, packet_ref.at[pl.ds(half, half)]),
                (out_hbm, out_ref),
                (key_hbm, pair_ref.at[0]),
                (value_hbm, pair_ref.at[1]),
                (query_hbm, packet_ref.at[pl.ds(0, half)]),
            ]
        )
    ]
    for copy in copies:
        copy.start()
    stat_ref[...] = jnp.zeros_like(stat_ref)
    copies[0].wait()
    my_index = lax.axis_index("inner")
    turned = lax.rem(lax.axis_index("outer"), 2) == 1
    for step in range(inner_count):
        offset = jnp.where(turned, peer_offset(step, 1, inner_count), peer_offset(step, 0, inner_count))
        rank_ref[step : step + 1, :] = jnp.full((1, row_count), order_ref[my_index ^ offset], jnp.int32)
    for copy in copies[1:4]:
        copy.wait()
    stat_ref[:group_size] = norm_ref[...]
    for head in range(group_size):
        rows = slice(head * row_count, (head + 1) * row_count)
        grads = packet_ref[half + head * row_count : half + (head + 1) * row_count, :]
        product = grads.astype(jnp.float32) * out_ref[rows, :].astype(jnp.float32)
        stat_ref[8 + head : 9 + head, :] = jnp.sum(product.T, axis=0, keepdims=True)
    rest = jnp.clip(stat_ref[...], -3.38e38, 3.38e38)
    for term in range(SPLIT):
        piece = rest.astype(jnp.bfloat16)
        start = 2 * half + term * STAT_ROWS
        packet_ref[start : start + STAT_ROWS, :] = piece
        rest = rest - piece.astype(jnp.float32)
    for copy in copies[4:]:
        copy.wait()


def packet_stats(packet_ref, sizes):
    group_size, row_count, _ = sizes
    start = 2 * group_size * row_count
    pieces = [
        packet_ref[start + term * STAT_ROWS : start + (term + 1) * STAT_ROWS, :].astype(jnp.float32)
        for term in range(SPLIT)
    ]
    stats = pieces[0] + (pieces[1] + pieces[2])
    return stats[:8] * LOG2E, stats[8:]


def block_terms(keys, values, visible, packet_ref, scores_ref, sizes):
    group_size, row_count, head_size = sizes
    half = group_size * row_count
    scale = LOG2E / math.sqrt(head_size)
    per_step = 2 if group_size % 2 == 0 else 1
    all_norms, all_dots = packet_stats(packet_ref, sizes)
    key_total = jnp.zeros((keys.shape[0], head_size), jnp.float32)
    value_total = jnp.zeros((keys.shape[0], head_size), jnp.float32)
    for first in range(0, group_size, per_step):
        start, stop = first * row_count, (first + per_step) * row_count
        queries = packet_ref[start:stop, :]
        grads = packet_ref[half + start : half + stop, :]
        scores = contract(keys, queries, 1, 1)
        grad_weights = contract(values, grads, 1, 1)
        weights_parts = []
        score_parts = []
        for at in range(per_step):
            head = first + at
            lanes = slice(at * row_count, (at + 1) * row_count)
            weights = jnp.exp2(scores[:, lanes] * scale - all_norms[head : head + 1, :])
            if visible is not None:
                weights = jnp.where(visible, weights, 0.0)
            weights_parts.append(weights.astype(jnp.bfloat16))
            score_parts.append(
                (weights * (grad_weights[:, lanes] - all_dots[head : head + 1, :])).astype(jnp.bfloat16)
            )
        weights_half = jnp.concatenate(weights_parts, axis=1)
        grad_scores = jnp.concatenate(score_parts, axis=1)
        scores_ref[:, start:stop] = grad_scores
        value_total += contract(weights_half, grads, 1, 0)
        key_total += contract(grad_scores, queries, 1, 0)
    return key_total, value_total


def visible_rows(rank_ref, steps, inner_count, row_count):
    span_rows = row_count // 2
    key_rows = lax.broadcasted_iota(jnp.int32, (row_count, row_count), 0)
    my_rows = lax.broadcasted_iota(jnp.int32, (row_count, row_count), 1)

    def positions(rank, rows):
        return jnp.where(
            rows < span_rows,
            rank * span_rows + rows,
            (2 * inner_count - 2 - rank) * span_rows + rows,
        )

    mine = positions(rank_ref[0:1, :], my_rows)
    return jnp.concatenate(
        [positions(rank_ref[step : step + 1, :], key_rows) <= mine for step in steps], axis=0
    )


def stacked(blocks, which):
    return jnp.concatenate([ref[which] for ref in blocks], axis=0)


def key_kernel(sizes, inner_count, outer_count, steps, packet_ref, next_ref, rank_ref, *refs):
    count = len(steps)
    _, row_count, _ = sizes
    blocks, (scores_ref, next_scores_ref, total_ref) = refs[:count], refs[count:]
    has_next = lax.axis_index("outer") < outer_count - 1
    keys, values = stacked(blocks, 0), stacked(blocks, 1)
    visible = visible_rows(rank_ref, steps, inner_count, row_count)
    key_terms, value_terms = block_terms(keys, values, visible, packet_ref, scores_ref, sizes)
    total_ref[0] = key_terms
    total_ref[1] = value_terms

    @pl.when(has_next)
    def _():
        key_terms, value_terms = block_terms(keys, values, None, next_ref, next_scores_ref, sizes)
        total_ref[0] += key_terms
        total_ref[1] += value_terms


def far_kernel(sizes, inner_count, outer_count, steps, packet_ref, next_ref, rank_ref, *refs):
    count = len(steps)
    _, row_count, head_size = sizes
    inv_root = 1.0 / math.sqrt(head_size)
    blocks, score_refs, sums, total_ref = refs[:count], refs[count : count + 2], refs[count + 2 : -1], refs[-1]
    key_kernel(
        sizes, inner_count, outer_count, steps, packet_ref, next_ref, rank_ref, *blocks, *score_refs, total_ref
    )
    for at, ref in enumerate(sums):
        rows = slice(at * row_count, (at + 1) * row_count)
        ref[0] = (total_ref[0, rows, :] * inv_root).astype(jnp.bfloat16)
        ref[1] = total_ref[1, rows, :].astype(jnp.bfloat16)


def query_terms(refs, lanes):
    scores = jnp.concatenate([refs[0][:, lanes], refs[1][:, lanes]], axis=0)
    return contract(stacked(refs[2:], 0), scores, 0, 0)


def back_kernel(sizes, outer_count, *refs):
    group_size, row_count, _ = sizes
    has_next = lax.axis_index("outer") < outer_count - 1

    @pl.when(has_next)
    def _():
        refs[-1][...] = query_terms(refs[:-1], slice(None)).astype(jnp.bfloat16)


def query_kernel(sizes, *refs):
    group_size, row_count, head_size = sizes
    inv_root = 1.0 / math.sqrt(head_size)
    back_ref, inputs = refs[0], refs[1:-4]
    result_hbm, total_ref, result_ref, sem = refs[-4:]
    has_prev = lax.axis_index("outer") > 0
    total_ref[...] = query_terms(inputs, slice(None))

    @pl.when(has_prev)
    def _():
        total_ref[...] += back_ref[...].astype(jnp.float32)

    for head in range(group_size):
        rows = slice(head * row_count, (head + 1) * row_count)
        result_ref[rows, :] = (total_ref[:, rows] * inv_root).T.astype(jnp.bfloat16)
    copy = pltpu.make_async_copy(result_ref, result_hbm, sem)
    copy.start()
    copy.wait()


def sum_kernel(sizes, *refs):
    _, _, head_size = sizes
    inv_root = 1.0 / math.sqrt(head_size)
    own_ref, returned = refs[0], refs[1:-5]
    key_hbm, value_hbm, key_ref, value_ref, sems = refs[-5:]
    key_total = own_ref[0] * inv_root
    value_total = own_ref[1]
    for ref in returned:
        key_total += ref[0].astype(jnp.float32)
        value_total += ref[1].astype(jnp.float32)
    key_ref[...] = key_total.astype(jnp.bfloat16)
    value_ref[...] = value_total.astype(jnp.bfloat16)
    copies = [
        pltpu.make_async_copy(key_ref, key_hbm, sems.at[0]),
        pltpu.make_async_copy(value_ref, value_hbm, sems.at[1]),
    ]
    for copy in copies:
        copy.start()
    for copy in copies:
        copy.wait()


def on_device(queries, key_rows, value_rows, attn_out, grad_out, log_norms, pair_order):
    row_count, group_size, head_size = queries.shape
    inner_count = lax.axis_size("inner")
    outer_count = lax.axis_size("outer")
    assert inner_count & (inner_count - 1) == 0 and inner_count > 1
    sizes = (group_size, row_count, head_size)
    half = group_size * row_count
    away = list(range(inner_count - 1, 0, -1))

    def flat(array):
        return jnp.swapaxes(array, 0, 1).reshape(-1, head_size)

    def in_hbm(array):
        return pltpu.with_memory_space_constraint(array, pltpu.HBM)

    def to_segment(block, ahead):
        route = [(at, (at + ahead) % outer_count) for at in range(outer_count)]
        return lax.ppermute(block, "outer", route)

    def exchange(block, step):
        route = []
        for inner in range(inner_count):
            for outer in range(outer_count):
                peer = inner ^ peer_offset(step, outer, inner_count)
                route.append((inner * outer_count + outer, peer * outer_count + outer))
        return lax.ppermute(block, ("inner", "outer"), route)

    vmem = pl.BlockSpec(memory_space=pltpu.VMEM)
    hbm = pl.BlockSpec(memory_space=pltpu.HBM)
    roomy = pltpu.CompilerParams(vmem_limit_bytes=32 * 2**20)

    def shape(dims, dtype):
        return jax.ShapeDtypeStruct(dims, dtype)

    def cost(blocks, data=2**20):
        each = group_size * row_count * row_count
        return pl.CostEstimate(
            flops=10 * blocks * each * head_size, bytes_accessed=data, transcendentals=blocks * each
        )

    block_shape = shape((2, row_count, head_size), jnp.bfloat16)

    pair, packet, rank = pl.pallas_call(
        functools.partial(load_kernel, sizes, inner_count),
        out_shape=(
            block_shape,
            shape((packet_rows(sizes), head_size), jnp.bfloat16),
            shape((max(8, inner_count), row_count), jnp.int32),
        ),
        in_specs=[hbm] * 7,
        out_specs=(vmem,) * 3,
        scratch_shapes=[
            pltpu.VMEM((half, head_size), jnp.bfloat16),
            pltpu.VMEM((group_size, row_count), jnp.float32),
            pltpu.VMEM((STAT_ROWS, row_count), jnp.float32),
            pltpu.SMEM((inner_count,), jnp.int32),
            pltpu.SemaphoreType.DMA((7,)),
        ],
        cost_estimate=cost(0),
        compiler_params=roomy,
    )(
        *(
            in_hbm(array)
            for array in (
                flat(queries), flat(grad_out), flat(attn_out), log_norms, pair_order,
                flat(key_rows), flat(value_rows),
            )
        )
    )
    next_packet = to_segment(packet, -1)
    blocks = {0: pair}
    for step in away:
        blocks[step] = exchange(pair, step)

    arrival = away[::-1]
    all_blocks = [blocks[step] for step in [0] + arrival]

    def scores_shape(count):
        return shape((count * row_count, half), jnp.bfloat16)

    near_scores, near_next_scores, own_total = pl.pallas_call(
        functools.partial(key_kernel, sizes, inner_count, outer_count, [0]),
        out_shape=(scores_shape(1), scores_shape(1), shape((2, row_count, head_size), jnp.float32)),
        in_specs=[vmem] * 4,
        out_specs=(vmem,) * 3,
        cost_estimate=cost(2),
        compiler_params=roomy,
    )(packet, next_packet, rank, pair)

    far_scores, far_next_scores, *sums = pl.pallas_call(
        functools.partial(far_kernel, sizes, inner_count, outer_count, arrival),
        out_shape=(scores_shape(len(away)),) * 2 + (block_shape,) * len(away),
        in_specs=[vmem] * (3 + len(away)),
        out_specs=(vmem,) * (2 + len(away)),
        scratch_shapes=[pltpu.VMEM((2, len(away) * row_count, head_size), jnp.float32)],
        cost_estimate=cost(2 * len(away)),
        compiler_params=roomy,
    )(packet, next_packet, rank, *all_blocks[1:])
    returned = [exchange(terms, step) for terms, step in zip(sums[::-1], away)]

    query_next = pl.pallas_call(
        functools.partial(back_kernel, sizes, outer_count),
        out_shape=shape((head_size, half), jnp.bfloat16),
        in_specs=[vmem] * (2 + inner_count),
        out_specs=vmem,
        cost_estimate=cost(inner_count),
        compiler_params=roomy,
    )(near_next_scores, far_next_scores, *all_blocks)
    query_back = to_segment(query_next, 1)

    query_out = pl.pallas_call(
        functools.partial(query_kernel, sizes),
        out_shape=shape((half, head_size), jnp.bfloat16),
        in_specs=[vmem] * (3 + inner_count),
        out_specs=hbm,
        scratch_shapes=[
            pltpu.VMEM((head_size, half), jnp.float32),
            pltpu.VMEM((half, head_size), jnp.bfloat16),
            pltpu.SemaphoreType.DMA,
        ],
        cost_estimate=cost(inner_count),
        compiler_params=roomy,
    )(query_back, near_scores, far_scores, *all_blocks)

    own_total, query_out = lax.optimization_barrier((own_total, query_out))
    key_out, value_out = pl.pallas_call(
        functools.partial(sum_kernel, sizes),
        out_shape=(shape((row_count, head_size), jnp.bfloat16),) * 2,
        in_specs=[vmem] * (1 + len(returned)),
        out_specs=(hbm, hbm),
        scratch_shapes=[
            pltpu.VMEM((row_count, head_size), jnp.bfloat16),
            pltpu.VMEM((row_count, head_size), jnp.bfloat16),
            pltpu.SemaphoreType.DMA((2,)),
        ],
        compiler_params=roomy,
    )(own_total, *returned)
    grad_queries = jnp.swapaxes(query_out.reshape(group_size, row_count, head_size), 0, 1)
    return (grad_queries, key_out[:, None, :], value_out[:, None, :])


def solution(mesh):
    in_specs = (
        P(("outer", "inner"), "head", None),
        P(("outer", "inner"), "head", None),
        P(("outer", "inner"), "head", None),
        P(("outer", "inner"), "head", None),
        P(("outer", "inner"), "head", None),
        P("head", ("outer", "inner")),
        P(),
    )
    out_specs = (
        P(("outer", "inner"), "head", None),
        P(("outer", "inner"), "head", None),
        P(("outer", "inner"), "head", None),
    )
    return jax.shard_map(
        on_device, mesh=mesh, in_specs=in_specs, out_specs=out_specs, check_vma=False
    )
```

```python
import functools
import math

import jax
import jax.numpy as jnp
from jax import lax
from jax.experimental import pallas as pl
from jax.experimental.pallas import tpu as pltpu
from jax.sharding import PartitionSpec as P

LOG2E = math.log2(math.e)
STAT_ROWS = 16
SPLIT = 3


def contract(lhs, rhs, lhs_dim, rhs_dim):
    return lax.dot_general(
        lhs, rhs, (((lhs_dim,), (rhs_dim,)), ((), ())), preferred_element_type=jnp.float32
    )


def packet_rows(sizes):
    group_size, row_count, _ = sizes
    return 3 * group_size * row_count + SPLIT * STAT_ROWS


def peer_offset(step, outer, inner_count):
    bits = inner_count.bit_length() - 1
    turn = outer % 2
    return ((step << turn) | (step >> (bits - turn))) & (inner_count - 1)


def load_kernel(
    sizes, query_hbm, grad_hbm, out_hbm, norm_hbm, key_hbm, value_hbm, pair_ref, packet_ref, norm_ref, sems
):
    group_size, row_count, _ = sizes
    half = group_size * row_count
    copies = [
        pltpu.make_async_copy(source, target, sems.at[at])
        for at, (source, target) in enumerate(
            [
                (norm_hbm, norm_ref.at[pl.ds(0, group_size)]),
                (key_hbm, pair_ref.at[0]),
                (value_hbm, pair_ref.at[1]),
                (query_hbm, packet_ref.at[pl.ds(0, half)]),
                (grad_hbm, packet_ref.at[pl.ds(half, half)]),
                (out_hbm, packet_ref.at[pl.ds(2 * half, half)]),
            ]
        )
    ]
    for copy in copies:
        copy.start()
    copies[0].wait()
    held = lax.broadcasted_iota(jnp.int32, (STAT_ROWS, row_count), 0) < group_size
    rest = jnp.where(held, jnp.clip(norm_ref[...], -3.38e38, 3.38e38), 0.0)
    for term in range(SPLIT):
        piece = rest.astype(jnp.bfloat16)
        start = 3 * half + term * STAT_ROWS
        packet_ref[start : start + STAT_ROWS, :] = piece
        rest = rest - piece.astype(jnp.float32)
    for copy in copies[1:]:
        copy.wait()


def row_stats(packet_ref, stat_ref, sizes):
    group_size, row_count, _ = sizes
    half = group_size * row_count
    start = 3 * half
    pieces = [
        packet_ref[start + term * STAT_ROWS : start + (term + 1) * STAT_ROWS, :].astype(jnp.float32)
        for term in range(SPLIT)
    ]
    stat_ref[...] = (pieces[0] + (pieces[1] + pieces[2])) * LOG2E
    for head in range(group_size):
        first = head * row_count
        grads = packet_ref[half + first : half + first + row_count, :].astype(jnp.float32)
        outs = packet_ref[2 * half + first : 2 * half + first + row_count, :].astype(jnp.float32)
        stat_ref[8 + head : 9 + head, :] = jnp.sum((grads * outs).T, axis=0, keepdims=True)


def block_terms(keys, values, parts, sizes):
    group_size, row_count, head_size = sizes
    half = group_size * row_count
    scale = LOG2E / math.sqrt(head_size)
    per_step = 2 if group_size % 2 == 0 else 1
    key_total = 0.0
    value_total = 0.0
    for packet_ref, stats, visible, scores_ref in parts:
        weights_parts = []
        score_parts = []
        for first in range(0, group_size, per_step):
            start, stop = first * row_count, (first + per_step) * row_count
            queries = packet_ref[start:stop, :]
            grads = packet_ref[half + start : half + stop, :]
            scores = contract(keys, queries, 1, 1)
            grad_weights = contract(values, grads, 1, 1)
            for at in range(per_step):
                head = first + at
                lanes = slice(at * row_count, (at + 1) * row_count)
                weights = jnp.exp2(scores[:, lanes] * scale - stats[head : head + 1, :])
                if visible is not None:
                    weights = jnp.where(visible, weights, 0.0)
                weights_parts.append(weights.astype(jnp.bfloat16))
                score_parts.append(
                    (weights * (grad_weights[:, lanes] - stats[8 + head : 9 + head, :])).astype(jnp.bfloat16)
                )
        grad_scores = jnp.concatenate(score_parts, axis=1)
        scores_ref[...] = grad_scores
        value_total += contract(jnp.concatenate(weights_parts, axis=1), packet_ref[half : 2 * half, :], 1, 0)
        key_total += contract(grad_scores, packet_ref[:half, :], 1, 0)
    return key_total, value_total


def visible_rows(rank_ref, steps, inner_count, row_count):
    span_rows = row_count // 2
    key_rows = lax.broadcasted_iota(jnp.int32, (row_count, row_count), 0)
    my_rows = lax.broadcasted_iota(jnp.int32, (row_count, row_count), 1)

    def positions(rank, rows):
        return jnp.where(
            rows < span_rows,
            rank * span_rows + rows,
            (2 * inner_count - 2 - rank) * span_rows + rows,
        )

    mine = positions(rank_ref[0:1, :], my_rows)
    return jnp.concatenate(
        [positions(rank_ref[step : step + 1, :], key_rows) <= mine for step in steps], axis=0
    )


def stacked(blocks, which):
    return jnp.concatenate([ref[which] for ref in blocks], axis=0)


def near_kernel(
    sizes, inner_count, outer_count, packet_ref, next_ref, order_hbm, pair_ref, scores_ref,
    next_scores_ref, total_ref, stat_ref, rank_ref, order_ref, sem,
):
    _, row_count, _ = sizes
    copy = pltpu.make_async_copy(order_hbm, order_ref, sem)
    copy.start()
    has_next = lax.axis_index("outer") < outer_count - 1
    row_stats(packet_ref, stat_ref.at[0], sizes)
    row_stats(next_ref, stat_ref.at[1], sizes)

    @pl.when(jnp.logical_not(has_next))
    def _():
        stat_ref[1, :8, :] = jnp.full((8, row_count), 1e30, jnp.float32)

    key_rows = lax.broadcasted_iota(jnp.int32, (row_count, row_count), 0)
    visible = key_rows <= lax.broadcasted_iota(jnp.int32, (row_count, row_count), 1)
    parts = ((packet_ref, stat_ref[0], visible, scores_ref), (next_ref, stat_ref[1], None, next_scores_ref))
    total_ref[0], total_ref[1] = block_terms(pair_ref[0], pair_ref[1], parts, sizes)
    copy.wait()
    my_index = lax.axis_index("inner")
    turned = lax.rem(lax.axis_index("outer"), 2) == 1
    for step in range(inner_count):
        offset = jnp.where(turned, peer_offset(step, 1, inner_count), peer_offset(step, 0, inner_count))
        rank_ref[step : step + 1, :] = jnp.full((1, row_count), order_ref[my_index ^ offset], jnp.int32)


def far_kernel(sizes, inner_count, steps, packet_ref, next_ref, rank_ref, stat_ref, *refs):
    count = len(steps)
    _, row_count, head_size = sizes
    inv_root = 1.0 / math.sqrt(head_size)
    blocks, (scores_ref, next_scores_ref), sums = refs[:count], refs[count : count + 2], refs[count + 2 :]
    visible = visible_rows(rank_ref, steps, inner_count, row_count)
    parts = ((packet_ref, stat_ref[0], visible, scores_ref), (next_ref, stat_ref[1], None, next_scores_ref))
    key_total, value_total = block_terms(stacked(blocks, 0), stacked(blocks, 1), parts, sizes)
    for at, ref in enumerate(sums):
        rows = slice(at * row_count, (at + 1) * row_count)
        ref[0] = (key_total[rows] * inv_root).astype(jnp.bfloat16)
        ref[1] = value_total[rows].astype(jnp.bfloat16)


def query_terms(refs, groups, lanes):
    scores = jnp.concatenate([ref[:, lanes] for ref in refs[:groups]], axis=0)
    return contract(stacked(refs[groups:], 0), scores, 0, 0)


def back_kernel(sizes, outer_count, groups, *refs):
    group_size, row_count, _ = sizes
    has_next = lax.axis_index("outer") < outer_count - 1

    @pl.when(has_next)
    def _():
        refs[-1][...] = query_terms(refs[:-1], groups, slice(None)).astype(jnp.bfloat16)


def query_kernel(sizes, groups, *refs):
    group_size, row_count, head_size = sizes
    inv_root = 1.0 / math.sqrt(head_size)
    back_ref, inputs = refs[0], refs[1:-4]
    result_hbm, total_ref, result_ref, sem = refs[-4:]
    has_prev = lax.axis_index("outer") > 0
    total_ref[...] = query_terms(inputs, groups, slice(None))

    @pl.when(has_prev)
    def _():
        total_ref[...] += back_ref[...].astype(jnp.float32)

    for head in range(group_size):
        rows = slice(head * row_count, (head + 1) * row_count)
        result_ref[rows, :] = (total_ref[:, rows] * inv_root).T.astype(jnp.bfloat16)
    copy = pltpu.make_async_copy(result_ref, result_hbm, sem)
    copy.start()
    copy.wait()


def early_kernel(sizes, *refs):
    inv_root = 1.0 / math.sqrt(sizes[2])
    own_ref, returned, total_ref = refs[0], refs[1:-1], refs[-1]
    for which, factor in ((0, inv_root), (1, 1.0)):
        total = own_ref[which] * factor
        for ref in returned:
            total += ref[which].astype(jnp.float32)
        total_ref[which] = total


def sum_kernel(*refs):
    total_ref, returned = refs[0], refs[1:-5]
    key_hbm, value_hbm, key_ref, value_ref, sems = refs[-5:]
    key_total = total_ref[0]
    value_total = total_ref[1]
    for ref in returned:
        key_total += ref[0].astype(jnp.float32)
        value_total += ref[1].astype(jnp.float32)
    key_ref[...] = key_total.astype(jnp.bfloat16)
    value_ref[...] = value_total.astype(jnp.bfloat16)
    copies = [
        pltpu.make_async_copy(key_ref, key_hbm, sems.at[0]),
        pltpu.make_async_copy(value_ref, value_hbm, sems.at[1]),
    ]
    for copy in copies:
        copy.start()
    for copy in copies:
        copy.wait()


def on_device(queries, key_rows, value_rows, attn_out, grad_out, log_norms, pair_order):
    row_count, group_size, head_size = queries.shape
    inner_count = lax.axis_size("inner")
    outer_count = lax.axis_size("outer")
    assert inner_count & (inner_count - 1) == 0 and inner_count > 1
    sizes = (group_size, row_count, head_size)
    half = group_size * row_count
    away = list(range(inner_count - 1, 0, -1))

    def flat(array):
        return jnp.swapaxes(array, 0, 1).reshape(-1, head_size)

    def in_hbm(array):
        return pltpu.with_memory_space_constraint(array, pltpu.HBM)

    def to_segment(block, ahead):
        route = [(at, (at + ahead) % outer_count) for at in range(outer_count)]
        return lax.ppermute(block, "outer", route)

    def exchange(block, step):
        route = []
        for inner in range(inner_count):
            for outer in range(outer_count):
                peer = inner ^ peer_offset(step, outer, inner_count)
                route.append((inner * outer_count + outer, peer * outer_count + outer))
        return lax.ppermute(block, ("inner", "outer"), route)

    vmem = pl.BlockSpec(memory_space=pltpu.VMEM)
    hbm = pl.BlockSpec(memory_space=pltpu.HBM)
    roomy = pltpu.CompilerParams(vmem_limit_bytes=32 * 2**20)

    def shape(dims, dtype):
        return jax.ShapeDtypeStruct(dims, dtype)

    def cost(blocks, data=2**20):
        each = group_size * row_count * row_count
        return pl.CostEstimate(
            flops=10 * blocks * each * head_size, bytes_accessed=data, transcendentals=blocks * each
        )

    block_shape = shape((2, row_count, head_size), jnp.bfloat16)

    pair, packet = pl.pallas_call(
        functools.partial(load_kernel, sizes),
        out_shape=(
            block_shape,
            shape((packet_rows(sizes), head_size), jnp.bfloat16),
        ),
        in_specs=[hbm] * 6,
        out_specs=(vmem,) * 2,
        scratch_shapes=[pltpu.VMEM((STAT_ROWS, row_count), jnp.float32), pltpu.SemaphoreType.DMA((6,))],
        cost_estimate=cost(0),
        compiler_params=roomy,
    )(
        *(
            in_hbm(array)
            for array in (
                flat(queries), flat(grad_out), flat(attn_out), log_norms, flat(key_rows), flat(value_rows)
            )
        )
    )
    next_packet = to_segment(packet, -1)
    blocks = {0: pair}
    for step in away:
        blocks[step] = exchange(pair, step)

    def scores_shape(count):
        return shape((count * row_count, half), jnp.bfloat16)

    near_scores, near_next_scores, own_total, stats, rank = pl.pallas_call(
        functools.partial(near_kernel, sizes, inner_count, outer_count),
        out_shape=(
            scores_shape(1),
            scores_shape(1),
            shape((2, row_count, head_size), jnp.float32),
            shape((2, STAT_ROWS, row_count), jnp.float32),
            shape((max(8, inner_count), row_count), jnp.int32),
        ),
        in_specs=[vmem] * 2 + [hbm, vmem],
        out_specs=(vmem,) * 5,
        scratch_shapes=[pltpu.SMEM((inner_count,), jnp.int32), pltpu.SemaphoreType.DMA],
        cost_estimate=cost(2),
        compiler_params=roomy,
    )(packet, next_packet, in_hbm(pair_order), pair)

    scores, next_scores, sums = [near_scores], [near_next_scores], {}
    middle = inner_count // 2 - 1
    held = [0]
    for steps in (away[:middle][::-1], away[middle:][::-1]):
        if steps:
            far_scores, far_next_scores, *terms = pl.pallas_call(
                functools.partial(far_kernel, sizes, inner_count, steps),
                out_shape=(scores_shape(len(steps)),) * 2 + (block_shape,) * len(steps),
                in_specs=[vmem] * (4 + len(steps)),
                out_specs=(vmem,) * (2 + len(steps)),
                cost_estimate=cost(2 * len(steps)),
                compiler_params=roomy,
            )(packet, next_packet, rank, stats, *(blocks[step] for step in steps))
            scores.append(far_scores)
            next_scores.append(far_next_scores)
            sums.update(zip(steps, terms))
            held += steps
    all_blocks = [blocks[step] for step in held]
    groups = len(scores)
    returned = [exchange(sums[step], step) for step in away]

    query_next = pl.pallas_call(
        functools.partial(back_kernel, sizes, outer_count, groups),
        out_shape=shape((head_size, half), jnp.bfloat16),
        in_specs=[vmem] * (groups + inner_count),
        out_specs=vmem,
        cost_estimate=cost(inner_count),
        compiler_params=roomy,
    )(*next_scores, *all_blocks)
    query_back = to_segment(query_next, 1)

    early_total = pl.pallas_call(
        functools.partial(early_kernel, sizes),
        out_shape=shape((2, row_count, head_size), jnp.float32),
        in_specs=[vmem] * (1 + middle),
        out_specs=vmem,
        cost_estimate=cost(8 * inner_count),
        compiler_params=roomy,
    )(own_total, *returned[:middle])
    early_total, scores[0] = lax.optimization_barrier((early_total, scores[0]))

    query_out = pl.pallas_call(
        functools.partial(query_kernel, sizes, groups),
        out_shape=shape((half, head_size), jnp.bfloat16),
        in_specs=[vmem] * (1 + groups + inner_count),
        out_specs=hbm,
        scratch_shapes=[
            pltpu.VMEM((head_size, half), jnp.float32),
            pltpu.VMEM((half, head_size), jnp.bfloat16),
            pltpu.SemaphoreType.DMA,
        ],
        cost_estimate=cost(inner_count),
        compiler_params=roomy,
    )(query_back, *scores, *all_blocks)

    early_total, query_out = lax.optimization_barrier((early_total, query_out))
    key_out, value_out = pl.pallas_call(
        sum_kernel,
        out_shape=(shape((row_count, head_size), jnp.bfloat16),) * 2,
        in_specs=[vmem] * (1 + len(away) - middle),
        out_specs=(hbm, hbm),
        scratch_shapes=[
            pltpu.VMEM((row_count, head_size), jnp.bfloat16),
            pltpu.VMEM((row_count, head_size), jnp.bfloat16),
            pltpu.SemaphoreType.DMA((2,)),
        ],
        compiler_params=roomy,
    )(early_total, *returned[middle:])
    grad_queries = jnp.swapaxes(query_out.reshape(group_size, row_count, head_size), 0, 1)
    return (grad_queries, key_out[:, None, :], value_out[:, None, :])


def solution(mesh):
    in_specs = (
        P(("outer", "inner"), "head", None),
        P(("outer", "inner"), "head", None),
        P(("outer", "inner"), "head", None),
        P(("outer", "inner"), "head", None),
        P(("outer", "inner"), "head", None),
        P("head", ("outer", "inner")),
        P(),
    )
    out_specs = (
        P(("outer", "inner"), "head", None),
        P(("outer", "inner"), "head", None),
        P(("outer", "inner"), "head", None),
    )
    return jax.shard_map(
        on_device, mesh=mesh, in_specs=in_specs, out_specs=out_specs, check_vma=False
    )
```

```python
import functools
import math

import jax
import jax.numpy as jnp
from jax import lax
from jax.experimental import pallas as pl
from jax.experimental.pallas import tpu as pltpu
from jax.sharding import PartitionSpec as P

LOG2E = math.log2(math.e)
STAT_ROWS = 16
SPLIT = 3


def contract(lhs, rhs, lhs_dim, rhs_dim):
    return lax.dot_general(
        lhs, rhs, (((lhs_dim,), (rhs_dim,)), ((), ())), preferred_element_type=jnp.float32
    )


def packet_rows(sizes):
    group_size, row_count, _ = sizes
    return 3 * group_size * row_count + SPLIT * STAT_ROWS


def peer_offset(step, outer, inner_count):
    bits = inner_count.bit_length() - 1
    turn = outer % 2
    return ((step << turn) | (step >> (bits - turn))) & (inner_count - 1)


def load_kernel(
    sizes, query_hbm, grad_hbm, out_hbm, norm_hbm, key_hbm, value_hbm, pair_ref, packet_ref, norm_ref, sems
):
    group_size, row_count, _ = sizes
    half = group_size * row_count
    copies = [
        pltpu.make_async_copy(source, target, sems.at[at])
        for at, (source, target) in enumerate(
            [
                (norm_hbm, norm_ref.at[pl.ds(0, group_size)]),
                (key_hbm, pair_ref.at[0]),
                (value_hbm, pair_ref.at[1]),
                (query_hbm, packet_ref.at[pl.ds(0, half)]),
                (grad_hbm, packet_ref.at[pl.ds(half, half)]),
                (out_hbm, packet_ref.at[pl.ds(2 * half, half)]),
            ]
        )
    ]
    for copy in copies:
        copy.start()
    copies[0].wait()
    held = lax.broadcasted_iota(jnp.int32, (STAT_ROWS, row_count), 0) < group_size
    rest = jnp.where(held, jnp.clip(norm_ref[...], -3.38e38, 3.38e38), 0.0)
    for term in range(SPLIT):
        piece = rest.astype(jnp.bfloat16)
        start = 3 * half + term * STAT_ROWS
        packet_ref[start : start + STAT_ROWS, :] = piece
        rest = rest - piece.astype(jnp.float32)
    for copy in copies[1:]:
        copy.wait()


def row_stats(packet_ref, stat_ref, sizes):
    group_size, row_count, _ = sizes
    half = group_size * row_count
    start = 3 * half
    pieces = [
        packet_ref[start + term * STAT_ROWS : start + (term + 1) * STAT_ROWS, :].astype(jnp.float32)
        for term in range(SPLIT)
    ]
    stat_ref[...] = (pieces[0] + (pieces[1] + pieces[2])) * LOG2E
    for head in range(group_size):
        first = head * row_count
        grads = packet_ref[half + first : half + first + row_count, :].astype(jnp.float32)
        outs = packet_ref[2 * half + first : 2 * half + first + row_count, :].astype(jnp.float32)
        stat_ref[8 + head : 9 + head, :] = jnp.sum((grads * outs).T, axis=0, keepdims=True)


def block_terms(keys, values, parts, sizes):
    group_size, row_count, head_size = sizes
    half = group_size * row_count
    scale = LOG2E / math.sqrt(head_size)
    per_step = 2 if group_size % 2 == 0 else 1
    key_total = 0.0
    value_total = 0.0
    for packet_ref, stats, visible, scores_ref in parts:
        weights_parts = []
        score_parts = []
        for first in range(0, group_size, per_step):
            start, stop = first * row_count, (first + per_step) * row_count
            queries = packet_ref[start:stop, :]
            grads = packet_ref[half + start : half + stop, :]
            scores = contract(keys, queries, 1, 1)
            grad_weights = contract(values, grads, 1, 1)
            for at in range(per_step):
                head = first + at
                lanes = slice(at * row_count, (at + 1) * row_count)
                weights = jnp.exp2(scores[:, lanes] * scale - stats[head : head + 1, :])
                if visible is not None:
                    weights = jnp.where(visible, weights, 0.0)
                weights_parts.append(weights.astype(jnp.bfloat16))
                score_parts.append(
                    (weights * (grad_weights[:, lanes] - stats[8 + head : 9 + head, :])).astype(jnp.bfloat16)
                )
        grad_scores = jnp.concatenate(score_parts, axis=1)
        scores_ref[...] = grad_scores
        value_total += contract(jnp.concatenate(weights_parts, axis=1), packet_ref[half : 2 * half, :], 1, 0)
        key_total += contract(grad_scores, packet_ref[:half, :], 1, 0)
    return key_total, value_total


def visible_rows(rank_ref, steps, inner_count, row_count):
    span_rows = row_count // 2
    key_rows = lax.broadcasted_iota(jnp.int32, (row_count, row_count), 0)
    my_rows = lax.broadcasted_iota(jnp.int32, (row_count, row_count), 1)

    def positions(rank, rows):
        return jnp.where(
            rows < span_rows,
            rank * span_rows + rows,
            (2 * inner_count - 2 - rank) * span_rows + rows,
        )

    mine = positions(rank_ref[0:1, :], my_rows)
    return jnp.concatenate(
        [positions(rank_ref[step : step + 1, :], key_rows) <= mine for step in steps], axis=0
    )


def stacked(blocks, which):
    return jnp.concatenate([ref[which] for ref in blocks], axis=0)


def near_kernel(
    sizes, inner_count, outer_count, packet_ref, next_ref, order_hbm, pair_ref, scores_ref,
    next_scores_ref, total_ref, stat_ref, rank_ref, order_ref, sem,
):
    _, row_count, _ = sizes
    copy = pltpu.make_async_copy(order_hbm, order_ref, sem)
    copy.start()
    has_next = lax.axis_index("outer") < outer_count - 1
    row_stats(packet_ref, stat_ref.at[0], sizes)
    row_stats(next_ref, stat_ref.at[1], sizes)

    @pl.when(jnp.logical_not(has_next))
    def _():
        stat_ref[1, :8, :] = jnp.full((8, row_count), 1e30, jnp.float32)

    key_rows = lax.broadcasted_iota(jnp.int32, (row_count, row_count), 0)
    visible = key_rows <= lax.broadcasted_iota(jnp.int32, (row_count, row_count), 1)
    parts = ((packet_ref, stat_ref[0], visible, scores_ref), (next_ref, stat_ref[1], None, next_scores_ref))
    total_ref[0], total_ref[1] = block_terms(pair_ref[0], pair_ref[1], parts, sizes)
    copy.wait()
    my_index = lax.axis_index("inner")
    turned = lax.rem(lax.axis_index("outer"), 2) == 1
    for step in range(inner_count):
        offset = jnp.where(turned, peer_offset(step, 1, inner_count), peer_offset(step, 0, inner_count))
        rank_ref[step : step + 1, :] = jnp.full((1, row_count), order_ref[my_index ^ offset], jnp.int32)


def far_kernel(sizes, inner_count, steps, packet_ref, next_ref, rank_ref, stat_ref, *refs):
    count = len(steps)
    _, row_count, head_size = sizes
    inv_root = 1.0 / math.sqrt(head_size)
    blocks, (scores_ref, next_scores_ref), sums = refs[:count], refs[count : count + 2], refs[count + 2 :]
    visible = visible_rows(rank_ref, steps, inner_count, row_count)
    parts = ((packet_ref, stat_ref[0], visible, scores_ref), (next_ref, stat_ref[1], None, next_scores_ref))
    key_total, value_total = block_terms(stacked(blocks, 0), stacked(blocks, 1), parts, sizes)
    for at, ref in enumerate(sums):
        rows = slice(at * row_count, (at + 1) * row_count)
        ref[0] = (key_total[rows] * inv_root).astype(jnp.bfloat16)
        ref[1] = value_total[rows].astype(jnp.bfloat16)


def query_terms(refs, groups, lanes):
    scores = jnp.concatenate([ref[:, lanes] for ref in refs[:groups]], axis=0)
    return contract(stacked(refs[groups:], 0), scores, 0, 0)


def store_queries(result_ref, refs, groups, sizes):
    group_size, row_count, _ = sizes
    terms = query_terms(refs, groups, slice(None))
    for head in range(group_size):
        rows = slice(head * row_count, (head + 1) * row_count)
        result_ref[rows, :] = terms[:, rows].T.astype(result_ref.dtype)


def back_kernel(sizes, outer_count, groups, *refs):
    has_next = lax.axis_index("outer") < outer_count - 1

    @pl.when(has_next)
    def _():
        store_queries(refs[-1], refs[:-1], groups, sizes)


def query_kernel(sizes, groups, *refs):
    store_queries(refs[-1], refs[:-1], groups, sizes)


def early_kernel(sizes, *refs):
    inv_root = 1.0 / math.sqrt(sizes[2])
    own_ref, returned, total_ref = refs[0], refs[1:-1], refs[-1]
    for which, factor in ((0, inv_root), (1, 1.0)):
        total = own_ref[which] * factor
        for ref in returned:
            total += ref[which].astype(jnp.float32)
        total_ref[which] = total


def late_kernel(*refs):
    total_ref, returned, sum_ref = refs[0], refs[1:-1], refs[-1]
    for which in range(2):
        total = total_ref[which]
        for ref in returned:
            total += ref[which].astype(jnp.float32)
        sum_ref[which] = total.astype(jnp.bfloat16)


def final_kernel(
    sizes, sum_ref, query_ref, back_ref, query_hbm, key_hbm, value_hbm, result_ref, sems
):
    inv_root = 1.0 / math.sqrt(sizes[2])
    copies = [
        pltpu.make_async_copy(sum_ref.at[0], key_hbm, sems.at[0]),
        pltpu.make_async_copy(sum_ref.at[1], value_hbm, sems.at[1]),
        pltpu.make_async_copy(result_ref, query_hbm, sems.at[2]),
    ]
    copies[0].start()
    copies[1].start()
    has_prev = lax.axis_index("outer") > 0
    back = jnp.where(has_prev, back_ref[...].astype(jnp.float32), 0.0)
    result_ref[...] = ((query_ref[...] + back) * inv_root).astype(jnp.bfloat16)
    copies[2].start()
    for copy in copies:
        copy.wait()


def on_device(queries, key_rows, value_rows, attn_out, grad_out, log_norms, pair_order):
    row_count, group_size, head_size = queries.shape
    inner_count = lax.axis_size("inner")
    outer_count = lax.axis_size("outer")
    assert inner_count & (inner_count - 1) == 0 and inner_count > 1
    sizes = (group_size, row_count, head_size)
    half = group_size * row_count
    away = list(range(inner_count - 1, 0, -1))

    def flat(array):
        return jnp.swapaxes(array, 0, 1).reshape(-1, head_size)

    def in_hbm(array):
        return pltpu.with_memory_space_constraint(array, pltpu.HBM)

    def to_segment(block, ahead):
        route = [(at, (at + ahead) % outer_count) for at in range(outer_count)]
        return lax.ppermute(block, "outer", route)

    def exchange(block, step):
        route = []
        for inner in range(inner_count):
            for outer in range(outer_count):
                peer = inner ^ peer_offset(step, outer, inner_count)
                route.append((inner * outer_count + outer, peer * outer_count + outer))
        return lax.ppermute(block, ("inner", "outer"), route)

    vmem = pl.BlockSpec(memory_space=pltpu.VMEM)
    hbm = pl.BlockSpec(memory_space=pltpu.HBM)
    roomy = pltpu.CompilerParams(vmem_limit_bytes=32 * 2**20)

    def shape(dims, dtype):
        return jax.ShapeDtypeStruct(dims, dtype)

    def cost(blocks, data=2**20):
        each = group_size * row_count * row_count
        return pl.CostEstimate(
            flops=10 * blocks * each * head_size, bytes_accessed=data, transcendentals=blocks * each
        )

    block_shape = shape((2, row_count, head_size), jnp.bfloat16)

    pair, packet = pl.pallas_call(
        functools.partial(load_kernel, sizes),
        out_shape=(
            block_shape,
            shape((packet_rows(sizes), head_size), jnp.bfloat16),
        ),
        in_specs=[hbm] * 6,
        out_specs=(vmem,) * 2,
        scratch_shapes=[pltpu.VMEM((STAT_ROWS, row_count), jnp.float32), pltpu.SemaphoreType.DMA((6,))],
        cost_estimate=cost(0),
        compiler_params=roomy,
    )(
        *(
            in_hbm(array)
            for array in (
                flat(queries), flat(grad_out), flat(attn_out), log_norms, flat(key_rows), flat(value_rows)
            )
        )
    )
    next_packet = to_segment(packet, -1)
    blocks = {0: pair}
    for step in away:
        blocks[step] = exchange(pair, step)

    def scores_shape(count):
        return shape((count * row_count, half), jnp.bfloat16)

    near_scores, near_next_scores, own_total, stats, rank = pl.pallas_call(
        functools.partial(near_kernel, sizes, inner_count, outer_count),
        out_shape=(
            scores_shape(1),
            scores_shape(1),
            shape((2, row_count, head_size), jnp.float32),
            shape((2, STAT_ROWS, row_count), jnp.float32),
            shape((max(8, inner_count), row_count), jnp.int32),
        ),
        in_specs=[vmem] * 2 + [hbm, vmem],
        out_specs=(vmem,) * 5,
        scratch_shapes=[pltpu.SMEM((inner_count,), jnp.int32), pltpu.SemaphoreType.DMA],
        cost_estimate=cost(2),
        compiler_params=roomy,
    )(packet, next_packet, in_hbm(pair_order), pair)

    scores, next_scores, sums = [near_scores], [near_next_scores], {}
    middle = inner_count // 2 - 1
    held = [0]
    for steps in (away[:middle][::-1], away[middle:][::-1]):
        if steps:
            far_scores, far_next_scores, *terms = pl.pallas_call(
                functools.partial(far_kernel, sizes, inner_count, steps),
                out_shape=(scores_shape(len(steps)),) * 2 + (block_shape,) * len(steps),
                in_specs=[vmem] * (4 + len(steps)),
                out_specs=(vmem,) * (2 + len(steps)),
                cost_estimate=cost(2 * len(steps)),
                compiler_params=roomy,
            )(packet, next_packet, rank, stats, *(blocks[step] for step in steps))
            scores.append(far_scores)
            next_scores.append(far_next_scores)
            sums.update(zip(steps, terms))
            held += steps
    all_blocks = [blocks[step] for step in held]
    groups = len(scores)
    returned = [exchange(sums[step], step) for step in away]

    early_total = pl.pallas_call(
        functools.partial(early_kernel, sizes),
        out_shape=shape((2, row_count, head_size), jnp.float32),
        in_specs=[vmem] * (1 + middle),
        out_specs=vmem,
        cost_estimate=cost(8 * inner_count),
        compiler_params=roomy,
    )(own_total, *returned[:middle])
    early_total, next_scores[0] = lax.optimization_barrier((early_total, next_scores[0]))

    query_next = pl.pallas_call(
        functools.partial(back_kernel, sizes, outer_count, groups),
        out_shape=shape((half, head_size), jnp.bfloat16),
        in_specs=[vmem] * (groups + inner_count),
        out_specs=vmem,
        cost_estimate=cost(0, 0),
        compiler_params=roomy,
    )(*next_scores, *all_blocks)
    query_back = to_segment(query_next, 1)

    query_own = pl.pallas_call(
        functools.partial(query_kernel, sizes, groups),
        out_shape=shape((half, head_size), jnp.float32),
        in_specs=[vmem] * (groups + inner_count),
        out_specs=vmem,
        cost_estimate=cost(0, 0),
        compiler_params=roomy,
    )(*scores, *all_blocks)

    late_sum = pl.pallas_call(
        late_kernel,
        out_shape=block_shape,
        in_specs=[vmem] * (1 + len(away) - middle),
        out_specs=vmem,
        cost_estimate=cost(8 * inner_count),
        compiler_params=roomy,
    )(early_total, *returned[middle:])

    query_out, key_out, value_out = pl.pallas_call(
        functools.partial(final_kernel, sizes),
        out_shape=(
            shape((half, head_size), jnp.bfloat16),
            shape((row_count, head_size), jnp.bfloat16),
            shape((row_count, head_size), jnp.bfloat16),
        ),
        in_specs=[vmem] * 3,
        out_specs=(hbm,) * 3,
        scratch_shapes=[pltpu.VMEM((half, head_size), jnp.bfloat16), pltpu.SemaphoreType.DMA((3,))],
        compiler_params=roomy,
    )(late_sum, query_own, query_back)
    grad_queries = jnp.swapaxes(query_out.reshape(group_size, row_count, head_size), 0, 1)
    return (grad_queries, key_out[:, None, :], value_out[:, None, :])


def solution(mesh):
    in_specs = (
        P(("outer", "inner"), "head", None),
        P(("outer", "inner"), "head", None),
        P(("outer", "inner"), "head", None),
        P(("outer", "inner"), "head", None),
        P(("outer", "inner"), "head", None),
        P("head", ("outer", "inner")),
        P(),
    )
    out_specs = (
        P(("outer", "inner"), "head", None),
        P(("outer", "inner"), "head", None),
        P(("outer", "inner"), "head", None),
    )
    return jax.shard_map(
        on_device, mesh=mesh, in_specs=in_specs, out_specs=out_specs, check_vma=False
    )
```

```python
import functools
import math

import jax
import jax.numpy as jnp
from jax import lax
from jax.experimental import pallas as pl
from jax.experimental.pallas import tpu as pltpu
from jax.sharding import PartitionSpec as P

LOG2E = math.log2(math.e)
STAT_ROWS = 16
SPLIT = 3


def contract(lhs, rhs, lhs_dim, rhs_dim):
    return lax.dot_general(
        lhs, rhs, (((lhs_dim,), (rhs_dim,)), ((), ())), preferred_element_type=jnp.float32
    )


def packet_rows(sizes):
    group_size, row_count, _ = sizes
    return 3 * group_size * row_count + SPLIT * STAT_ROWS


def peer_offset(step, outer, inner_count):
    if step == 0 or outer % 2 == 0:
        return step
    order = [inner_count - 1] + list(range(1, inner_count - 1))
    return order[order.index(step) - 1]


def load_kernel(
    sizes, query_hbm, grad_hbm, out_hbm, norm_hbm, key_hbm, value_hbm, pair_ref, packet_ref, norm_ref, sems
):
    group_size, row_count, _ = sizes
    half = group_size * row_count
    copies = [
        pltpu.make_async_copy(source, target, sems.at[at])
        for at, (source, target) in enumerate(
            [
                (norm_hbm, norm_ref.at[pl.ds(0, group_size)]),
                (key_hbm, pair_ref.at[0]),
                (value_hbm, pair_ref.at[1]),
                (query_hbm, packet_ref.at[pl.ds(0, half)]),
                (grad_hbm, packet_ref.at[pl.ds(half, half)]),
                (out_hbm, packet_ref.at[pl.ds(2 * half, half)]),
            ]
        )
    ]
    for copy in copies:
        copy.start()
    copies[0].wait()
    held = lax.broadcasted_iota(jnp.int32, (STAT_ROWS, row_count), 0) < group_size
    rest = jnp.where(held, jnp.clip(norm_ref[...], -3.38e38, 3.38e38), 0.0)
    for term in range(SPLIT):
        piece = rest.astype(jnp.bfloat16)
        start = 3 * half + term * STAT_ROWS
        packet_ref[start : start + STAT_ROWS, :] = piece
        rest = rest - piece.astype(jnp.float32)
    for copy in copies[1:]:
        copy.wait()


def row_stats(packet_ref, stat_ref, sizes):
    group_size, row_count, _ = sizes
    half = group_size * row_count
    start = 3 * half
    pieces = [
        packet_ref[start + term * STAT_ROWS : start + (term + 1) * STAT_ROWS, :].astype(jnp.float32)
        for term in range(SPLIT)
    ]
    stat_ref[...] = (pieces[0] + (pieces[1] + pieces[2])) * LOG2E
    for head in range(group_size):
        first = head * row_count
        grads = packet_ref[half + first : half + first + row_count, :].astype(jnp.float32)
        outs = packet_ref[2 * half + first : 2 * half + first + row_count, :].astype(jnp.float32)
        stat_ref[8 + head : 9 + head, :] = jnp.sum((grads * outs).T, axis=0, keepdims=True)


def block_terms(keys, values, parts, sizes):
    group_size, row_count, head_size = sizes
    half = group_size * row_count
    scale = LOG2E / math.sqrt(head_size)
    per_step = 2 if group_size % 2 == 0 else 1
    key_total = 0.0
    value_total = 0.0
    for packet_ref, stats, visible, scores_ref in parts:
        weights_parts = []
        score_parts = []
        for first in range(0, group_size, per_step):
            start, stop = first * row_count, (first + per_step) * row_count
            queries = packet_ref[start:stop, :]
            grads = packet_ref[half + start : half + stop, :]
            scores = contract(keys, queries, 1, 1)
            grad_weights = contract(values, grads, 1, 1)
            for at in range(per_step):
                head = first + at
                lanes = slice(at * row_count, (at + 1) * row_count)
                weights = jnp.exp2(scores[:, lanes] * scale - stats[head : head + 1, :])
                if visible is not None:
                    weights = jnp.where(visible, weights, 0.0)
                weights_parts.append(weights.astype(jnp.bfloat16))
                score_parts.append(
                    (weights * (grad_weights[:, lanes] - stats[8 + head : 9 + head, :])).astype(jnp.bfloat16)
                )
        grad_scores = jnp.concatenate(score_parts, axis=1)
        scores_ref[...] = grad_scores
        value_total += contract(jnp.concatenate(weights_parts, axis=1), packet_ref[half : 2 * half, :], 1, 0)
        key_total += contract(grad_scores, packet_ref[:half, :], 1, 0)
    return key_total, value_total


def visible_rows(rank_ref, steps, inner_count, row_count):
    span_rows = row_count // 2
    key_rows = lax.broadcasted_iota(jnp.int32, (row_count, row_count), 0)
    my_rows = lax.broadcasted_iota(jnp.int32, (row_count, row_count), 1)

    def positions(rank, rows):
        return jnp.where(
            rows < span_rows,
            rank * span_rows + rows,
            (2 * inner_count - 2 - rank) * span_rows + rows,
        )

    mine = positions(rank_ref[0:1, :], my_rows)
    return jnp.concatenate(
        [positions(rank_ref[step : step + 1, :], key_rows) <= mine for step in steps], axis=0
    )


def stacked(blocks, which):
    return jnp.concatenate([ref[which] for ref in blocks], axis=0)


def near_kernel(
    sizes, inner_count, outer_count, packet_ref, next_ref, order_hbm, pair_ref, scores_ref,
    next_scores_ref, total_ref, stat_ref, rank_ref, order_ref, sem,
):
    _, row_count, _ = sizes
    copy = pltpu.make_async_copy(order_hbm, order_ref, sem)
    copy.start()
    has_next = lax.axis_index("outer") < outer_count - 1
    row_stats(packet_ref, stat_ref.at[0], sizes)
    row_stats(next_ref, stat_ref.at[1], sizes)

    @pl.when(jnp.logical_not(has_next))
    def _():
        stat_ref[1, :8, :] = jnp.full((8, row_count), 1e30, jnp.float32)

    key_rows = lax.broadcasted_iota(jnp.int32, (row_count, row_count), 0)
    visible = key_rows <= lax.broadcasted_iota(jnp.int32, (row_count, row_count), 1)
    parts = ((packet_ref, stat_ref[0], visible, scores_ref), (next_ref, stat_ref[1], None, next_scores_ref))
    total_ref[0], total_ref[1] = block_terms(pair_ref[0], pair_ref[1], parts, sizes)
    copy.wait()
    my_index = lax.axis_index("inner")
    turned = lax.rem(lax.axis_index("outer"), 2) == 1
    for step in range(inner_count):
        offset = jnp.where(turned, peer_offset(step, 1, inner_count), peer_offset(step, 0, inner_count))
        rank_ref[step : step + 1, :] = jnp.full((1, row_count), order_ref[my_index ^ offset], jnp.int32)


def far_kernel(sizes, inner_count, steps, packet_ref, next_ref, rank_ref, stat_ref, *refs):
    count = len(steps)
    _, row_count, head_size = sizes
    inv_root = 1.0 / math.sqrt(head_size)
    blocks, (scores_ref, next_scores_ref), sums = refs[:count], refs[count : count + 2], refs[count + 2 :]
    visible = visible_rows(rank_ref, steps, inner_count, row_count)
    parts = ((packet_ref, stat_ref[0], visible, scores_ref), (next_ref, stat_ref[1], None, next_scores_ref))
    key_total, value_total = block_terms(stacked(blocks, 0), stacked(blocks, 1), parts, sizes)
    for at, ref in enumerate(sums):
        rows = slice(at * row_count, (at + 1) * row_count)
        ref[0] = (key_total[rows] * inv_root).astype(jnp.bfloat16)
        ref[1] = value_total[rows].astype(jnp.bfloat16)


def query_terms(refs, groups, lanes):
    scores = jnp.concatenate([ref[:, lanes] for ref in refs[:groups]], axis=0)
    return contract(stacked(refs[groups:], 0), scores, 0, 0)


def store_queries(result_ref, refs, groups, sizes):
    group_size, row_count, _ = sizes
    terms = query_terms(refs, groups, slice(None))
    for head in range(group_size):
        rows = slice(head * row_count, (head + 1) * row_count)
        result_ref[rows, :] = terms[:, rows].T.astype(result_ref.dtype)


def back_kernel(sizes, outer_count, groups, *refs):
    has_next = lax.axis_index("outer") < outer_count - 1

    @pl.when(has_next)
    def _():
        store_queries(refs[-1], refs[:-1], groups, sizes)


def query_kernel(sizes, groups, *refs):
    store_queries(refs[-1], refs[:-1], groups, sizes)


def early_kernel(sizes, *refs):
    inv_root = 1.0 / math.sqrt(sizes[2])
    own_ref, returned, total_ref = refs[0], refs[1:-1], refs[-1]
    for which, factor in ((0, inv_root), (1, 1.0)):
        total = own_ref[which] * factor
        for ref in returned:
            total += ref[which].astype(jnp.float32)
        total_ref[which] = total


def late_kernel(*refs):
    total_ref, returned, sum_ref = refs[0], refs[1:-1], refs[-1]
    for which in range(2):
        total = total_ref[which]
        for ref in returned:
            total += ref[which].astype(jnp.float32)
        sum_ref[which] = total.astype(jnp.bfloat16)


def final_kernel(
    sizes, sum_ref, query_ref, back_ref, query_hbm, key_hbm, value_hbm, result_ref, sems
):
    inv_root = 1.0 / math.sqrt(sizes[2])
    copies = [
        pltpu.make_async_copy(sum_ref.at[0], key_hbm, sems.at[0]),
        pltpu.make_async_copy(sum_ref.at[1], value_hbm, sems.at[1]),
        pltpu.make_async_copy(result_ref, query_hbm, sems.at[2]),
    ]
    copies[0].start()
    copies[1].start()
    has_prev = lax.axis_index("outer") > 0
    back = jnp.where(has_prev, back_ref[...].astype(jnp.float32), 0.0)
    result_ref[...] = ((query_ref[...] + back) * inv_root).astype(jnp.bfloat16)
    copies[2].start()
    for copy in copies:
        copy.wait()


def on_device(queries, key_rows, value_rows, attn_out, grad_out, log_norms, pair_order):
    row_count, group_size, head_size = queries.shape
    inner_count = lax.axis_size("inner")
    outer_count = lax.axis_size("outer")
    assert inner_count & (inner_count - 1) == 0 and inner_count > 1
    sizes = (group_size, row_count, head_size)
    half = group_size * row_count
    away = list(range(inner_count - 1, 0, -1))

    def flat(array):
        return jnp.swapaxes(array, 0, 1).reshape(-1, head_size)

    def in_hbm(array):
        return pltpu.with_memory_space_constraint(array, pltpu.HBM)

    def to_segment(block, ahead):
        route = [(at, (at + ahead) % outer_count) for at in range(outer_count)]
        return lax.ppermute(block, "outer", route)

    def exchange(block, step):
        route = []
        for inner in range(inner_count):
            for outer in range(outer_count):
                peer = inner ^ peer_offset(step, outer, inner_count)
                route.append((inner * outer_count + outer, peer * outer_count + outer))
        return lax.ppermute(block, ("inner", "outer"), route)

    vmem = pl.BlockSpec(memory_space=pltpu.VMEM)
    hbm = pl.BlockSpec(memory_space=pltpu.HBM)
    roomy = pltpu.CompilerParams(vmem_limit_bytes=32 * 2**20)

    def shape(dims, dtype):
        return jax.ShapeDtypeStruct(dims, dtype)

    def cost(blocks, data=2**20):
        each = group_size * row_count * row_count
        return pl.CostEstimate(
            flops=10 * blocks * each * head_size, bytes_accessed=data, transcendentals=blocks * each
        )

    block_shape = shape((2, row_count, head_size), jnp.bfloat16)

    pair, packet = pl.pallas_call(
        functools.partial(load_kernel, sizes),
        out_shape=(
            block_shape,
            shape((packet_rows(sizes), head_size), jnp.bfloat16),
        ),
        in_specs=[hbm] * 6,
        out_specs=(vmem,) * 2,
        scratch_shapes=[pltpu.VMEM((STAT_ROWS, row_count), jnp.float32), pltpu.SemaphoreType.DMA((6,))],
        cost_estimate=cost(0),
        compiler_params=roomy,
    )(
        *(
            in_hbm(array)
            for array in (
                flat(queries), flat(grad_out), flat(attn_out), log_norms, flat(key_rows), flat(value_rows)
            )
        )
    )
    next_packet = to_segment(packet, -1)
    blocks = {0: pair}
    for step in away:
        blocks[step] = exchange(pair, step)

    def scores_shape(count):
        return shape((count * row_count, half), jnp.bfloat16)

    near_scores, near_next_scores, own_total, stats, rank = pl.pallas_call(
        functools.partial(near_kernel, sizes, inner_count, outer_count),
        out_shape=(
            scores_shape(1),
            scores_shape(1),
            shape((2, row_count, head_size), jnp.float32),
            shape((2, STAT_ROWS, row_count), jnp.float32),
            shape((max(8, inner_count), row_count), jnp.int32),
        ),
        in_specs=[vmem] * 2 + [hbm, vmem],
        out_specs=(vmem,) * 5,
        scratch_shapes=[pltpu.SMEM((inner_count,), jnp.int32), pltpu.SemaphoreType.DMA],
        cost_estimate=cost(2),
        compiler_params=roomy,
    )(packet, next_packet, in_hbm(pair_order), pair)

    scores, next_scores, sums = [near_scores], [near_next_scores], {}
    middle = inner_count // 2 - 1
    held = [0]
    for steps in (away[:middle][::-1], away[middle:][::-1]):
        if steps:
            far_scores, far_next_scores, *terms = pl.pallas_call(
                functools.partial(far_kernel, sizes, inner_count, steps),
                out_shape=(scores_shape(len(steps)),) * 2 + (block_shape,) * len(steps),
                in_specs=[vmem] * (4 + len(steps)),
                out_specs=(vmem,) * (2 + len(steps)),
                cost_estimate=cost(2 * len(steps)),
                compiler_params=roomy,
            )(packet, next_packet, rank, stats, *(blocks[step] for step in steps))
            scores.append(far_scores)
            next_scores.append(far_next_scores)
            sums.update(zip(steps, terms))
            held += steps
    all_blocks = [blocks[step] for step in held]
    groups = len(scores)
    returned = [exchange(sums[step], step) for step in away]

    early_total = pl.pallas_call(
        functools.partial(early_kernel, sizes),
        out_shape=shape((2, row_count, head_size), jnp.float32),
        in_specs=[vmem] * (1 + middle),
        out_specs=vmem,
        cost_estimate=cost(8 * inner_count),
        compiler_params=roomy,
    )(own_total, *returned[:middle])
    early_total, next_scores[0] = lax.optimization_barrier((early_total, next_scores[0]))

    query_next = pl.pallas_call(
        functools.partial(back_kernel, sizes, outer_count, groups),
        out_shape=shape((half, head_size), jnp.bfloat16),
        in_specs=[vmem] * (groups + inner_count),
        out_specs=vmem,
        cost_estimate=cost(0, 0),
        compiler_params=roomy,
    )(*next_scores, *all_blocks)
    query_back = to_segment(query_next, 1)

    query_own = pl.pallas_call(
        functools.partial(query_kernel, sizes, groups),
        out_shape=shape((half, head_size), jnp.float32),
        in_specs=[vmem] * (groups + inner_count),
        out_specs=vmem,
        cost_estimate=cost(0, 0),
        compiler_params=roomy,
    )(*scores, *all_blocks)

    late_sum = pl.pallas_call(
        late_kernel,
        out_shape=block_shape,
        in_specs=[vmem] * (1 + len(away) - middle),
        out_specs=vmem,
        cost_estimate=cost(8 * inner_count),
        compiler_params=roomy,
    )(early_total, *returned[middle:])

    query_out, key_out, value_out = pl.pallas_call(
        functools.partial(final_kernel, sizes),
        out_shape=(
            shape((half, head_size), jnp.bfloat16),
            shape((row_count, head_size), jnp.bfloat16),
            shape((row_count, head_size), jnp.bfloat16),
        ),
        in_specs=[vmem] * 3,
        out_specs=(hbm,) * 3,
        scratch_shapes=[pltpu.VMEM((half, head_size), jnp.bfloat16), pltpu.SemaphoreType.DMA((3,))],
        compiler_params=roomy,
    )(late_sum, query_own, query_back)
    grad_queries = jnp.swapaxes(query_out.reshape(group_size, row_count, head_size), 0, 1)
    return (grad_queries, key_out[:, None, :], value_out[:, None, :])


def solution(mesh):
    in_specs = (
        P(("outer", "inner"), "head", None),
        P(("outer", "inner"), "head", None),
        P(("outer", "inner"), "head", None),
        P(("outer", "inner"), "head", None),
        P(("outer", "inner"), "head", None),
        P("head", ("outer", "inner")),
        P(),
    )
    out_specs = (
        P(("outer", "inner"), "head", None),
        P(("outer", "inner"), "head", None),
        P(("outer", "inner"), "head", None),
    )
    return jax.shard_map(
        on_device, mesh=mesh, in_specs=in_specs, out_specs=out_specs, check_vma=False
    )
```

```python
import functools
import math

import jax
import jax.numpy as jnp
from jax import lax
from jax.experimental import pallas as pl
from jax.experimental.pallas import tpu as pltpu
from jax.sharding import PartitionSpec as P

LOG2E = math.log2(math.e)
STAT_ROWS = 16
SPLIT = 3


def contract(lhs, rhs, lhs_dim, rhs_dim):
    return lax.dot_general(
        lhs, rhs, (((lhs_dim,), (rhs_dim,)), ((), ())), preferred_element_type=jnp.float32
    )


def packet_rows(sizes):
    group_size, row_count, _ = sizes
    return 3 * group_size * row_count + SPLIT * STAT_ROWS


def peer_offset(step, outer, inner_count):
    last = inner_count - 1
    if outer % 2 == 1:
        return {0: 0, 1: last}.get(step, step - 1)
    return {0: 0, 1: last - 1, 2: last}.get(step, step - 2) if last > 1 else step


def load_kernel(
    sizes, query_hbm, grad_hbm, out_hbm, norm_hbm, key_hbm, value_hbm, pair_ref, packet_ref, norm_ref, sems
):
    group_size, row_count, _ = sizes
    half = group_size * row_count
    copies = [
        pltpu.make_async_copy(source, target, sems.at[at])
        for at, (source, target) in enumerate(
            [
                (norm_hbm, norm_ref.at[pl.ds(0, group_size)]),
                (key_hbm, pair_ref.at[0]),
                (value_hbm, pair_ref.at[1]),
                (query_hbm, packet_ref.at[pl.ds(0, half)]),
                (grad_hbm, packet_ref.at[pl.ds(half, half)]),
                (out_hbm, packet_ref.at[pl.ds(2 * half, half)]),
            ]
        )
    ]
    for copy in copies:
        copy.start()
    copies[0].wait()
    held = lax.broadcasted_iota(jnp.int32, (STAT_ROWS, row_count), 0) < group_size
    rest = jnp.where(held, jnp.clip(norm_ref[...], -3.38e38, 3.38e38), 0.0)
    for term in range(SPLIT):
        piece = rest.astype(jnp.bfloat16)
        start = 3 * half + term * STAT_ROWS
        packet_ref[start : start + STAT_ROWS, :] = piece
        rest = rest - piece.astype(jnp.float32)
    for copy in copies[1:]:
        copy.wait()


def row_stats(packet_ref, stat_ref, sizes):
    group_size, row_count, _ = sizes
    half = group_size * row_count
    start = 3 * half
    pieces = [
        packet_ref[start + term * STAT_ROWS : start + (term + 1) * STAT_ROWS, :].astype(jnp.float32)
        for term in range(SPLIT)
    ]
    stat_ref[...] = (pieces[0] + (pieces[1] + pieces[2])) * LOG2E
    for head in range(group_size):
        first = head * row_count
        grads = packet_ref[half + first : half + first + row_count, :].astype(jnp.float32)
        outs = packet_ref[2 * half + first : 2 * half + first + row_count, :].astype(jnp.float32)
        stat_ref[8 + head : 9 + head, :] = jnp.sum((grads * outs).T, axis=0, keepdims=True)


def block_terms(keys, values, parts, sizes):
    group_size, row_count, head_size = sizes
    half = group_size * row_count
    scale = LOG2E / math.sqrt(head_size)
    per_step = 2 if group_size % 2 == 0 else 1
    key_total = 0.0
    value_total = 0.0
    for packet_ref, stats, visible, scores_ref in parts:
        weights_parts = []
        score_parts = []
        for first in range(0, group_size, per_step):
            start, stop = first * row_count, (first + per_step) * row_count
            queries = packet_ref[start:stop, :]
            grads = packet_ref[half + start : half + stop, :]
            scores = contract(keys, queries, 1, 1)
            grad_weights = contract(values, grads, 1, 1)
            for at in range(per_step):
                head = first + at
                lanes = slice(at * row_count, (at + 1) * row_count)
                weights = jnp.exp2(scores[:, lanes] * scale - stats[head : head + 1, :])
                if visible is not None:
                    weights = jnp.where(visible, weights, 0.0)
                weights_parts.append(weights.astype(jnp.bfloat16))
                score_parts.append(
                    (weights * (grad_weights[:, lanes] - stats[8 + head : 9 + head, :])).astype(jnp.bfloat16)
                )
        grad_scores = jnp.concatenate(score_parts, axis=1)
        scores_ref[...] = grad_scores
        value_total += contract(jnp.concatenate(weights_parts, axis=1), packet_ref[half : 2 * half, :], 1, 0)
        key_total += contract(grad_scores, packet_ref[:half, :], 1, 0)
    return key_total, value_total


def visible_rows(rank_ref, steps, inner_count, row_count):
    span_rows = row_count // 2
    key_rows = lax.broadcasted_iota(jnp.int32, (row_count, row_count), 0)
    my_rows = lax.broadcasted_iota(jnp.int32, (row_count, row_count), 1)

    def positions(rank, rows):
        return jnp.where(
            rows < span_rows,
            rank * span_rows + rows,
            (2 * inner_count - 2 - rank) * span_rows + rows,
        )

    mine = positions(rank_ref[0:1, :], my_rows)
    return jnp.concatenate(
        [positions(rank_ref[step : step + 1, :], key_rows) <= mine for step in steps], axis=0
    )


def stacked(blocks, which):
    return jnp.concatenate([ref[which] for ref in blocks], axis=0)


def near_kernel(
    sizes, inner_count, outer_count, packet_ref, next_ref, order_hbm, pair_ref, scores_ref,
    next_scores_ref, total_ref, stat_ref, rank_ref, order_ref, sem,
):
    _, row_count, _ = sizes
    copy = pltpu.make_async_copy(order_hbm, order_ref, sem)
    copy.start()
    has_next = lax.axis_index("outer") < outer_count - 1
    row_stats(packet_ref, stat_ref.at[0], sizes)
    row_stats(next_ref, stat_ref.at[1], sizes)

    @pl.when(jnp.logical_not(has_next))
    def _():
        stat_ref[1, :8, :] = jnp.full((8, row_count), 1e30, jnp.float32)

    key_rows = lax.broadcasted_iota(jnp.int32, (row_count, row_count), 0)
    visible = key_rows <= lax.broadcasted_iota(jnp.int32, (row_count, row_count), 1)
    parts = ((packet_ref, stat_ref[0], visible, scores_ref), (next_ref, stat_ref[1], None, next_scores_ref))
    total_ref[0], total_ref[1] = block_terms(pair_ref[0], pair_ref[1], parts, sizes)
    copy.wait()
    my_index = lax.axis_index("inner")
    turned = lax.rem(lax.axis_index("outer"), 2) == 1
    for step in range(inner_count):
        offset = jnp.where(turned, peer_offset(step, 1, inner_count), peer_offset(step, 0, inner_count))
        rank_ref[step : step + 1, :] = jnp.full((1, row_count), order_ref[my_index ^ offset], jnp.int32)


def far_kernel(sizes, inner_count, steps, packet_ref, next_ref, rank_ref, stat_ref, *refs):
    count = len(steps)
    _, row_count, head_size = sizes
    inv_root = 1.0 / math.sqrt(head_size)
    blocks, (scores_ref, next_scores_ref), sums = refs[:count], refs[count : count + 2], refs[count + 2 :]
    visible = visible_rows(rank_ref, steps, inner_count, row_count)
    parts = ((packet_ref, stat_ref[0], visible, scores_ref), (next_ref, stat_ref[1], None, next_scores_ref))
    key_total, value_total = block_terms(stacked(blocks, 0), stacked(blocks, 1), parts, sizes)
    for at, ref in enumerate(sums):
        rows = slice(at * row_count, (at + 1) * row_count)
        ref[0] = (key_total[rows] * inv_root).astype(jnp.bfloat16)
        ref[1] = value_total[rows].astype(jnp.bfloat16)


def query_terms(refs, groups, lanes):
    scores = jnp.concatenate([ref[:, lanes] for ref in refs[:groups]], axis=0)
    return contract(stacked(refs[groups:], 0), scores, 0, 0)


def store_queries(result_ref, refs, groups, sizes):
    group_size, row_count, _ = sizes
    terms = query_terms(refs, groups, slice(None))
    for head in range(group_size):
        rows = slice(head * row_count, (head + 1) * row_count)
        result_ref[rows, :] = terms[:, rows].T.astype(result_ref.dtype)


def back_kernel(sizes, outer_count, groups, *refs):
    has_next = lax.axis_index("outer") < outer_count - 1

    @pl.when(has_next)
    def _():
        store_queries(refs[-1], refs[:-1], groups, sizes)


def query_kernel(sizes, groups, *refs):
    store_queries(refs[-1], refs[:-1], groups, sizes)


def early_kernel(sizes, *refs):
    inv_root = 1.0 / math.sqrt(sizes[2])
    own_ref, returned, total_ref = refs[0], refs[1:-1], refs[-1]
    for which, factor in ((0, inv_root), (1, 1.0)):
        total = own_ref[which] * factor
        for ref in returned:
            total += ref[which].astype(jnp.float32)
        total_ref[which] = total


def late_kernel(*refs):
    total_ref, returned, sum_ref = refs[0], refs[1:-1], refs[-1]
    for which in range(2):
        total = total_ref[which]
        for ref in returned:
            total += ref[which].astype(jnp.float32)
        sum_ref[which] = total.astype(jnp.bfloat16)


def final_kernel(
    sizes, sum_ref, query_ref, back_ref, query_hbm, key_hbm, value_hbm, result_ref, sems
):
    inv_root = 1.0 / math.sqrt(sizes[2])
    copies = [
        pltpu.make_async_copy(sum_ref.at[0], key_hbm, sems.at[0]),
        pltpu.make_async_copy(sum_ref.at[1], value_hbm, sems.at[1]),
        pltpu.make_async_copy(result_ref, query_hbm, sems.at[2]),
    ]
    copies[0].start()
    copies[1].start()
    has_prev = lax.axis_index("outer") > 0
    back = jnp.where(has_prev, back_ref[...].astype(jnp.float32), 0.0)
    result_ref[...] = ((query_ref[...] + back) * inv_root).astype(jnp.bfloat16)
    copies[2].start()
    for copy in copies:
        copy.wait()


def on_device(queries, key_rows, value_rows, attn_out, grad_out, log_norms, pair_order):
    row_count, group_size, head_size = queries.shape
    inner_count = lax.axis_size("inner")
    outer_count = lax.axis_size("outer")
    assert inner_count & (inner_count - 1) == 0 and inner_count > 1
    sizes = (group_size, row_count, head_size)
    half = group_size * row_count
    away = list(range(1, inner_count))

    def flat(array):
        return jnp.swapaxes(array, 0, 1).reshape(-1, head_size)

    def in_hbm(array):
        return pltpu.with_memory_space_constraint(array, pltpu.HBM)

    def to_segment(block, ahead):
        route = [(at, (at + ahead) % outer_count) for at in range(outer_count)]
        return lax.ppermute(block, "outer", route)

    def exchange(block, step):
        route = []
        for inner in range(inner_count):
            for outer in range(outer_count):
                peer = inner ^ peer_offset(step, outer, inner_count)
                route.append((inner * outer_count + outer, peer * outer_count + outer))
        return lax.ppermute(block, ("inner", "outer"), route)

    vmem = pl.BlockSpec(memory_space=pltpu.VMEM)
    hbm = pl.BlockSpec(memory_space=pltpu.HBM)
    roomy = pltpu.CompilerParams(vmem_limit_bytes=32 * 2**20)

    def shape(dims, dtype):
        return jax.ShapeDtypeStruct(dims, dtype)

    def cost(blocks, data=2**20):
        each = group_size * row_count * row_count
        return pl.CostEstimate(
            flops=10 * blocks * each * head_size, bytes_accessed=data, transcendentals=blocks * each
        )

    block_shape = shape((2, row_count, head_size), jnp.bfloat16)

    pair, packet = pl.pallas_call(
        functools.partial(load_kernel, sizes),
        out_shape=(
            block_shape,
            shape((packet_rows(sizes), head_size), jnp.bfloat16),
        ),
        in_specs=[hbm] * 6,
        out_specs=(vmem,) * 2,
        scratch_shapes=[pltpu.VMEM((STAT_ROWS, row_count), jnp.float32), pltpu.SemaphoreType.DMA((6,))],
        cost_estimate=cost(0),
        compiler_params=roomy,
    )(
        *(
            in_hbm(array)
            for array in (
                flat(queries), flat(grad_out), flat(attn_out), log_norms, flat(key_rows), flat(value_rows)
            )
        )
    )
    next_packet = to_segment(packet, -1)
    blocks = {0: pair}
    for step in away:
        blocks[step] = exchange(pair, step)

    def scores_shape(count):
        return shape((count * row_count, half), jnp.bfloat16)

    near_scores, near_next_scores, own_total, stats, rank = pl.pallas_call(
        functools.partial(near_kernel, sizes, inner_count, outer_count),
        out_shape=(
            scores_shape(1),
            scores_shape(1),
            shape((2, row_count, head_size), jnp.float32),
            shape((2, STAT_ROWS, row_count), jnp.float32),
            shape((max(8, inner_count), row_count), jnp.int32),
        ),
        in_specs=[vmem] * 2 + [hbm, vmem],
        out_specs=(vmem,) * 5,
        scratch_shapes=[pltpu.SMEM((inner_count,), jnp.int32), pltpu.SemaphoreType.DMA],
        cost_estimate=cost(2),
        compiler_params=roomy,
    )(packet, next_packet, in_hbm(pair_order), pair)

    scores, next_scores, sums = [near_scores], [near_next_scores], {}
    middle = inner_count // 2 - 1
    held = [0]
    for steps in (away[:middle], away[middle:]):
        if steps:
            far_scores, far_next_scores, *terms = pl.pallas_call(
                functools.partial(far_kernel, sizes, inner_count, steps),
                out_shape=(scores_shape(len(steps)),) * 2 + (block_shape,) * len(steps),
                in_specs=[vmem] * (4 + len(steps)),
                out_specs=(vmem,) * (2 + len(steps)),
                cost_estimate=cost(2 * len(steps)),
                compiler_params=roomy,
            )(packet, next_packet, rank, stats, *(blocks[step] for step in steps))
            scores.append(far_scores)
            next_scores.append(far_next_scores)
            sums.update(zip(steps, terms))
            held += steps
    all_blocks = [blocks[step] for step in held]
    groups = len(scores)
    returned = [exchange(sums[step], step) for step in away]

    early_total = pl.pallas_call(
        functools.partial(early_kernel, sizes),
        out_shape=shape((2, row_count, head_size), jnp.float32),
        in_specs=[vmem] * (1 + middle),
        out_specs=vmem,
        cost_estimate=cost(8 * inner_count),
        compiler_params=roomy,
    )(own_total, *returned[:middle])
    early_total, next_scores[0] = lax.optimization_barrier((early_total, next_scores[0]))

    query_next = pl.pallas_call(
        functools.partial(back_kernel, sizes, outer_count, groups),
        out_shape=shape((half, head_size), jnp.bfloat16),
        in_specs=[vmem] * (groups + inner_count),
        out_specs=vmem,
        cost_estimate=cost(0, 0),
        compiler_params=roomy,
    )(*next_scores, *all_blocks)
    query_back = to_segment(query_next, 1)

    query_own = pl.pallas_call(
        functools.partial(query_kernel, sizes, groups),
        out_shape=shape((half, head_size), jnp.float32),
        in_specs=[vmem] * (groups + inner_count),
        out_specs=vmem,
        cost_estimate=cost(0, 0),
        compiler_params=roomy,
    )(*scores, *all_blocks)

    late_sum = pl.pallas_call(
        late_kernel,
        out_shape=block_shape,
        in_specs=[vmem] * (1 + len(away) - middle),
        out_specs=vmem,
        cost_estimate=cost(8 * inner_count),
        compiler_params=roomy,
    )(early_total, *returned[middle:])

    query_out, key_out, value_out = pl.pallas_call(
        functools.partial(final_kernel, sizes),
        out_shape=(
            shape((half, head_size), jnp.bfloat16),
            shape((row_count, head_size), jnp.bfloat16),
            shape((row_count, head_size), jnp.bfloat16),
        ),
        in_specs=[vmem] * 3,
        out_specs=(hbm,) * 3,
        scratch_shapes=[pltpu.VMEM((half, head_size), jnp.bfloat16), pltpu.SemaphoreType.DMA((3,))],
        compiler_params=roomy,
    )(late_sum, query_own, query_back)
    grad_queries = jnp.swapaxes(query_out.reshape(group_size, row_count, head_size), 0, 1)
    return (grad_queries, key_out[:, None, :], value_out[:, None, :])


def solution(mesh):
    in_specs = (
        P(("outer", "inner"), "head", None),
        P(("outer", "inner"), "head", None),
        P(("outer", "inner"), "head", None),
        P(("outer", "inner"), "head", None),
        P(("outer", "inner"), "head", None),
        P("head", ("outer", "inner")),
        P(),
    )
    out_specs = (
        P(("outer", "inner"), "head", None),
        P(("outer", "inner"), "head", None),
        P(("outer", "inner"), "head", None),
    )
    return jax.shard_map(
        on_device, mesh=mesh, in_specs=in_specs, out_specs=out_specs, check_vma=False
    )
```

```python
import functools
import math

import jax
import jax.numpy as jnp
from jax import lax
from jax.experimental import pallas as pl
from jax.experimental.pallas import tpu as pltpu
from jax.sharding import PartitionSpec as P

LOG2E = math.log2(math.e)
STAT_ROWS = 16
SPLIT = 3


def contract(lhs, rhs, lhs_dim, rhs_dim):
    return lax.dot_general(
        lhs, rhs, (((lhs_dim,), (rhs_dim,)), ((), ())), preferred_element_type=jnp.float32
    )


def packet_rows(sizes):
    group_size, row_count, _ = sizes
    return 3 * group_size * row_count + SPLIT * STAT_ROWS


def peer_offset(step, outer, inner_count):
    last = inner_count - 1
    if outer % 2 == 1:
        return (inner_count - step) % inner_count
    return {0: 0, 1: 1, 2: last}.get(step, step - 1)


def load_kernel(
    sizes, query_hbm, grad_hbm, out_hbm, norm_hbm, key_hbm, value_hbm, pair_ref, packet_ref, norm_ref, sems
):
    group_size, row_count, _ = sizes
    half = group_size * row_count
    copies = [
        pltpu.make_async_copy(source, target, sems.at[at])
        for at, (source, target) in enumerate(
            [
                (query_hbm, packet_ref.at[pl.ds(0, half)]),
                (grad_hbm, packet_ref.at[pl.ds(half, half)]),
                (out_hbm, packet_ref.at[pl.ds(2 * half, half)]),
                (norm_hbm, norm_ref.at[pl.ds(0, group_size)]),
                (key_hbm, pair_ref.at[0]),
                (value_hbm, pair_ref.at[1]),
            ]
        )
    ]
    for copy in copies:
        copy.start()
    copies[3].wait()
    held = lax.broadcasted_iota(jnp.int32, (STAT_ROWS, row_count), 0) < group_size
    rest = jnp.where(held, jnp.clip(norm_ref[...], -3.38e38, 3.38e38), 0.0)
    for term in range(SPLIT):
        piece = rest.astype(jnp.bfloat16)
        start = 3 * half + term * STAT_ROWS
        packet_ref[start : start + STAT_ROWS, :] = piece
        rest = rest - piece.astype(jnp.float32)
    for copy in copies[:3] + copies[4:]:
        copy.wait()


def row_stats(packet_ref, stat_ref, sizes):
    group_size, row_count, _ = sizes
    half = group_size * row_count
    start = 3 * half
    pieces = [
        packet_ref[start + term * STAT_ROWS : start + (term + 1) * STAT_ROWS, :].astype(jnp.float32)
        for term in range(SPLIT)
    ]
    stat_ref[...] = (pieces[0] + (pieces[1] + pieces[2])) * LOG2E
    for head in range(group_size):
        first = head * row_count
        grads = packet_ref[half + first : half + first + row_count, :].astype(jnp.float32)
        outs = packet_ref[2 * half + first : 2 * half + first + row_count, :].astype(jnp.float32)
        stat_ref[8 + head : 9 + head, :] = jnp.sum((grads * outs).T, axis=0, keepdims=True)


def block_terms(keys, values, parts, sizes):
    group_size, row_count, head_size = sizes
    half = group_size * row_count
    scale = LOG2E / math.sqrt(head_size)
    per_step = 2 if group_size % 2 == 0 else 1
    key_total = 0.0
    value_total = 0.0
    for packet_ref, stats, visible, scores_ref in parts:
        weights_parts = []
        score_parts = []
        for first in range(0, group_size, per_step):
            start, stop = first * row_count, (first + per_step) * row_count
            queries = packet_ref[start:stop, :]
            grads = packet_ref[half + start : half + stop, :]
            scores = contract(keys, queries, 1, 1)
            grad_weights = contract(values, grads, 1, 1)
            for at in range(per_step):
                head = first + at
                lanes = slice(at * row_count, (at + 1) * row_count)
                weights = jnp.exp2(scores[:, lanes] * scale - stats[head : head + 1, :])
                if visible is not None:
                    weights = jnp.where(visible, weights, 0.0)
                weights_parts.append(weights.astype(jnp.bfloat16))
                score_parts.append(
                    (weights * (grad_weights[:, lanes] - stats[8 + head : 9 + head, :])).astype(jnp.bfloat16)
                )
        grad_scores = jnp.concatenate(score_parts, axis=1)
        scores_ref[...] = grad_scores
        value_total += contract(jnp.concatenate(weights_parts, axis=1), packet_ref[half : 2 * half, :], 1, 0)
        key_total += contract(grad_scores, packet_ref[:half, :], 1, 0)
    return key_total, value_total


def visible_rows(rank_ref, steps, inner_count, row_count):
    span_rows = row_count // 2
    key_rows = lax.broadcasted_iota(jnp.int32, (row_count, row_count), 0)
    my_rows = lax.broadcasted_iota(jnp.int32, (row_count, row_count), 1)

    def positions(rank, rows):
        return jnp.where(
            rows < span_rows,
            rank * span_rows + rows,
            (2 * inner_count - 2 - rank) * span_rows + rows,
        )

    mine = positions(rank_ref[0:1, :], my_rows)
    return jnp.concatenate(
        [positions(rank_ref[step : step + 1, :], key_rows) <= mine for step in steps], axis=0
    )


def stacked(blocks, which):
    return jnp.concatenate([ref[which] for ref in blocks], axis=0)


def near_kernel(
    sizes, inner_count, outer_count, packet_ref, next_ref, order_hbm, pair_ref, scores_ref,
    next_scores_ref, total_ref, stat_ref, rank_ref, order_ref, sem,
):
    _, row_count, _ = sizes
    copy = pltpu.make_async_copy(order_hbm, order_ref, sem)
    copy.start()
    has_next = lax.axis_index("outer") < outer_count - 1
    key_rows = lax.broadcasted_iota(jnp.int32, (row_count, row_count), 0)
    visible = key_rows <= lax.broadcasted_iota(jnp.int32, (row_count, row_count), 1)
    row_stats(packet_ref, stat_ref.at[0], sizes)

    def add_up(both):
        parts = [(packet_ref, stat_ref[0], visible, scores_ref)]
        if both:
            row_stats(next_ref, stat_ref.at[1], sizes)
            parts.append((next_ref, stat_ref[1], None, next_scores_ref))
        total_ref[0], total_ref[1] = block_terms(pair_ref[0], pair_ref[1], parts, sizes)

    pl.when(has_next)(lambda: add_up(True))
    pl.when(jnp.logical_not(has_next))(lambda: add_up(False))
    copy.wait()
    my_index = lax.axis_index("inner")
    turned = lax.rem(lax.axis_index("outer"), 2) == 1
    for step in range(inner_count):
        offset = jnp.where(turned, peer_offset(step, 1, inner_count), peer_offset(step, 0, inner_count))
        rank_ref[step : step + 1, :] = jnp.full((1, row_count), order_ref[my_index ^ offset], jnp.int32)


def far_kernel(sizes, inner_count, outer_count, steps, packet_ref, next_ref, rank_ref, stat_ref, *refs):
    count = len(steps)
    _, row_count, head_size = sizes
    inv_root = 1.0 / math.sqrt(head_size)
    blocks, (scores_ref, next_scores_ref), sums = refs[:count], refs[count : count + 2], refs[count + 2 :]
    has_next = lax.axis_index("outer") < outer_count - 1

    def add_up(both):
        visible = visible_rows(rank_ref, steps, inner_count, row_count)
        parts = [(packet_ref, stat_ref[0], visible, scores_ref)]
        if both:
            parts.append((next_ref, stat_ref[1], None, next_scores_ref))
        key_total, value_total = block_terms(stacked(blocks, 0), stacked(blocks, 1), parts, sizes)
        for at, ref in enumerate(sums):
            rows = slice(at * row_count, (at + 1) * row_count)
            ref[0] = (key_total[rows] * inv_root).astype(jnp.bfloat16)
            ref[1] = value_total[rows].astype(jnp.bfloat16)

    pl.when(has_next)(lambda: add_up(True))
    pl.when(jnp.logical_not(has_next))(lambda: add_up(False))


def query_terms(refs, groups, lanes):
    scores = jnp.concatenate([ref[:, lanes] for ref in refs[:groups]], axis=0)
    return contract(stacked(refs[groups:], 0), scores, 0, 0)


def store_queries(result_ref, refs, groups, sizes):
    group_size, row_count, head_size = sizes
    terms = query_terms(refs, groups, slice(None)) * (1.0 / math.sqrt(head_size))
    for head in range(group_size):
        rows = slice(head * row_count, (head + 1) * row_count)
        result_ref[rows, :] = terms[:, rows].T.astype(result_ref.dtype)


def back_kernel(sizes, outer_count, groups, *refs):
    has_next = lax.axis_index("outer") < outer_count - 1

    @pl.when(has_next)
    def _():
        store_queries(refs[-1], refs[:-1], groups, sizes)


def query_kernel(sizes, groups, *refs):
    store_queries(refs[-1], refs[:-1], groups, sizes)


def early_kernel(sizes, *refs):
    inv_root = 1.0 / math.sqrt(sizes[2])
    own_ref, returned, total_ref = refs[0], refs[1:-1], refs[-1]
    for which, factor in ((0, inv_root), (1, 1.0)):
        total = own_ref[which] * factor
        for ref in returned:
            total += ref[which].astype(jnp.float32)
        total_ref[which] = total


def late_kernel(*refs):
    total_ref, returned, sum_ref = refs[0], refs[1:-1], refs[-1]
    for which in range(2):
        total = total_ref[which]
        for ref in returned:
            total += ref[which].astype(jnp.float32)
        sum_ref[which] = total.astype(jnp.bfloat16)


def final_kernel(
    parts, sum_ref, query_ref, back_ref, query_hbm, key_hbm, value_hbm, result_ref, sems
):
    copies = [
        pltpu.make_async_copy(sum_ref.at[0], key_hbm, sems.at[0]),
        pltpu.make_async_copy(sum_ref.at[1], value_hbm, sems.at[1]),
    ]
    for copy in copies:
        copy.start()
    has_prev = lax.axis_index("outer") > 0
    count = query_ref.shape[0] // parts
    for part in range(parts):
        rows = pl.ds(part * count, count)
        back = jnp.where(has_prev, back_ref[rows, :].astype(jnp.float32), 0.0)
        result_ref[rows, :] = (query_ref[rows, :] + back).astype(jnp.bfloat16)
        copy = pltpu.make_async_copy(result_ref.at[rows], query_hbm.at[rows], sems.at[2 + part])
        copy.start()
        copies.append(copy)
    for copy in copies:
        copy.wait()


def on_device(queries, key_rows, value_rows, attn_out, grad_out, log_norms, pair_order):
    row_count, group_size, head_size = queries.shape
    inner_count = lax.axis_size("inner")
    outer_count = lax.axis_size("outer")
    assert inner_count & (inner_count - 1) == 0 and inner_count > 1
    sizes = (group_size, row_count, head_size)
    half = group_size * row_count
    away = list(range(1, inner_count))

    def flat(array):
        return jnp.swapaxes(array, 0, 1).reshape(-1, head_size)

    def in_hbm(array):
        return pltpu.with_memory_space_constraint(array, pltpu.HBM)

    def to_segment(block, ahead):
        route = [(at, (at + ahead) % outer_count) for at in range(outer_count)]
        return lax.ppermute(block, "outer", route)

    def exchange(block, step):
        route = []
        for inner in range(inner_count):
            for outer in range(outer_count):
                peer = inner ^ peer_offset(step, outer, inner_count)
                route.append((inner * outer_count + outer, peer * outer_count + outer))
        return lax.ppermute(block, ("inner", "outer"), route)

    vmem = pl.BlockSpec(memory_space=pltpu.VMEM)
    hbm = pl.BlockSpec(memory_space=pltpu.HBM)
    roomy = pltpu.CompilerParams(vmem_limit_bytes=32 * 2**20)

    def shape(dims, dtype):
        return jax.ShapeDtypeStruct(dims, dtype)

    def cost(blocks, data=2**20):
        each = group_size * row_count * row_count
        return pl.CostEstimate(
            flops=10 * blocks * each * head_size, bytes_accessed=data, transcendentals=blocks * each
        )

    block_shape = shape((2, row_count, head_size), jnp.bfloat16)

    pair, packet = pl.pallas_call(
        functools.partial(load_kernel, sizes),
        out_shape=(
            block_shape,
            shape((packet_rows(sizes), head_size), jnp.bfloat16),
        ),
        in_specs=[hbm] * 6,
        out_specs=(vmem,) * 2,
        scratch_shapes=[pltpu.VMEM((STAT_ROWS, row_count), jnp.float32), pltpu.SemaphoreType.DMA((6,))],
        cost_estimate=cost(0),
        compiler_params=roomy,
    )(
        *(
            in_hbm(array)
            for array in (
                flat(queries), flat(grad_out), flat(attn_out), log_norms, flat(key_rows), flat(value_rows)
            )
        )
    )
    next_packet = to_segment(packet, -1)
    blocks = {0: pair}
    for step in away:
        blocks[step] = exchange(pair, step)

    def scores_shape(count):
        return shape((count * row_count, half), jnp.bfloat16)

    near_scores, near_next_scores, own_total, stats, rank = pl.pallas_call(
        functools.partial(near_kernel, sizes, inner_count, outer_count),
        out_shape=(
            scores_shape(1),
            scores_shape(1),
            shape((2, row_count, head_size), jnp.float32),
            shape((2, STAT_ROWS, row_count), jnp.float32),
            shape((max(8, inner_count), row_count), jnp.int32),
        ),
        in_specs=[vmem] * 2 + [hbm, vmem],
        out_specs=(vmem,) * 5,
        scratch_shapes=[pltpu.SMEM((inner_count,), jnp.int32), pltpu.SemaphoreType.DMA],
        cost_estimate=cost(2),
        compiler_params=roomy,
    )(packet, next_packet, in_hbm(pair_order), pair)

    scores, next_scores, sums = [near_scores], [near_next_scores], {}
    middle = inner_count // 2 - 1
    held = [0]
    for steps in (away[:middle], away[middle:]):
        if steps:
            far_scores, far_next_scores, *terms = pl.pallas_call(
                functools.partial(far_kernel, sizes, inner_count, outer_count, steps),
                out_shape=(scores_shape(len(steps)),) * 2 + (block_shape,) * len(steps),
                in_specs=[vmem] * (4 + len(steps)),
                out_specs=(vmem,) * (2 + len(steps)),
                cost_estimate=cost(2 * len(steps)),
                compiler_params=roomy,
            )(packet, next_packet, rank, stats, *(blocks[step] for step in steps))
            scores.append(far_scores)
            next_scores.append(far_next_scores)
            sums.update(zip(steps, terms))
            held += steps
    all_blocks = [blocks[step] for step in held]
    groups = len(scores)
    returned = [exchange(sums[step], step) for step in away]

    early_total = pl.pallas_call(
        functools.partial(early_kernel, sizes),
        out_shape=shape((2, row_count, head_size), jnp.float32),
        in_specs=[vmem] * (1 + middle),
        out_specs=vmem,
        cost_estimate=cost(8 * inner_count),
        compiler_params=roomy,
    )(own_total, *returned[:middle])
    early_total, next_scores[0] = lax.optimization_barrier((early_total, next_scores[0]))

    query_next = pl.pallas_call(
        functools.partial(back_kernel, sizes, outer_count, groups),
        out_shape=shape((half, head_size), jnp.bfloat16),
        in_specs=[vmem] * (groups + inner_count),
        out_specs=vmem,
        cost_estimate=cost(0, 0),
        compiler_params=roomy,
    )(*next_scores, *all_blocks)
    query_back = to_segment(query_next, 1)

    query_own = pl.pallas_call(
        functools.partial(query_kernel, sizes, groups),
        out_shape=shape((half, head_size), jnp.float32),
        in_specs=[vmem] * (groups + inner_count),
        out_specs=vmem,
        cost_estimate=cost(0, 0),
        compiler_params=roomy,
    )(*scores, *all_blocks)

    late_sum = pl.pallas_call(
        late_kernel,
        out_shape=block_shape,
        in_specs=[vmem] * (1 + len(away) - middle),
        out_specs=vmem,
        cost_estimate=cost(8 * inner_count),
        compiler_params=roomy,
    )(early_total, *returned[middle:])

    query_out, key_out, value_out = pl.pallas_call(
        functools.partial(final_kernel, group_size),
        out_shape=(
            shape((half, head_size), jnp.bfloat16),
            shape((row_count, head_size), jnp.bfloat16),
            shape((row_count, head_size), jnp.bfloat16),
        ),
        in_specs=[vmem] * 3,
        out_specs=(hbm,) * 3,
        scratch_shapes=[pltpu.VMEM((half, head_size), jnp.bfloat16), pltpu.SemaphoreType.DMA((2 + group_size,))],
        compiler_params=roomy,
    )(late_sum, query_own, query_back)
    grad_queries = jnp.swapaxes(query_out.reshape(group_size, row_count, head_size), 0, 1)
    return (grad_queries, key_out[:, None, :], value_out[:, None, :])


def solution(mesh):
    in_specs = (
        P(("outer", "inner"), "head", None),
        P(("outer", "inner"), "head", None),
        P(("outer", "inner"), "head", None),
        P(("outer", "inner"), "head", None),
        P(("outer", "inner"), "head", None),
        P("head", ("outer", "inner")),
        P(),
    )
    out_specs = (
        P(("outer", "inner"), "head", None),
        P(("outer", "inner"), "head", None),
        P(("outer", "inner"), "head", None),
    )
    return jax.shard_map(
        on_device, mesh=mesh, in_specs=in_specs, out_specs=out_specs, check_vma=False
    )
```

```python
import functools
import math

import jax
import jax.numpy as jnp
from jax import lax
from jax.experimental import pallas as pl
from jax.experimental.pallas import tpu as pltpu
from jax.sharding import PartitionSpec as P

LOG2E = math.log2(math.e)
STAT_ROWS = 16
SPLIT = 3


def contract(lhs, rhs, lhs_dim, rhs_dim):
    return lax.dot_general(
        lhs, rhs, (((lhs_dim,), (rhs_dim,)), ((), ())), preferred_element_type=jnp.float32
    )


def packet_rows(sizes):
    group_size, row_count, _ = sizes
    return 3 * group_size * row_count + SPLIT * STAT_ROWS


def peer_offset(step, outer, inner_count):
    last = inner_count - 1
    if outer % 2 == 1:
        return (inner_count - step) % inner_count
    return {0: 0, 1: 1, 2: last}.get(step, step - 1)


def load_kernel(
    sizes, query_hbm, grad_hbm, out_hbm, norm_hbm, key_hbm, value_hbm, pair_ref, packet_ref, norm_ref, sems
):
    group_size, row_count, _ = sizes
    half = group_size * row_count
    copies = [
        pltpu.make_async_copy(source, target, sems.at[at])
        for at, (source, target) in enumerate(
            [
                (query_hbm, packet_ref.at[pl.ds(0, half)]),
                (grad_hbm, packet_ref.at[pl.ds(half, half)]),
                (out_hbm, packet_ref.at[pl.ds(2 * half, half)]),
                (norm_hbm, norm_ref.at[pl.ds(0, group_size)]),
                (key_hbm, pair_ref.at[0]),
                (value_hbm, pair_ref.at[1]),
            ]
        )
    ]
    for copy in copies:
        copy.start()
    copies[3].wait()
    held = lax.broadcasted_iota(jnp.int32, (STAT_ROWS, row_count), 0) < group_size
    rest = jnp.where(held, jnp.clip(norm_ref[...], -3.38e38, 3.38e38), 0.0)
    for term in range(SPLIT):
        piece = rest.astype(jnp.bfloat16)
        start = 3 * half + term * STAT_ROWS
        packet_ref[start : start + STAT_ROWS, :] = piece
        rest = rest - piece.astype(jnp.float32)
    for copy in copies[:3] + copies[4:]:
        copy.wait()


def row_stats(packet_ref, stat_ref, sizes):
    group_size, row_count, _ = sizes
    half = group_size * row_count
    start = 3 * half
    pieces = [
        packet_ref[start + term * STAT_ROWS : start + (term + 1) * STAT_ROWS, :].astype(jnp.float32)
        for term in range(SPLIT)
    ]
    stat_ref[...] = (pieces[0] + (pieces[1] + pieces[2])) * LOG2E
    for head in range(group_size):
        first = head * row_count
        grads = packet_ref[half + first : half + first + row_count, :].astype(jnp.float32)
        outs = packet_ref[2 * half + first : 2 * half + first + row_count, :].astype(jnp.float32)
        stat_ref[8 + head : 9 + head, :] = jnp.sum((grads * outs).T, axis=0, keepdims=True)


def block_terms(keys, values, parts, sizes):
    group_size, row_count, head_size = sizes
    half = group_size * row_count
    scale = LOG2E / math.sqrt(head_size)
    key_total = 0.0
    value_total = 0.0
    for packet_ref, stats, visible, scores_ref in parts:
        weights_parts = []
        score_parts = []
        scores = contract(keys, packet_ref[:half, :], 1, 1)
        grad_weights = contract(values, packet_ref[half : 2 * half, :], 1, 1)
        for head in range(group_size):
            lanes = slice(head * row_count, (head + 1) * row_count)
            weights = jnp.exp2(scores[:, lanes] * scale - stats[head : head + 1, :])
            if visible is not None:
                weights = jnp.where(visible, weights, 0.0)
            weights_parts.append(weights.astype(jnp.bfloat16))
            score_parts.append(
                (weights * (grad_weights[:, lanes] - stats[8 + head : 9 + head, :])).astype(jnp.bfloat16)
            )
        grad_scores = jnp.concatenate(score_parts, axis=1)
        scores_ref[...] = grad_scores
        value_total += contract(jnp.concatenate(weights_parts, axis=1), packet_ref[half : 2 * half, :], 1, 0)
        key_total += contract(grad_scores, packet_ref[:half, :], 1, 0)
    return key_total, value_total


def visible_rows(rank_ref, steps, inner_count, row_count):
    span_rows = row_count // 2
    key_rows = lax.broadcasted_iota(jnp.int32, (row_count, row_count), 0)
    my_rows = lax.broadcasted_iota(jnp.int32, (row_count, row_count), 1)

    def positions(rank, rows):
        return jnp.where(
            rows < span_rows,
            rank * span_rows + rows,
            (2 * inner_count - 2 - rank) * span_rows + rows,
        )

    mine = positions(rank_ref[0:1, :], my_rows)
    return jnp.concatenate(
        [positions(rank_ref[step : step + 1, :], key_rows) <= mine for step in steps], axis=0
    )


def stacked(blocks, which):
    return jnp.concatenate([ref[which] for ref in blocks], axis=0)


def near_kernel(
    sizes, inner_count, outer_count, packet_ref, next_ref, order_hbm, pair_ref, scores_ref,
    next_scores_ref, total_ref, stat_ref, rank_ref, order_ref, sem,
):
    _, row_count, _ = sizes
    copy = pltpu.make_async_copy(order_hbm, order_ref, sem)
    copy.start()
    has_next = lax.axis_index("outer") < outer_count - 1
    key_rows = lax.broadcasted_iota(jnp.int32, (row_count, row_count), 0)
    visible = key_rows <= lax.broadcasted_iota(jnp.int32, (row_count, row_count), 1)
    row_stats(packet_ref, stat_ref.at[0], sizes)

    def add_up(both):
        parts = [(packet_ref, stat_ref[0], visible, scores_ref)]
        if both:
            row_stats(next_ref, stat_ref.at[1], sizes)
            parts.append((next_ref, stat_ref[1], None, next_scores_ref))
        total_ref[0], total_ref[1] = block_terms(pair_ref[0], pair_ref[1], parts, sizes)

    pl.when(has_next)(lambda: add_up(True))
    pl.when(jnp.logical_not(has_next))(lambda: add_up(False))
    copy.wait()
    my_index = lax.axis_index("inner")
    turned = lax.rem(lax.axis_index("outer"), 2) == 1
    for step in range(inner_count):
        offset = jnp.where(turned, peer_offset(step, 1, inner_count), peer_offset(step, 0, inner_count))
        rank_ref[step : step + 1, :] = jnp.full((1, row_count), order_ref[my_index ^ offset], jnp.int32)


def far_kernel(sizes, inner_count, outer_count, steps, packet_ref, next_ref, rank_ref, stat_ref, *refs):
    count = len(steps)
    _, row_count, head_size = sizes
    inv_root = 1.0 / math.sqrt(head_size)
    blocks, (scores_ref, next_scores_ref), sums = refs[:count], refs[count : count + 2], refs[count + 2 :]
    has_next = lax.axis_index("outer") < outer_count - 1

    def add_up(both):
        visible = visible_rows(rank_ref, steps, inner_count, row_count)
        parts = [(packet_ref, stat_ref[0], visible, scores_ref)]
        if both:
            parts.append((next_ref, stat_ref[1], None, next_scores_ref))
        key_total, value_total = block_terms(stacked(blocks, 0), stacked(blocks, 1), parts, sizes)
        for at, ref in enumerate(sums):
            rows = slice(at * row_count, (at + 1) * row_count)
            ref[0] = (key_total[rows] * inv_root).astype(jnp.bfloat16)
            ref[1] = value_total[rows].astype(jnp.bfloat16)

    pl.when(has_next)(lambda: add_up(True))
    pl.when(jnp.logical_not(has_next))(lambda: add_up(False))


def query_terms(refs, groups, lanes):
    scores = jnp.concatenate([ref[:, lanes] for ref in refs[:groups]], axis=0)
    return contract(stacked(refs[groups:], 0), scores, 0, 0)


def store_queries(result_ref, refs, groups, sizes):
    group_size, row_count, head_size = sizes
    terms = query_terms(refs, groups, slice(None)) * (1.0 / math.sqrt(head_size))
    for head in range(group_size):
        rows = slice(head * row_count, (head + 1) * row_count)
        result_ref[rows, :] = terms[:, rows].T.astype(result_ref.dtype)


def back_kernel(sizes, outer_count, groups, *refs):
    has_next = lax.axis_index("outer") < outer_count - 1

    @pl.when(has_next)
    def _():
        store_queries(refs[-1], refs[:-1], groups, sizes)


def query_kernel(sizes, groups, *refs):
    store_queries(refs[-1], refs[:-1], groups, sizes)


def early_kernel(sizes, *refs):
    inv_root = 1.0 / math.sqrt(sizes[2])
    own_ref, returned, total_ref = refs[0], refs[1:-1], refs[-1]
    for which, factor in ((0, inv_root), (1, 1.0)):
        total = own_ref[which] * factor
        for ref in returned:
            total += ref[which].astype(jnp.float32)
        total_ref[which] = total


def late_kernel(*refs):
    total_ref, returned, sum_ref = refs[0], refs[1:-1], refs[-1]
    for which in range(2):
        total = total_ref[which]
        for ref in returned:
            total += ref[which].astype(jnp.float32)
        sum_ref[which] = total.astype(jnp.bfloat16)


def final_kernel(
    parts, sum_ref, query_ref, back_ref, query_hbm, key_hbm, value_hbm, result_ref, sems
):
    copies = [
        pltpu.make_async_copy(sum_ref.at[0], key_hbm, sems.at[0]),
        pltpu.make_async_copy(sum_ref.at[1], value_hbm, sems.at[1]),
    ]
    for copy in copies:
        copy.start()
    has_prev = lax.axis_index("outer") > 0
    count = query_ref.shape[0] // parts
    for part in range(parts):
        rows = pl.ds(part * count, count)
        back = jnp.where(has_prev, back_ref[rows, :].astype(jnp.float32), 0.0)
        result_ref[rows, :] = (query_ref[rows, :] + back).astype(jnp.bfloat16)
        copy = pltpu.make_async_copy(result_ref.at[rows], query_hbm.at[rows], sems.at[2 + part])
        copy.start()
        copies.append(copy)
    for copy in copies:
        copy.wait()


def on_device(queries, key_rows, value_rows, attn_out, grad_out, log_norms, pair_order):
    row_count, group_size, head_size = queries.shape
    inner_count = lax.axis_size("inner")
    outer_count = lax.axis_size("outer")
    assert inner_count & (inner_count - 1) == 0 and inner_count > 1
    sizes = (group_size, row_count, head_size)
    half = group_size * row_count
    away = list(range(1, inner_count))

    def flat(array):
        return jnp.swapaxes(array, 0, 1).reshape(-1, head_size)

    def in_hbm(array):
        return pltpu.with_memory_space_constraint(array, pltpu.HBM)

    def to_segment(block, ahead):
        route = [(at, (at + ahead) % outer_count) for at in range(outer_count)]
        return lax.ppermute(block, "outer", route)

    def exchange(block, step):
        route = []
        for inner in range(inner_count):
            for outer in range(outer_count):
                peer = inner ^ peer_offset(step, outer, inner_count)
                route.append((inner * outer_count + outer, peer * outer_count + outer))
        return lax.ppermute(block, ("inner", "outer"), route)

    vmem = pl.BlockSpec(memory_space=pltpu.VMEM)
    hbm = pl.BlockSpec(memory_space=pltpu.HBM)
    roomy = pltpu.CompilerParams(vmem_limit_bytes=32 * 2**20)

    def shape(dims, dtype):
        return jax.ShapeDtypeStruct(dims, dtype)

    def cost(blocks, data=2**20):
        each = group_size * row_count * row_count
        return pl.CostEstimate(
            flops=10 * blocks * each * head_size, bytes_accessed=data, transcendentals=blocks * each
        )

    block_shape = shape((2, row_count, head_size), jnp.bfloat16)

    pair, packet = pl.pallas_call(
        functools.partial(load_kernel, sizes),
        out_shape=(
            block_shape,
            shape((packet_rows(sizes), head_size), jnp.bfloat16),
        ),
        in_specs=[hbm] * 6,
        out_specs=(vmem,) * 2,
        scratch_shapes=[pltpu.VMEM((STAT_ROWS, row_count), jnp.float32), pltpu.SemaphoreType.DMA((6,))],
        cost_estimate=cost(0),
        compiler_params=roomy,
    )(
        *(
            in_hbm(array)
            for array in (
                flat(queries), flat(grad_out), flat(attn_out), log_norms, flat(key_rows), flat(value_rows)
            )
        )
    )
    next_packet = to_segment(packet, -1)
    blocks = {0: pair}
    for step in away:
        blocks[step] = exchange(pair, step)

    def scores_shape(count):
        return shape((count * row_count, half), jnp.bfloat16)

    near_scores, near_next_scores, own_total, stats, rank = pl.pallas_call(
        functools.partial(near_kernel, sizes, inner_count, outer_count),
        out_shape=(
            scores_shape(1),
            scores_shape(1),
            shape((2, row_count, head_size), jnp.float32),
            shape((2, STAT_ROWS, row_count), jnp.float32),
            shape((max(8, inner_count), row_count), jnp.int32),
        ),
        in_specs=[vmem] * 2 + [hbm, vmem],
        out_specs=(vmem,) * 5,
        scratch_shapes=[pltpu.SMEM((inner_count,), jnp.int32), pltpu.SemaphoreType.DMA],
        cost_estimate=cost(2),
        compiler_params=roomy,
    )(packet, next_packet, in_hbm(pair_order), pair)

    scores, next_scores, sums = [near_scores], [near_next_scores], {}
    middle = inner_count // 2 - 1
    held = [0]
    for steps in (away[:middle], away[middle:]):
        if steps:
            far_scores, far_next_scores, *terms = pl.pallas_call(
                functools.partial(far_kernel, sizes, inner_count, outer_count, steps),
                out_shape=(scores_shape(len(steps)),) * 2 + (block_shape,) * len(steps),
                in_specs=[vmem] * (4 + len(steps)),
                out_specs=(vmem,) * (2 + len(steps)),
                cost_estimate=cost(2 * len(steps)),
                compiler_params=roomy,
            )(packet, next_packet, rank, stats, *(blocks[step] for step in steps))
            scores.append(far_scores)
            next_scores.append(far_next_scores)
            sums.update(zip(steps, terms))
            held += steps
    all_blocks = [blocks[step] for step in held]
    groups = len(scores)
    returned = [exchange(sums[step], step) for step in away]

    early_total = pl.pallas_call(
        functools.partial(early_kernel, sizes),
        out_shape=shape((2, row_count, head_size), jnp.float32),
        in_specs=[vmem] * (1 + middle),
        out_specs=vmem,
        cost_estimate=cost(8 * inner_count),
        compiler_params=roomy,
    )(own_total, *returned[:middle])
    early_total, next_scores[0] = lax.optimization_barrier((early_total, next_scores[0]))

    query_next = pl.pallas_call(
        functools.partial(back_kernel, sizes, outer_count, groups),
        out_shape=shape((half, head_size), jnp.bfloat16),
        in_specs=[vmem] * (groups + inner_count),
        out_specs=vmem,
        cost_estimate=cost(0, 0),
        compiler_params=roomy,
    )(*next_scores, *all_blocks)
    query_back = to_segment(query_next, 1)

    query_own = pl.pallas_call(
        functools.partial(query_kernel, sizes, groups),
        out_shape=shape((half, head_size), jnp.float32),
        in_specs=[vmem] * (groups + inner_count),
        out_specs=vmem,
        cost_estimate=cost(0, 0),
        compiler_params=roomy,
    )(*scores, *all_blocks)

    late_sum = pl.pallas_call(
        late_kernel,
        out_shape=block_shape,
        in_specs=[vmem] * (1 + len(away) - middle),
        out_specs=vmem,
        cost_estimate=cost(8 * inner_count),
        compiler_params=roomy,
    )(early_total, *returned[middle:])

    query_out, key_out, value_out = pl.pallas_call(
        functools.partial(final_kernel, group_size),
        out_shape=(
            shape((half, head_size), jnp.bfloat16),
            shape((row_count, head_size), jnp.bfloat16),
            shape((row_count, head_size), jnp.bfloat16),
        ),
        in_specs=[vmem] * 3,
        out_specs=(hbm,) * 3,
        scratch_shapes=[pltpu.VMEM((half, head_size), jnp.bfloat16), pltpu.SemaphoreType.DMA((2 + group_size,))],
        compiler_params=roomy,
    )(late_sum, query_own, query_back)
    grad_queries = jnp.swapaxes(query_out.reshape(group_size, row_count, head_size), 0, 1)
    return (grad_queries, key_out[:, None, :], value_out[:, None, :])


def solution(mesh):
    in_specs = (
        P(("outer", "inner"), "head", None),
        P(("outer", "inner"), "head", None),
        P(("outer", "inner"), "head", None),
        P(("outer", "inner"), "head", None),
        P(("outer", "inner"), "head", None),
        P("head", ("outer", "inner")),
        P(),
    )
    out_specs = (
        P(("outer", "inner"), "head", None),
        P(("outer", "inner"), "head", None),
        P(("outer", "inner"), "head", None),
    )
    return jax.shard_map(
        on_device, mesh=mesh, in_specs=in_specs, out_specs=out_specs, check_vma=False
    )
```

```python
import functools
import math

import jax
import jax.numpy as jnp
from jax import lax
from jax.experimental import pallas as pl
from jax.experimental.pallas import tpu as pltpu
from jax.sharding import PartitionSpec as P

LOG2E = math.log2(math.e)
STAT_ROWS = 16
SPLIT = 3


def contract(lhs, rhs, lhs_dim, rhs_dim):
    return lax.dot_general(
        lhs, rhs, (((lhs_dim,), (rhs_dim,)), ((), ())), preferred_element_type=jnp.float32
    )


def packet_rows(sizes):
    group_size, row_count, _ = sizes
    return 3 * group_size * row_count + SPLIT * STAT_ROWS


def peer_offset(step, outer, inner_count):
    last = inner_count - 1
    if outer % 2 == 1:
        return {0: 0, 1: last - 1, last: last}.get(step, step - 1)
    return {0: 0, 1: 1, 2: last}.get(step, step - 1)


def load_kernel(
    sizes, query_hbm, grad_hbm, out_hbm, norm_hbm, key_hbm, value_hbm, pair_ref, packet_ref, norm_ref, sems
):
    group_size, row_count, _ = sizes
    half = group_size * row_count
    copies = [
        pltpu.make_async_copy(source, target, sems.at[at])
        for at, (source, target) in enumerate(
            [
                (query_hbm, packet_ref.at[pl.ds(0, half)]),
                (grad_hbm, packet_ref.at[pl.ds(half, half)]),
                (out_hbm, packet_ref.at[pl.ds(2 * half, half)]),
                (norm_hbm, norm_ref.at[pl.ds(0, group_size)]),
                (key_hbm, pair_ref.at[0]),
                (value_hbm, pair_ref.at[1]),
            ]
        )
    ]
    for copy in copies:
        copy.start()
    copies[3].wait()
    held = lax.broadcasted_iota(jnp.int32, (STAT_ROWS, row_count), 0) < group_size
    rest = jnp.where(held, jnp.clip(norm_ref[...], -3.38e38, 3.38e38), 0.0)
    for term in range(SPLIT):
        piece = rest.astype(jnp.bfloat16)
        start = 3 * half + term * STAT_ROWS
        packet_ref[start : start + STAT_ROWS, :] = piece
        rest = rest - piece.astype(jnp.float32)
    for copy in copies[:3] + copies[4:]:
        copy.wait()


def row_stats(packet_ref, stat_ref, sizes):
    group_size, row_count, _ = sizes
    half = group_size * row_count
    start = 3 * half
    pieces = [
        packet_ref[start + term * STAT_ROWS : start + (term + 1) * STAT_ROWS, :].astype(jnp.float32)
        for term in range(SPLIT)
    ]
    stat_ref[...] = (pieces[0] + (pieces[1] + pieces[2])) * LOG2E
    for head in range(group_size):
        first = head * row_count
        grads = packet_ref[half + first : half + first + row_count, :].astype(jnp.float32)
        outs = packet_ref[2 * half + first : 2 * half + first + row_count, :].astype(jnp.float32)
        stat_ref[8 + head : 9 + head, :] = jnp.sum((grads * outs).T, axis=0, keepdims=True)


def block_terms(keys, values, parts, sizes):
    group_size, row_count, head_size = sizes
    half = group_size * row_count
    scale = LOG2E / math.sqrt(head_size)
    per_step = 2 if group_size % 2 == 0 else 1
    key_total = 0.0
    value_total = 0.0
    for packet_ref, stats, visible, scores_ref in parts:
        weights_parts = []
        score_parts = []
        for first in range(0, group_size, per_step):
            start, stop = first * row_count, (first + per_step) * row_count
            queries = packet_ref[start:stop, :]
            grads = packet_ref[half + start : half + stop, :]
            scores = contract(keys, queries, 1, 1)
            grad_weights = contract(values, grads, 1, 1)
            for at in range(per_step):
                head = first + at
                lanes = slice(at * row_count, (at + 1) * row_count)
                weights = jnp.exp2(scores[:, lanes] * scale - stats[head : head + 1, :])
                if visible is not None:
                    weights = jnp.where(visible, weights, 0.0)
                weights_parts.append(weights.astype(jnp.bfloat16))
                score_parts.append(
                    (weights * (grad_weights[:, lanes] - stats[8 + head : 9 + head, :])).astype(jnp.bfloat16)
                )
        grad_scores = jnp.concatenate(score_parts, axis=1)
        scores_ref[...] = grad_scores
        value_total += contract(jnp.concatenate(weights_parts, axis=1), packet_ref[half : 2 * half, :], 1, 0)
        key_total += contract(grad_scores, packet_ref[:half, :], 1, 0)
    return key_total, value_total


def visible_rows(rank_ref, steps, inner_count, row_count):
    span_rows = row_count // 2
    key_rows = lax.broadcasted_iota(jnp.int32, (row_count, row_count), 0)
    my_rows = lax.broadcasted_iota(jnp.int32, (row_count, row_count), 1)

    def positions(rank, rows):
        return jnp.where(
            rows < span_rows,
            rank * span_rows + rows,
            (2 * inner_count - 2 - rank) * span_rows + rows,
        )

    mine = positions(rank_ref[0:1, :], my_rows)
    return jnp.concatenate(
        [positions(rank_ref[step : step + 1, :], key_rows) <= mine for step in steps], axis=0
    )


def stacked(blocks, which):
    return jnp.concatenate([ref[which] for ref in blocks], axis=0)


def near_kernel(
    sizes, inner_count, outer_count, packet_ref, next_ref, order_hbm, pair_ref, scores_ref,
    next_scores_ref, total_ref, stat_ref, rank_ref, order_ref, sem,
):
    _, row_count, _ = sizes
    copy = pltpu.make_async_copy(order_hbm, order_ref, sem)
    copy.start()
    has_next = lax.axis_index("outer") < outer_count - 1
    key_rows = lax.broadcasted_iota(jnp.int32, (row_count, row_count), 0)
    visible = key_rows <= lax.broadcasted_iota(jnp.int32, (row_count, row_count), 1)
    row_stats(packet_ref, stat_ref.at[0], sizes)

    def add_up(both):
        parts = [(packet_ref, stat_ref[0], visible, scores_ref)]
        if both:
            row_stats(next_ref, stat_ref.at[1], sizes)
            parts.append((next_ref, stat_ref[1], None, next_scores_ref))
        total_ref[0], total_ref[1] = block_terms(pair_ref[0], pair_ref[1], parts, sizes)

    pl.when(has_next)(lambda: add_up(True))
    pl.when(jnp.logical_not(has_next))(lambda: add_up(False))
    copy.wait()
    my_index = lax.axis_index("inner")
    turned = lax.rem(lax.axis_index("outer"), 2) == 1
    for step in range(inner_count):
        offset = jnp.where(turned, peer_offset(step, 1, inner_count), peer_offset(step, 0, inner_count))
        rank_ref[step : step + 1, :] = jnp.full((1, row_count), order_ref[my_index ^ offset], jnp.int32)


def far_kernel(sizes, inner_count, outer_count, steps, packet_ref, next_ref, rank_ref, stat_ref, *refs):
    count = len(steps)
    _, row_count, head_size = sizes
    inv_root = 1.0 / math.sqrt(head_size)
    blocks, (scores_ref, next_scores_ref), sums = refs[:count], refs[count : count + 2], refs[count + 2 :]
    has_next = lax.axis_index("outer") < outer_count - 1

    def add_up(both):
        visible = visible_rows(rank_ref, steps, inner_count, row_count)
        parts = [(packet_ref, stat_ref[0], visible, scores_ref)]
        if both:
            parts.append((next_ref, stat_ref[1], None, next_scores_ref))
        key_total, value_total = block_terms(stacked(blocks, 0), stacked(blocks, 1), parts, sizes)
        for at, ref in enumerate(sums):
            rows = slice(at * row_count, (at + 1) * row_count)
            ref[0] = (key_total[rows] * inv_root).astype(jnp.bfloat16)
            ref[1] = value_total[rows].astype(jnp.bfloat16)

    pl.when(has_next)(lambda: add_up(True))
    pl.when(jnp.logical_not(has_next))(lambda: add_up(False))


def query_terms(refs, groups, lanes):
    scores = jnp.concatenate([ref[:, lanes] for ref in refs[:groups]], axis=0)
    return contract(stacked(refs[groups:], 0), scores, 0, 0)


def store_queries(result_ref, refs, groups, sizes):
    group_size, row_count, head_size = sizes
    terms = query_terms(refs, groups, slice(None)) * (1.0 / math.sqrt(head_size))
    for head in range(group_size):
        rows = slice(head * row_count, (head + 1) * row_count)
        result_ref[rows, :] = terms[:, rows].T.astype(result_ref.dtype)


def back_kernel(sizes, outer_count, groups, *refs):
    has_next = lax.axis_index("outer") < outer_count - 1

    @pl.when(has_next)
    def _():
        store_queries(refs[-1], refs[:-1], groups, sizes)


def query_kernel(sizes, groups, *refs):
    store_queries(refs[-1], refs[:-1], groups, sizes)


def early_kernel(sizes, *refs):
    inv_root = 1.0 / math.sqrt(sizes[2])
    own_ref, returned, total_ref = refs[0], refs[1:-1], refs[-1]
    for which, factor in ((0, inv_root), (1, 1.0)):
        total = own_ref[which] * factor
        for ref in returned:
            total += ref[which].astype(jnp.float32)
        total_ref[which] = total


def late_kernel(*refs):
    total_ref, returned, sum_ref = refs[0], refs[1:-1], refs[-1]
    for which in range(2):
        total = total_ref[which]
        for ref in returned:
            total += ref[which].astype(jnp.float32)
        sum_ref[which] = total.astype(jnp.bfloat16)


def final_kernel(
    parts, sum_ref, query_ref, back_ref, query_hbm, key_hbm, value_hbm, result_ref, sems
):
    copies = [
        pltpu.make_async_copy(sum_ref.at[0], key_hbm, sems.at[0]),
        pltpu.make_async_copy(sum_ref.at[1], value_hbm, sems.at[1]),
    ]
    for copy in copies:
        copy.start()
    has_prev = lax.axis_index("outer") > 0
    count = query_ref.shape[0] // parts
    for part in range(parts):
        rows = pl.ds(part * count, count)
        back = jnp.where(has_prev, back_ref[rows, :].astype(jnp.float32), 0.0)
        result_ref[rows, :] = (query_ref[rows, :] + back).astype(jnp.bfloat16)
        copy = pltpu.make_async_copy(result_ref.at[rows], query_hbm.at[rows], sems.at[2 + part])
        copy.start()
        copies.append(copy)
    for copy in copies:
        copy.wait()


def on_device(queries, key_rows, value_rows, attn_out, grad_out, log_norms, pair_order):
    row_count, group_size, head_size = queries.shape
    inner_count = lax.axis_size("inner")
    outer_count = lax.axis_size("outer")
    assert inner_count & (inner_count - 1) == 0 and inner_count > 1
    sizes = (group_size, row_count, head_size)
    half = group_size * row_count
    away = list(range(1, inner_count))

    def flat(array):
        return jnp.swapaxes(array, 0, 1).reshape(-1, head_size)

    def in_hbm(array):
        return pltpu.with_memory_space_constraint(array, pltpu.HBM)

    def to_segment(block, ahead):
        route = [(at, (at + ahead) % outer_count) for at in range(outer_count)]
        return lax.ppermute(block, "outer", route)

    def exchange(block, step):
        route = []
        for inner in range(inner_count):
            for outer in range(outer_count):
                peer = inner ^ peer_offset(step, outer, inner_count)
                route.append((inner * outer_count + outer, peer * outer_count + outer))
        return lax.ppermute(block, ("inner", "outer"), route)

    vmem = pl.BlockSpec(memory_space=pltpu.VMEM)
    hbm = pl.BlockSpec(memory_space=pltpu.HBM)
    roomy = pltpu.CompilerParams(vmem_limit_bytes=32 * 2**20)

    def shape(dims, dtype):
        return jax.ShapeDtypeStruct(dims, dtype)

    def cost(blocks, data=2**20):
        each = group_size * row_count * row_count
        return pl.CostEstimate(
            flops=10 * blocks * each * head_size, bytes_accessed=data, transcendentals=blocks * each
        )

    block_shape = shape((2, row_count, head_size), jnp.bfloat16)

    pair, packet = pl.pallas_call(
        functools.partial(load_kernel, sizes),
        out_shape=(
            block_shape,
            shape((packet_rows(sizes), head_size), jnp.bfloat16),
        ),
        in_specs=[hbm] * 6,
        out_specs=(vmem,) * 2,
        scratch_shapes=[pltpu.VMEM((STAT_ROWS, row_count), jnp.float32), pltpu.SemaphoreType.DMA((6,))],
        cost_estimate=cost(0),
        compiler_params=roomy,
    )(
        *(
            in_hbm(array)
            for array in (
                flat(queries), flat(grad_out), flat(attn_out), log_norms, flat(key_rows), flat(value_rows)
            )
        )
    )
    next_packet = to_segment(packet, -1)
    blocks = {0: pair}
    for step in away:
        blocks[step] = exchange(pair, step)

    def scores_shape(count):
        return shape((count * row_count, half), jnp.bfloat16)

    near_scores, near_next_scores, own_total, stats, rank = pl.pallas_call(
        functools.partial(near_kernel, sizes, inner_count, outer_count),
        out_shape=(
            scores_shape(1),
            scores_shape(1),
            shape((2, row_count, head_size), jnp.float32),
            shape((2, STAT_ROWS, row_count), jnp.float32),
            shape((max(8, inner_count), row_count), jnp.int32),
        ),
        in_specs=[vmem] * 2 + [hbm, vmem],
        out_specs=(vmem,) * 5,
        scratch_shapes=[pltpu.SMEM((inner_count,), jnp.int32), pltpu.SemaphoreType.DMA],
        cost_estimate=cost(2),
        compiler_params=roomy,
    )(packet, next_packet, in_hbm(pair_order), pair)

    scores, next_scores, sums = [near_scores], [near_next_scores], {}
    middle = inner_count // 2 - 1
    held = [0]
    for steps in (away[:middle], away[middle:]):
        if steps:
            far_scores, far_next_scores, *terms = pl.pallas_call(
                functools.partial(far_kernel, sizes, inner_count, outer_count, steps),
                out_shape=(scores_shape(len(steps)),) * 2 + (block_shape,) * len(steps),
                in_specs=[vmem] * (4 + len(steps)),
                out_specs=(vmem,) * (2 + len(steps)),
                cost_estimate=cost(2 * len(steps)),
                compiler_params=roomy,
            )(packet, next_packet, rank, stats, *(blocks[step] for step in steps))
            scores.append(far_scores)
            next_scores.append(far_next_scores)
            sums.update(zip(steps, terms))
            held += steps
    all_blocks = [blocks[step] for step in held]
    groups = len(scores)
    returned = [exchange(sums[step], step) for step in away]

    early_total = pl.pallas_call(
        functools.partial(early_kernel, sizes),
        out_shape=shape((2, row_count, head_size), jnp.float32),
        in_specs=[vmem] * (1 + middle),
        out_specs=vmem,
        cost_estimate=cost(8 * inner_count),
        compiler_params=roomy,
    )(own_total, *returned[:middle])
    early_total, next_scores[0] = lax.optimization_barrier((early_total, next_scores[0]))

    query_next = pl.pallas_call(
        functools.partial(back_kernel, sizes, outer_count, groups),
        out_shape=shape((half, head_size), jnp.bfloat16),
        in_specs=[vmem] * (groups + inner_count),
        out_specs=vmem,
        cost_estimate=cost(0, 0),
        compiler_params=roomy,
    )(*next_scores, *all_blocks)
    query_back = to_segment(query_next, 1)

    query_own = pl.pallas_call(
        functools.partial(query_kernel, sizes, groups),
        out_shape=shape((half, head_size), jnp.float32),
        in_specs=[vmem] * (groups + inner_count),
        out_specs=vmem,
        cost_estimate=cost(0, 0),
        compiler_params=roomy,
    )(*scores, *all_blocks)

    late_sum = pl.pallas_call(
        late_kernel,
        out_shape=block_shape,
        in_specs=[vmem] * (1 + len(away) - middle),
        out_specs=vmem,
        cost_estimate=cost(8 * inner_count),
        compiler_params=roomy,
    )(early_total, *returned[middle:])

    query_out, key_out, value_out = pl.pallas_call(
        functools.partial(final_kernel, group_size),
        out_shape=(
            shape((half, head_size), jnp.bfloat16),
            shape((row_count, head_size), jnp.bfloat16),
            shape((row_count, head_size), jnp.bfloat16),
        ),
        in_specs=[vmem] * 3,
        out_specs=(hbm,) * 3,
        scratch_shapes=[pltpu.VMEM((half, head_size), jnp.bfloat16), pltpu.SemaphoreType.DMA((2 + group_size,))],
        compiler_params=roomy,
    )(late_sum, query_own, query_back)
    grad_queries = jnp.swapaxes(query_out.reshape(group_size, row_count, head_size), 0, 1)
    return (grad_queries, key_out[:, None, :], value_out[:, None, :])


def solution(mesh):
    in_specs = (
        P(("outer", "inner"), "head", None),
        P(("outer", "inner"), "head", None),
        P(("outer", "inner"), "head", None),
        P(("outer", "inner"), "head", None),
        P(("outer", "inner"), "head", None),
        P("head", ("outer", "inner")),
        P(),
    )
    out_specs = (
        P(("outer", "inner"), "head", None),
        P(("outer", "inner"), "head", None),
        P(("outer", "inner"), "head", None),
    )
    return jax.shard_map(
        on_device, mesh=mesh, in_specs=in_specs, out_specs=out_specs, check_vma=False
    )
```

```python
import functools
import math

import jax
import jax.numpy as jnp
from jax import lax
from jax.experimental import pallas as pl
from jax.experimental.pallas import tpu as pltpu
from jax.sharding import PartitionSpec as P

LOG2E = math.log2(math.e)
STAT_ROWS = 16
SPLIT = 3


def contract(lhs, rhs, lhs_dim, rhs_dim):
    return lax.dot_general(
        lhs, rhs, (((lhs_dim,), (rhs_dim,)), ((), ())), preferred_element_type=jnp.float32
    )


def packet_rows(sizes):
    group_size, row_count, _ = sizes
    return 3 * group_size * row_count + SPLIT * STAT_ROWS


def peer_offset(step, outer, inner_count):
    last = inner_count - 1
    if outer % 2 == 1:
        return (inner_count - step) % inner_count
    return {0: 0, 1: 1, 2: last}.get(step, step - 1)


def load_kernel(
    sizes, query_hbm, grad_hbm, out_hbm, norm_hbm, key_hbm, value_hbm, pair_ref, packet_ref, norm_ref, sems
):
    group_size, row_count, _ = sizes
    half = group_size * row_count
    copies = [
        pltpu.make_async_copy(source, target, sems.at[at])
        for at, (source, target) in enumerate(
            [
                (query_hbm, packet_ref.at[pl.ds(0, half)]),
                (grad_hbm, packet_ref.at[pl.ds(half, half)]),
                (out_hbm, packet_ref.at[pl.ds(2 * half, half)]),
                (norm_hbm, norm_ref.at[pl.ds(0, group_size)]),
                (key_hbm, pair_ref.at[0]),
                (value_hbm, pair_ref.at[1]),
            ]
        )
    ]
    for copy in copies:
        copy.start()
    copies[3].wait()
    held = lax.broadcasted_iota(jnp.int32, (STAT_ROWS, row_count), 0) < group_size
    rest = jnp.where(held, jnp.clip(norm_ref[...], -3.38e38, 3.38e38), 0.0)
    for term in range(SPLIT):
        piece = rest.astype(jnp.bfloat16)
        start = 3 * half + term * STAT_ROWS
        packet_ref[start : start + STAT_ROWS, :] = piece
        rest = rest - piece.astype(jnp.float32)
    for copy in copies[:3] + copies[4:]:
        copy.wait()


def row_stats(packet_ref, stat_ref, sizes):
    group_size, row_count, _ = sizes
    half = group_size * row_count
    start = 3 * half
    pieces = [
        packet_ref[start + term * STAT_ROWS : start + (term + 1) * STAT_ROWS, :].astype(jnp.float32)
        for term in range(SPLIT)
    ]
    stat_ref[...] = (pieces[0] + (pieces[1] + pieces[2])) * LOG2E
    for head in range(group_size):
        first = head * row_count
        grads = packet_ref[half + first : half + first + row_count, :].astype(jnp.float32)
        outs = packet_ref[2 * half + first : 2 * half + first + row_count, :].astype(jnp.float32)
        stat_ref[8 + head : 9 + head, :] = jnp.sum((grads * outs).T, axis=0, keepdims=True)


def block_terms(keys, values, parts, sizes):
    group_size, row_count, head_size = sizes
    half = group_size * row_count
    scale = LOG2E / math.sqrt(head_size)
    per_step = 2 if group_size % 2 == 0 else 1
    key_total = 0.0
    value_total = 0.0
    for packet_ref, stats, visible, scores_ref in parts:
        weights_parts = []
        score_parts = []
        for first in range(0, group_size, per_step):
            start, stop = first * row_count, (first + per_step) * row_count
            queries = packet_ref[start:stop, :]
            grads = packet_ref[half + start : half + stop, :]
            scores = contract(keys, queries, 1, 1)
            grad_weights = contract(values, grads, 1, 1)
            for at in range(per_step):
                head = first + at
                lanes = slice(at * row_count, (at + 1) * row_count)
                weights = jnp.exp2(scores[:, lanes] * scale - stats[head : head + 1, :])
                if visible is not None:
                    weights = jnp.where(visible, weights, 0.0)
                weights_parts.append(weights.astype(jnp.bfloat16))
                score_parts.append(
                    (weights * (grad_weights[:, lanes] - stats[8 + head : 9 + head, :])).astype(jnp.bfloat16)
                )
        grad_scores = jnp.concatenate(score_parts, axis=1)
        scores_ref[...] = grad_scores
        value_total += contract(jnp.concatenate(weights_parts, axis=1), packet_ref[half : 2 * half, :], 1, 0)
        key_total += contract(grad_scores, packet_ref[:half, :], 1, 0)
    return key_total, value_total


def visible_rows(rank_ref, steps, inner_count, row_count):
    span_rows = row_count // 2
    key_rows = lax.broadcasted_iota(jnp.int32, (row_count, row_count), 0)
    my_rows = lax.broadcasted_iota(jnp.int32, (row_count, row_count), 1)

    def positions(rank, rows):
        return jnp.where(
            rows < span_rows,
            rank * span_rows + rows,
            (2 * inner_count - 2 - rank) * span_rows + rows,
        )

    mine = positions(rank_ref[0:1, :], my_rows)
    return jnp.concatenate(
        [positions(rank_ref[step : step + 1, :], key_rows) <= mine for step in steps], axis=0
    )


def stacked(blocks, which):
    return jnp.concatenate([ref[which] for ref in blocks], axis=0)


def near_kernel(
    sizes, inner_count, outer_count, packet_ref, next_ref, order_hbm, pair_ref, scores_ref,
    next_scores_ref, total_ref, stat_ref, rank_ref, order_ref, sem,
):
    _, row_count, _ = sizes
    copy = pltpu.make_async_copy(order_hbm, order_ref, sem)
    copy.start()
    has_next = lax.axis_index("outer") < outer_count - 1
    key_rows = lax.broadcasted_iota(jnp.int32, (row_count, row_count), 0)
    visible = key_rows <= lax.broadcasted_iota(jnp.int32, (row_count, row_count), 1)
    row_stats(packet_ref, stat_ref.at[0], sizes)

    def add_up(both):
        parts = [(packet_ref, stat_ref[0], visible, scores_ref)]
        if both:
            row_stats(next_ref, stat_ref.at[1], sizes)
            parts.append((next_ref, stat_ref[1], None, next_scores_ref))
        total_ref[0], total_ref[1] = block_terms(pair_ref[0], pair_ref[1], parts, sizes)

    pl.when(has_next)(lambda: add_up(True))
    pl.when(jnp.logical_not(has_next))(lambda: add_up(False))
    copy.wait()
    my_index = lax.axis_index("inner")
    turned = lax.rem(lax.axis_index("outer"), 2) == 1
    for step in range(inner_count):
        offset = jnp.where(turned, peer_offset(step, 1, inner_count), peer_offset(step, 0, inner_count))
        rank_ref[step : step + 1, :] = jnp.full((1, row_count), order_ref[my_index ^ offset], jnp.int32)


def far_kernel(sizes, inner_count, outer_count, steps, packet_ref, next_ref, rank_ref, stat_ref, *refs):
    count = len(steps)
    _, row_count, head_size = sizes
    inv_root = 1.0 / math.sqrt(head_size)
    blocks, (scores_ref, next_scores_ref), sums = refs[:count], refs[count : count + 2], refs[count + 2 :]
    has_next = lax.axis_index("outer") < outer_count - 1

    def add_up(both):
        visible = visible_rows(rank_ref, steps, inner_count, row_count)
        parts = [(packet_ref, stat_ref[0], visible, scores_ref)]
        if both:
            parts.append((next_ref, stat_ref[1], None, next_scores_ref))
        key_total, value_total = block_terms(stacked(blocks, 0), stacked(blocks, 1), parts, sizes)
        for at, ref in enumerate(sums):
            rows = slice(at * row_count, (at + 1) * row_count)
            ref[0] = (key_total[rows] * inv_root).astype(jnp.bfloat16)
            ref[1] = value_total[rows].astype(jnp.bfloat16)

    pl.when(has_next)(lambda: add_up(True))
    pl.when(jnp.logical_not(has_next))(lambda: add_up(False))


def query_terms(refs, groups, lanes):
    scores = jnp.concatenate([ref[:, lanes] for ref in refs[:groups]], axis=0)
    return contract(stacked(refs[groups:], 0), scores, 0, 0)


def store_queries(result_ref, refs, groups, sizes):
    group_size, row_count, head_size = sizes
    terms = query_terms(refs, groups, slice(None)) * (1.0 / math.sqrt(head_size))
    for head in range(group_size):
        rows = slice(head * row_count, (head + 1) * row_count)
        result_ref[rows, :] = terms[:, rows].T.astype(result_ref.dtype)


def back_kernel(sizes, outer_count, groups, *refs):
    has_next = lax.axis_index("outer") < outer_count - 1

    @pl.when(has_next)
    def _():
        store_queries(refs[-1], refs[:-1], groups, sizes)


def query_kernel(sizes, groups, *refs):
    store_queries(refs[-1], refs[:-1], groups, sizes)


def early_kernel(sizes, *refs):
    inv_root = 1.0 / math.sqrt(sizes[2])
    own_ref, returned, total_ref = refs[0], refs[1:-1], refs[-1]
    for which, factor in ((0, inv_root), (1, 1.0)):
        total = own_ref[which] * factor
        for ref in returned:
            total += ref[which].astype(jnp.float32)
        total_ref[which] = total


def late_kernel(*refs):
    total_ref, returned, sum_ref = refs[0], refs[1:-1], refs[-1]
    for which in range(2):
        total = total_ref[which]
        for ref in returned:
            total += ref[which].astype(jnp.float32)
        sum_ref[which] = total.astype(jnp.bfloat16)


def final_kernel(
    parts, sum_ref, query_ref, back_ref, query_hbm, key_hbm, value_hbm, result_ref, sems
):
    copies = [
        pltpu.make_async_copy(sum_ref.at[0], key_hbm, sems.at[0]),
        pltpu.make_async_copy(sum_ref.at[1], value_hbm, sems.at[1]),
    ]
    for copy in copies:
        copy.start()
    has_prev = lax.axis_index("outer") > 0
    count = query_ref.shape[0] // parts
    for part in range(parts):
        rows = pl.ds(part * count, count)
        back = jnp.where(has_prev, back_ref[rows, :].astype(jnp.float32), 0.0)
        result_ref[rows, :] = (query_ref[rows, :] + back).astype(jnp.bfloat16)
        copy = pltpu.make_async_copy(result_ref.at[rows], query_hbm.at[rows], sems.at[2 + part])
        copy.start()
        copies.append(copy)
    for copy in copies:
        copy.wait()


def on_device(queries, key_rows, value_rows, attn_out, grad_out, log_norms, pair_order):
    row_count, group_size, head_size = queries.shape
    inner_count = lax.axis_size("inner")
    outer_count = lax.axis_size("outer")
    assert inner_count & (inner_count - 1) == 0 and inner_count > 1
    sizes = (group_size, row_count, head_size)
    half = group_size * row_count
    away = list(range(1, inner_count))

    def flat(array):
        return jnp.swapaxes(array, 0, 1).reshape(-1, head_size)

    def in_hbm(array):
        return pltpu.with_memory_space_constraint(array, pltpu.HBM)

    def to_segment(block, ahead):
        route = [(at, (at + ahead) % outer_count) for at in range(outer_count)]
        return lax.ppermute(block, "outer", route)

    def exchange(block, step):
        route = []
        for inner in range(inner_count):
            for outer in range(outer_count):
                peer = inner ^ peer_offset(step, outer, inner_count)
                route.append((inner * outer_count + outer, peer * outer_count + outer))
        return lax.ppermute(block, ("inner", "outer"), route)

    vmem = pl.BlockSpec(memory_space=pltpu.VMEM)
    hbm = pl.BlockSpec(memory_space=pltpu.HBM)
    roomy = pltpu.CompilerParams(vmem_limit_bytes=32 * 2**20)

    def shape(dims, dtype):
        return jax.ShapeDtypeStruct(dims, dtype)

    def cost(blocks, data=2**20):
        each = group_size * row_count * row_count
        return pl.CostEstimate(
            flops=10 * blocks * each * head_size, bytes_accessed=data, transcendentals=blocks * each
        )

    block_shape = shape((2, row_count, head_size), jnp.bfloat16)

    pair, packet = pl.pallas_call(
        functools.partial(load_kernel, sizes),
        out_shape=(
            block_shape,
            shape((packet_rows(sizes), head_size), jnp.bfloat16),
        ),
        in_specs=[hbm] * 6,
        out_specs=(vmem,) * 2,
        scratch_shapes=[pltpu.VMEM((STAT_ROWS, row_count), jnp.float32), pltpu.SemaphoreType.DMA((6,))],
        cost_estimate=cost(0),
        compiler_params=roomy,
    )(
        *(
            in_hbm(array)
            for array in (
                flat(queries), flat(grad_out), flat(attn_out), log_norms, flat(key_rows), flat(value_rows)
            )
        )
    )
    next_packet = to_segment(packet, -1)
    blocks = {0: pair}
    for step in away:
        blocks[step] = exchange(pair, step)

    def scores_shape(count):
        return shape((count * row_count, half), jnp.bfloat16)

    near_scores, near_next_scores, own_total, stats, rank = pl.pallas_call(
        functools.partial(near_kernel, sizes, inner_count, outer_count),
        out_shape=(
            scores_shape(1),
            scores_shape(1),
            shape((2, row_count, head_size), jnp.float32),
            shape((2, STAT_ROWS, row_count), jnp.float32),
            shape((max(8, inner_count), row_count), jnp.int32),
        ),
        in_specs=[vmem] * 2 + [hbm, vmem],
        out_specs=(vmem,) * 5,
        scratch_shapes=[pltpu.SMEM((inner_count,), jnp.int32), pltpu.SemaphoreType.DMA],
        cost_estimate=cost(2),
        compiler_params=roomy,
    )(packet, next_packet, in_hbm(pair_order), pair)

    scores, next_scores, sums = [near_scores], [near_next_scores], {}
    middle = inner_count // 2 - 1
    held = [0]
    for steps in (away[:middle], away[middle : middle + 1], away[middle + 1 :]):
        if steps:
            far_scores, far_next_scores, *terms = pl.pallas_call(
                functools.partial(far_kernel, sizes, inner_count, outer_count, steps),
                out_shape=(scores_shape(len(steps)),) * 2 + (block_shape,) * len(steps),
                in_specs=[vmem] * (4 + len(steps)),
                out_specs=(vmem,) * (2 + len(steps)),
                cost_estimate=cost(2 * len(steps)),
                compiler_params=roomy,
            )(packet, next_packet, rank, stats, *(blocks[step] for step in steps))
            scores.append(far_scores)
            next_scores.append(far_next_scores)
            sums.update(zip(steps, terms))
            held += steps
    all_blocks = [blocks[step] for step in held]
    groups = len(scores)
    returned = [exchange(sums[step], step) for step in away]

    early_total = pl.pallas_call(
        functools.partial(early_kernel, sizes),
        out_shape=shape((2, row_count, head_size), jnp.float32),
        in_specs=[vmem] * (1 + middle),
        out_specs=vmem,
        cost_estimate=cost(8 * inner_count),
        compiler_params=roomy,
    )(own_total, *returned[:middle])
    early_total, next_scores[0] = lax.optimization_barrier((early_total, next_scores[0]))

    query_next = pl.pallas_call(
        functools.partial(back_kernel, sizes, outer_count, groups),
        out_shape=shape((half, head_size), jnp.bfloat16),
        in_specs=[vmem] * (groups + inner_count),
        out_specs=vmem,
        cost_estimate=cost(0, 0),
        compiler_params=roomy,
    )(*next_scores, *all_blocks)
    query_back = to_segment(query_next, 1)

    query_own = pl.pallas_call(
        functools.partial(query_kernel, sizes, groups),
        out_shape=shape((half, head_size), jnp.float32),
        in_specs=[vmem] * (groups + inner_count),
        out_specs=vmem,
        cost_estimate=cost(0, 0),
        compiler_params=roomy,
    )(*scores, *all_blocks)

    late_sum = pl.pallas_call(
        late_kernel,
        out_shape=block_shape,
        in_specs=[vmem] * (1 + len(away) - middle),
        out_specs=vmem,
        cost_estimate=cost(8 * inner_count),
        compiler_params=roomy,
    )(early_total, *returned[middle:])

    query_out, key_out, value_out = pl.pallas_call(
        functools.partial(final_kernel, group_size),
        out_shape=(
            shape((half, head_size), jnp.bfloat16),
            shape((row_count, head_size), jnp.bfloat16),
            shape((row_count, head_size), jnp.bfloat16),
        ),
        in_specs=[vmem] * 3,
        out_specs=(hbm,) * 3,
        scratch_shapes=[pltpu.VMEM((half, head_size), jnp.bfloat16), pltpu.SemaphoreType.DMA((2 + group_size,))],
        compiler_params=roomy,
    )(late_sum, query_own, query_back)
    grad_queries = jnp.swapaxes(query_out.reshape(group_size, row_count, head_size), 0, 1)
    return (grad_queries, key_out[:, None, :], value_out[:, None, :])


def solution(mesh):
    in_specs = (
        P(("outer", "inner"), "head", None),
        P(("outer", "inner"), "head", None),
        P(("outer", "inner"), "head", None),
        P(("outer", "inner"), "head", None),
        P(("outer", "inner"), "head", None),
        P("head", ("outer", "inner")),
        P(),
    )
    out_specs = (
        P(("outer", "inner"), "head", None),
        P(("outer", "inner"), "head", None),
        P(("outer", "inner"), "head", None),
    )
    return jax.shard_map(
        on_device, mesh=mesh, in_specs=in_specs, out_specs=out_specs, check_vma=False
    )
```

```python
import functools
import math

import jax
import jax.numpy as jnp
from jax import lax
from jax.experimental import pallas as pl
from jax.experimental.pallas import tpu as pltpu
from jax.sharding import PartitionSpec as P

LOG2E = math.log2(math.e)
STAT_ROWS = 16
SPLIT = 3


def contract(lhs, rhs, lhs_dim, rhs_dim):
    return lax.dot_general(
        lhs, rhs, (((lhs_dim,), (rhs_dim,)), ((), ())), preferred_element_type=jnp.float32
    )


def packet_rows(sizes):
    group_size, row_count, _ = sizes
    return 3 * group_size * row_count + SPLIT * STAT_ROWS


def peer_offset(step, outer, inner_count):
    last = inner_count - 1
    if outer % 2 == 1:
        return {0: 0, 1: last}.get(step, step - 1)
    return {0: 0, 1: last - 1, 2: last}.get(step, step - 2) if last > 1 else step


def load_kernel(
    sizes, query_hbm, grad_hbm, out_hbm, norm_hbm, key_hbm, value_hbm, pair_ref, packet_ref, norm_ref, sems
):
    group_size, row_count, _ = sizes
    half = group_size * row_count
    copies = [
        pltpu.make_async_copy(source, target, sems.at[at])
        for at, (source, target) in enumerate(
            [
                (query_hbm, packet_ref.at[pl.ds(0, half)]),
                (grad_hbm, packet_ref.at[pl.ds(half, half)]),
                (out_hbm, packet_ref.at[pl.ds(2 * half, half)]),
                (norm_hbm, norm_ref.at[pl.ds(0, group_size)]),
                (key_hbm, pair_ref.at[0]),
                (value_hbm, pair_ref.at[1]),
            ]
        )
    ]
    for copy in copies:
        copy.start()
    copies[3].wait()
    held = lax.broadcasted_iota(jnp.int32, (STAT_ROWS, row_count), 0) < group_size
    rest = jnp.where(held, jnp.clip(norm_ref[...], -3.38e38, 3.38e38), 0.0)
    for term in range(SPLIT):
        piece = rest.astype(jnp.bfloat16)
        start = 3 * half + term * STAT_ROWS
        packet_ref[start : start + STAT_ROWS, :] = piece
        rest = rest - piece.astype(jnp.float32)
    for copy in copies[:3] + copies[4:]:
        copy.wait()


def row_stats(packet_ref, stat_ref, sizes):
    group_size, row_count, _ = sizes
    half = group_size * row_count
    start = 3 * half
    pieces = [
        packet_ref[start + term * STAT_ROWS : start + (term + 1) * STAT_ROWS, :].astype(jnp.float32)
        for term in range(SPLIT)
    ]
    stat_ref[...] = (pieces[0] + (pieces[1] + pieces[2])) * LOG2E
    for head in range(group_size):
        first = head * row_count
        grads = packet_ref[half + first : half + first + row_count, :].astype(jnp.float32)
        outs = packet_ref[2 * half + first : 2 * half + first + row_count, :].astype(jnp.float32)
        stat_ref[8 + head : 9 + head, :] = jnp.sum((grads * outs).T, axis=0, keepdims=True)


def block_terms(keys, values, parts, sizes):
    group_size, row_count, head_size = sizes
    half = group_size * row_count
    scale = LOG2E / math.sqrt(head_size)
    per_step = 2 if group_size % 2 == 0 else 1
    key_total = 0.0
    value_total = 0.0
    for packet_ref, stats, visible, scores_ref in parts:
        weights_parts = []
        score_parts = []
        for first in range(0, group_size, per_step):
            start, stop = first * row_count, (first + per_step) * row_count
            queries = packet_ref[start:stop, :]
            grads = packet_ref[half + start : half + stop, :]
            scores = contract(keys, queries, 1, 1)
            grad_weights = contract(values, grads, 1, 1)
            for at in range(per_step):
                head = first + at
                lanes = slice(at * row_count, (at + 1) * row_count)
                weights = jnp.exp2(scores[:, lanes] * scale - stats[head : head + 1, :])
                if visible is not None:
                    weights = jnp.where(visible, weights, 0.0)
                weights_parts.append(weights.astype(jnp.bfloat16))
                score_parts.append(
                    (weights * (grad_weights[:, lanes] - stats[8 + head : 9 + head, :])).astype(jnp.bfloat16)
                )
        grad_scores = jnp.concatenate(score_parts, axis=1)
        scores_ref[...] = grad_scores
        value_total += contract(jnp.concatenate(weights_parts, axis=1), packet_ref[half : 2 * half, :], 1, 0)
        key_total += contract(grad_scores, packet_ref[:half, :], 1, 0)
    return key_total, value_total


def visible_rows(rank_ref, steps, inner_count, row_count):
    span_rows = row_count // 2
    key_rows = lax.broadcasted_iota(jnp.int32, (row_count, row_count), 0)
    my_rows = lax.broadcasted_iota(jnp.int32, (row_count, row_count), 1)

    def positions(rank, rows):
        return jnp.where(
            rows < span_rows,
            rank * span_rows + rows,
            (2 * inner_count - 2 - rank) * span_rows + rows,
        )

    mine = positions(rank_ref[0:1, :], my_rows)
    return jnp.concatenate(
        [positions(rank_ref[step : step + 1, :], key_rows) <= mine for step in steps], axis=0
    )


def stacked(blocks, which):
    return jnp.concatenate([ref[which] for ref in blocks], axis=0)


def near_kernel(
    sizes, inner_count, outer_count, packet_ref, next_ref, order_hbm, pair_ref, scores_ref,
    next_scores_ref, total_ref, stat_ref, rank_ref, order_ref, sem,
):
    _, row_count, _ = sizes
    copy = pltpu.make_async_copy(order_hbm, order_ref, sem)
    copy.start()
    has_next = lax.axis_index("outer") < outer_count - 1
    key_rows = lax.broadcasted_iota(jnp.int32, (row_count, row_count), 0)
    visible = key_rows <= lax.broadcasted_iota(jnp.int32, (row_count, row_count), 1)
    row_stats(packet_ref, stat_ref.at[0], sizes)

    def add_up(both):
        parts = [(packet_ref, stat_ref[0], visible, scores_ref)]
        if both:
            row_stats(next_ref, stat_ref.at[1], sizes)
            parts.append((next_ref, stat_ref[1], None, next_scores_ref))
        total_ref[0], total_ref[1] = block_terms(pair_ref[0], pair_ref[1], parts, sizes)

    pl.when(has_next)(lambda: add_up(True))
    pl.when(jnp.logical_not(has_next))(lambda: add_up(False))
    copy.wait()
    my_index = lax.axis_index("inner")
    turned = lax.rem(lax.axis_index("outer"), 2) == 1
    for step in range(inner_count):
        offset = jnp.where(turned, peer_offset(step, 1, inner_count), peer_offset(step, 0, inner_count))
        rank_ref[step : step + 1, :] = jnp.full((1, row_count), order_ref[my_index ^ offset], jnp.int32)


def far_kernel(sizes, inner_count, outer_count, steps, packet_ref, next_ref, rank_ref, stat_ref, *refs):
    count = len(steps)
    _, row_count, head_size = sizes
    inv_root = 1.0 / math.sqrt(head_size)
    blocks, (scores_ref, next_scores_ref), sums = refs[:count], refs[count : count + 2], refs[count + 2 :]
    has_next = lax.axis_index("outer") < outer_count - 1

    def add_up(both):
        visible = visible_rows(rank_ref, steps, inner_count, row_count)
        parts = [(packet_ref, stat_ref[0], visible, scores_ref)]
        if both:
            parts.append((next_ref, stat_ref[1], None, next_scores_ref))
        key_total, value_total = block_terms(stacked(blocks, 0), stacked(blocks, 1), parts, sizes)
        for at, ref in enumerate(sums):
            rows = slice(at * row_count, (at + 1) * row_count)
            ref[0] = (key_total[rows] * inv_root).astype(jnp.bfloat16)
            ref[1] = value_total[rows].astype(jnp.bfloat16)

    pl.when(has_next)(lambda: add_up(True))
    pl.when(jnp.logical_not(has_next))(lambda: add_up(False))


def query_terms(refs, groups, lanes):
    scores = jnp.concatenate([ref[:, lanes] for ref in refs[:groups]], axis=0)
    return contract(stacked(refs[groups:], 0), scores, 0, 0)


def store_queries(result_ref, refs, groups, sizes):
    group_size, row_count, head_size = sizes
    terms = query_terms(refs, groups, slice(None)) * (1.0 / math.sqrt(head_size))
    for head in range(group_size):
        rows = slice(head * row_count, (head + 1) * row_count)
        result_ref[rows, :] = terms[:, rows].T.astype(result_ref.dtype)


def back_kernel(sizes, outer_count, groups, *refs):
    has_next = lax.axis_index("outer") < outer_count - 1

    @pl.when(has_next)
    def _():
        store_queries(refs[-1], refs[:-1], groups, sizes)


def query_kernel(sizes, groups, *refs):
    store_queries(refs[-1], refs[:-1], groups, sizes)


def early_kernel(sizes, *refs):
    inv_root = 1.0 / math.sqrt(sizes[2])
    own_ref, returned, total_ref = refs[0], refs[1:-1], refs[-1]
    for which, factor in ((0, inv_root), (1, 1.0)):
        total = own_ref[which] * factor
        for ref in returned:
            total += ref[which].astype(jnp.float32)
        total_ref[which] = total


def late_kernel(*refs):
    total_ref, returned, sum_ref = refs[0], refs[1:-1], refs[-1]
    for which in range(2):
        total = total_ref[which]
        for ref in returned:
            total += ref[which].astype(jnp.float32)
        sum_ref[which] = total.astype(jnp.bfloat16)


def final_kernel(
    parts, sum_ref, query_ref, back_ref, query_hbm, key_hbm, value_hbm, result_ref, sems
):
    copies = [
        pltpu.make_async_copy(sum_ref.at[0], key_hbm, sems.at[0]),
        pltpu.make_async_copy(sum_ref.at[1], value_hbm, sems.at[1]),
    ]
    for copy in copies:
        copy.start()
    has_prev = lax.axis_index("outer") > 0
    count = query_ref.shape[0] // parts
    for part in range(parts):
        rows = pl.ds(part * count, count)
        back = jnp.where(has_prev, back_ref[rows, :].astype(jnp.float32), 0.0)
        result_ref[rows, :] = (query_ref[rows, :] + back).astype(jnp.bfloat16)
        copy = pltpu.make_async_copy(result_ref.at[rows], query_hbm.at[rows], sems.at[2 + part])
        copy.start()
        copies.append(copy)
    for copy in copies:
        copy.wait()


def on_device(queries, key_rows, value_rows, attn_out, grad_out, log_norms, pair_order):
    row_count, group_size, head_size = queries.shape
    inner_count = lax.axis_size("inner")
    outer_count = lax.axis_size("outer")
    assert inner_count & (inner_count - 1) == 0 and inner_count > 1
    sizes = (group_size, row_count, head_size)
    half = group_size * row_count
    away = list(range(1, inner_count))

    def flat(array):
        return jnp.swapaxes(array, 0, 1).reshape(-1, head_size)

    def in_hbm(array):
        return pltpu.with_memory_space_constraint(array, pltpu.HBM)

    def to_segment(block, ahead):
        route = [(at, (at + ahead) % outer_count) for at in range(outer_count)]
        return lax.ppermute(block, "outer", route)

    def exchange(block, step):
        route = []
        for inner in range(inner_count):
            for outer in range(outer_count):
                peer = inner ^ peer_offset(step, outer, inner_count)
                route.append((inner * outer_count + outer, peer * outer_count + outer))
        return lax.ppermute(block, ("inner", "outer"), route)

    vmem = pl.BlockSpec(memory_space=pltpu.VMEM)
    hbm = pl.BlockSpec(memory_space=pltpu.HBM)
    roomy = pltpu.CompilerParams(vmem_limit_bytes=32 * 2**20)

    def shape(dims, dtype):
        return jax.ShapeDtypeStruct(dims, dtype)

    def cost(blocks, data=2**20):
        each = group_size * row_count * row_count
        return pl.CostEstimate(
            flops=10 * blocks * each * head_size, bytes_accessed=data, transcendentals=blocks * each
        )

    block_shape = shape((2, row_count, head_size), jnp.bfloat16)

    pair, packet = pl.pallas_call(
        functools.partial(load_kernel, sizes),
        out_shape=(
            block_shape,
            shape((packet_rows(sizes), head_size), jnp.bfloat16),
        ),
        in_specs=[hbm] * 6,
        out_specs=(vmem,) * 2,
        scratch_shapes=[pltpu.VMEM((STAT_ROWS, row_count), jnp.float32), pltpu.SemaphoreType.DMA((6,))],
        cost_estimate=cost(0),
        compiler_params=roomy,
    )(
        *(
            in_hbm(array)
            for array in (
                flat(queries), flat(grad_out), flat(attn_out), log_norms, flat(key_rows), flat(value_rows)
            )
        )
    )
    next_packet = to_segment(packet, -1)
    blocks = {0: pair}
    for step in away:
        blocks[step] = exchange(pair, step)

    def scores_shape(count):
        return shape((count * row_count, half), jnp.bfloat16)

    near_scores, near_next_scores, own_total, stats, rank = pl.pallas_call(
        functools.partial(near_kernel, sizes, inner_count, outer_count),
        out_shape=(
            scores_shape(1),
            scores_shape(1),
            shape((2, row_count, head_size), jnp.float32),
            shape((2, STAT_ROWS, row_count), jnp.float32),
            shape((max(8, inner_count), row_count), jnp.int32),
        ),
        in_specs=[vmem] * 2 + [hbm, vmem],
        out_specs=(vmem,) * 5,
        scratch_shapes=[pltpu.SMEM((inner_count,), jnp.int32), pltpu.SemaphoreType.DMA],
        cost_estimate=cost(2),
        compiler_params=roomy,
    )(packet, next_packet, in_hbm(pair_order), pair)

    scores, next_scores, sums = [near_scores], [near_next_scores], {}
    middle = inner_count // 2 - 1
    held = [0]
    for steps in (away[:middle], away[middle:]):
        if steps:
            far_scores, far_next_scores, *terms = pl.pallas_call(
                functools.partial(far_kernel, sizes, inner_count, outer_count, steps),
                out_shape=(scores_shape(len(steps)),) * 2 + (block_shape,) * len(steps),
                in_specs=[vmem] * (4 + len(steps)),
                out_specs=(vmem,) * (2 + len(steps)),
                cost_estimate=cost(2 * len(steps)),
                compiler_params=roomy,
            )(packet, next_packet, rank, stats, *(blocks[step] for step in steps))
            scores.append(far_scores)
            next_scores.append(far_next_scores)
            sums.update(zip(steps, terms))
            held += steps
    all_blocks = [blocks[step] for step in held]
    groups = len(scores)
    returned = [exchange(sums[step], step) for step in away]

    early_total = pl.pallas_call(
        functools.partial(early_kernel, sizes),
        out_shape=shape((2, row_count, head_size), jnp.float32),
        in_specs=[vmem] * (1 + middle),
        out_specs=vmem,
        cost_estimate=cost(8 * inner_count),
        compiler_params=roomy,
    )(own_total, *returned[:middle])
    early_total, next_scores[0] = lax.optimization_barrier((early_total, next_scores[0]))

    query_next = pl.pallas_call(
        functools.partial(back_kernel, sizes, outer_count, groups),
        out_shape=shape((half, head_size), jnp.bfloat16),
        in_specs=[vmem] * (groups + inner_count),
        out_specs=vmem,
        cost_estimate=cost(0, 0),
        compiler_params=roomy,
    )(*next_scores, *all_blocks)
    query_back = to_segment(query_next, 1)

    query_own = pl.pallas_call(
        functools.partial(query_kernel, sizes, groups),
        out_shape=shape((half, head_size), jnp.float32),
        in_specs=[vmem] * (groups + inner_count),
        out_specs=vmem,
        cost_estimate=cost(0, 0),
        compiler_params=roomy,
    )(*scores, *all_blocks)

    late_sum = pl.pallas_call(
        late_kernel,
        out_shape=block_shape,
        in_specs=[vmem] * (1 + len(away) - middle),
        out_specs=vmem,
        cost_estimate=cost(8 * inner_count),
        compiler_params=roomy,
    )(early_total, *returned[middle:])

    query_out, key_out, value_out = pl.pallas_call(
        functools.partial(final_kernel, group_size),
        out_shape=(
            shape((half, head_size), jnp.bfloat16),
            shape((row_count, head_size), jnp.bfloat16),
            shape((row_count, head_size), jnp.bfloat16),
        ),
        in_specs=[vmem] * 3,
        out_specs=(hbm,) * 3,
        scratch_shapes=[pltpu.VMEM((half, head_size), jnp.bfloat16), pltpu.SemaphoreType.DMA((2 + group_size,))],
        compiler_params=roomy,
    )(late_sum, query_own, query_back)
    grad_queries = jnp.swapaxes(query_out.reshape(group_size, row_count, head_size), 0, 1)
    return (grad_queries, key_out[:, None, :], value_out[:, None, :])


def solution(mesh):
    in_specs = (
        P(("outer", "inner"), "head", None),
        P(("outer", "inner"), "head", None),
        P(("outer", "inner"), "head", None),
        P(("outer", "inner"), "head", None),
        P(("outer", "inner"), "head", None),
        P("head", ("outer", "inner")),
        P(),
    )
    out_specs = (
        P(("outer", "inner"), "head", None),
        P(("outer", "inner"), "head", None),
        P(("outer", "inner"), "head", None),
    )
    return jax.shard_map(
        on_device, mesh=mesh, in_specs=in_specs, out_specs=out_specs, check_vma=False
    )
```
